32 devices in a mesh: groups: 2 (over y), dom: 4 (over z), pair: 2 (over x), sub: 2 (over core).
Axes of the slice: x: 2, y: 2, z: 4, core: 2. Of those that a mesh axis runs over, the one named last changes fastest.
Arguments:
- nodes: bfloat16 [16384, 128], P(('groups', 'dom', 'pair', 'sub')), parts along dimension 0, may hold values from -6 to 6
- cotangent: bfloat16 [16384, 128], P(('groups', 'dom', 'pair', 'sub')), parts along dimension 0, may hold values from -6 to 6
- send_blocks: int32 [32, 2, 1], P(('groups', 'dom', 'pair', 'sub')), parts along dimension 0, may hold values from 0 to 3
- neighbour_blocks: int32 [128, 4], P(('groups', 'dom', 'pair', 'sub')), parts along dimension 0, may hold values from 0 to 5
- neighbour_nodes: int32 [128, 4, 128], P(('groups', 'dom', 'pair', 'sub')), parts along dimension 0, may hold values from 0 to 127
- pool_map: int32 [128], P(('groups', 'dom', 'pair', 'sub')), parts along dimension 0, may hold values from 0 to 3
- coarse_blocks: int32 [32, 4], P(('groups', 'dom', 'pair', 'sub')), parts along dimension 0, may hold values from 0 to 2
- coarse_nodes: int32 [32, 4, 128], P(('groups', 'dom', 'pair', 'sub')), parts along dimension 0, may hold values from 0 to 127
- weights: bfloat16 [3, 6, 128, 128], replicated, may hold values from -0.5 to 0.5
- biases: float32 [3, 2, 128], replicated, may hold values from -3 to 3
Outputs:
- out_nodes: bfloat16 [16384, 128], P(('groups', 'dom', 'pair', 'sub')), parts along dimension 0
- grad_nodes: float32 [16384, 128], P(('groups', 'dom', 'pair', 'sub')), parts along dimension 0
The draws below stay inside these ranges and needn't reach their ends.
There are 2 independent parts, one for each index of `groups`. The reference program is written for one: setup_inputs(seed, part) draws one part's arguments, and reference() takes and returns one part's arrays. A program takes and returns all parts, laid end to end along the dimension named above; an argument that names none is the same for every part. Nothing has to cross between parts.
Inputs may be any that keep to these rules, and one draw needn't show every extreme that they name: `send_blocks`: entries index a device's own blocks. `neighbour_blocks`: entries under 4 are own blocks, the rest received blocks in round order. `pool_map`: a coarse block of the pooling group, which may receive no fine block. `coarse_blocks`: entries under 1 are own coarse blocks, the rest received ones in round order.
All inputs are finite; a program needn't handle non-finite values.
Results may differ from the reference program's by a relative error of at most 0.013.
Values may be sent and summed in bfloat16 or wider, within the bound.
No kernel may reach another device: no remote copies, remote signals or barrier semaphores. Data moves between devices by JAX's collectives and lax.ppermute only.
A program may use at most 64 MiB of HBM per device.

```python
import jax
import jax.numpy as jnp
from jax import lax

D = 128
BLOCK = 128
FINE_DEV = 4
DEGREE = 4
ROUNDS = 2
LAYERS = 3
HALO_DEV = 1
COARSE_DEV = 1
GROUP = 4
DEVS = 16
SLOTS = 4
FINE_BLOCKS = 64
COARSE_BLOCKS = 16
NODES = 8192
N_DOM = 4


def place_ends(entries, stream_key, smallest, high):
    spot = [jax.random.randint(jax.random.fold_in(stream_key, axis), (), 0, length) for axis, length in enumerate(entries.shape)]
    main_axis = entries.shape.index(max(entries.shape))
    neighbour = spot[:main_axis] + [(spot[main_axis] + 1) % entries.shape[main_axis]] + spot[main_axis + 1:]
    return entries.at[tuple(spot)].set(smallest).at[tuple(neighbour)].set(high)


def steps_of(own_key, dims, cuts, low, largest):
    loudness = 1.0
    for position, shards_of in cuts:
        steps = jax.random.uniform(jax.random.fold_in(jax.random.fold_in(own_key, 6), position), (shards_of,), jnp.float32, low / len(cuts), largest / len(cuts))
        loudness = loudness * jnp.repeat(jnp.exp(steps), dims[position] // shards_of).reshape((-1,) + (1,) * (len(dims) - 1 - position))
    return loudness


def centred(rng, dims, spread, most, cuts=(), kind=jnp.bfloat16):
    array = jax.random.normal(rng, dims, jnp.float32) * spread
    if len(cuts) > 0:
        array = steps_of(rng, dims, cuts, -0.22, 0.18) * array
    return jnp.clip(array, min=-most, max=most).astype(kind)


def setup_inputs(seed: int = 0, part: int = 0) -> dict:
    seeds = jax.random.split(jax.random.key(seed), 11)
    part_keys = jax.random.split(jax.random.fold_in(seeds[10], part), 11)
    nodes = centred(part_keys[0], (NODES, D), 1.0, 6.0, ((0, 16),))
    cotangent = centred(part_keys[1], (NODES, D), 1.0, 6.0, ((0, 16),))
    send_blocks = place_ends(jax.random.randint(part_keys[2], (DEVS, ROUNDS, HALO_DEV), 0, FINE_DEV), jax.random.fold_in(part_keys[2], 1), 0, FINE_DEV - 1).astype(jnp.int32)
    neighbour_blocks = place_ends(jax.random.randint(part_keys[3], (FINE_BLOCKS, DEGREE), 0, FINE_DEV + ROUNDS * HALO_DEV), jax.random.fold_in(part_keys[3], 1), 0, (FINE_DEV + ROUNDS * HALO_DEV) - 1).astype(jnp.int32)
    neighbour_nodes = place_ends(jax.random.randint(part_keys[4], (FINE_BLOCKS, DEGREE, BLOCK), 0, BLOCK), jax.random.fold_in(part_keys[4], 1), 0, BLOCK - 1).astype(jnp.int32)
    pool_map = place_ends(jax.random.randint(part_keys[5], (FINE_BLOCKS,), 0, SLOTS), jax.random.fold_in(part_keys[5], 1), 0, SLOTS - 1).astype(jnp.int32)
    coarse_blocks = place_ends(jax.random.randint(part_keys[6], (COARSE_BLOCKS, DEGREE), 0, COARSE_DEV * (ROUNDS + 1)), jax.random.fold_in(part_keys[6], 1), 0, (COARSE_DEV * (ROUNDS + 1)) - 1).astype(jnp.int32)
    coarse_nodes = place_ends(jax.random.randint(part_keys[7], (COARSE_BLOCKS, DEGREE, BLOCK), 0, BLOCK), jax.random.fold_in(part_keys[7], 1), 0, BLOCK - 1).astype(jnp.int32)
    weights = centred(seeds[8], (LAYERS, 6, D, D), D ** -0.5, 0.5)
    biases = centred(seeds[9], (LAYERS, 2, D), 0.5, 3.0, (), jnp.float32)
    return {"nodes": nodes, "cotangent": cotangent, "send_blocks": send_blocks, "neighbour_blocks": neighbour_blocks, "neighbour_nodes": neighbour_nodes, "pool_map": pool_map, "coarse_blocks": coarse_blocks, "coarse_nodes": coarse_nodes, "weights": weights, "biases": biases}


def project(inputs, matrix):
    leading = inputs.shape[:-1]
    flat_inputs = inputs.reshape(-1, inputs.shape[-1])
    return jnp.dot(flat_inputs, matrix, preferred_element_type=jnp.float32).reshape(leading + (matrix.shape[1],))

def message_layer(own_field, halo_field, near_blocks, near_nodes, weights, biases):
    own_state = own_field.astype(jnp.bfloat16)
    halo_state = halo_field.astype(jnp.bfloat16)
    blocks, block_size, features = own_state.shape
    degree = near_blocks.shape[1]
    everyone = jnp.concatenate([own_state, halo_state], axis=0)
    sender = project(everyone, weights[1]).reshape(-1, features)
    receiver = project(own_state, weights[0]) + biases[0]
    flat_index = (near_blocks[:, :, None] * block_size + near_nodes).reshape(-1).astype(jnp.int32)
    picked = jnp.take(sender, flat_index, axis=0).reshape(blocks, degree, block_size, features)
    active = jax.nn.silu(receiver[:, None] + picked).astype(jnp.bfloat16)
    message = project(active, weights[2])
    average = (lax.optimization_barrier(jnp.sum(message, axis=1)) / degree).astype(jnp.bfloat16)
    hidden = jax.nn.silu(project(own_state, weights[3]) + project(average, weights[4]) + biases[1]).astype(jnp.bfloat16)
    return own_field + project(hidden, weights[5])

def rounded(values):
    return lax.optimization_barrier(values.astype(jnp.bfloat16)).astype(jnp.float32)

def partner_of(xor_bit):
    return jnp.bitwise_xor(jnp.arange(N_DOM, dtype=jnp.int32), jnp.int32(xor_bit))

def select_rows(states, chosen_lists):
    return jax.vmap(jax.vmap(lambda source_rows, chosen_ids: source_rows[chosen_ids]))(states, chosen_lists)

def fine_halo(states, send_lists):
    pieces = []
    for section, xor_bit in enumerate((1, N_DOM // 2)):
        chosen = select_rows(states, send_lists[:, :, section])
        pieces.append(chosen[partner_of(xor_bit)])
    return jnp.concatenate(pieces, axis=2)

def fine_return(halo_grad, send_lists, grads):
    for section, xor_bit in enumerate((1, N_DOM // 2)):
        arrived = halo_grad[:, :, section * HALO_DEV:(section + 1) * HALO_DEV][partner_of(xor_bit)]
        grads = jax.vmap(jax.vmap(lambda target, chosen_ids, update: target.at[chosen_ids].add(update)))(grads, send_lists[:, :, section], arrived)
    return grads

def coarse_halo(states):
    return jnp.concatenate([states[partner_of(xor_bit)] for xor_bit in (1, N_DOM // 2)], axis=2)

def coarse_return(halo_grad, grads):
    for section, xor_bit in enumerate((1, N_DOM // 2)):
        grads = grads + halo_grad[:, :, section * COARSE_DEV:(section + 1) * COARSE_DEV][partner_of(xor_bit)]
    return grads

def apply_layer(states, halo, near_blocks, near_nodes, weights, biases):

    def per_dom(items):
        return jax.vmap(lambda own_field, halo_field, blocks_in, nodes_in: message_layer(own_field, halo_field, blocks_in, nodes_in, weights, biases))(*items)
    return lax.map(per_dom, (states, halo, near_blocks, near_nodes))

def pull_layer(states, halo, near_blocks, near_nodes, weights, biases, grads):

    def one_device(own_field, halo_field, blocks_in, nodes_in, grad_in):
        _, pullback = jax.vjp(lambda first_in, second_in: message_layer(first_in, second_in, blocks_in, nodes_in, weights, biases), own_field, halo_field)
        return pullback(grad_in)

    def per_dom(items):
        return jax.vmap(one_device)(*items)
    return lax.map(per_dom, (states, halo, near_blocks, near_nodes, grads))

def group_sum(rows_all, slot_ids):
    return jax.vmap(lambda rows_in, ids_in: jax.ops.segment_sum(rows_in, ids_in, num_segments=SLOTS))(rows_all, slot_ids)

def reference(nodes, cotangent, send_blocks, neighbour_blocks, neighbour_nodes, pool_map, coarse_blocks, coarse_nodes, weights, biases):
    shape_fine = (N_DOM, GROUP, FINE_DEV, BLOCK, D)
    shape_coarse = (N_DOM, GROUP, COARSE_DEV, BLOCK, D)
    start_state = nodes.reshape(shape_fine).astype(jnp.float32)
    send_lists = send_blocks.reshape(N_DOM, GROUP, ROUNDS, HALO_DEV)
    fine_near = neighbour_blocks.reshape(N_DOM, GROUP, FINE_DEV, DEGREE)
    fine_ends = neighbour_nodes.reshape(N_DOM, GROUP, FINE_DEV, DEGREE, BLOCK)
    coarse_near = coarse_blocks.reshape(N_DOM, GROUP, COARSE_DEV, DEGREE)
    coarse_ends = coarse_nodes.reshape(N_DOM, GROUP, COARSE_DEV, DEGREE, BLOCK)
    slot_ids = pool_map.reshape(N_DOM, GROUP * FINE_DEV)
    halo_first = fine_halo(start_state, send_lists)
    after_first = rounded(apply_layer(start_state, halo_first, fine_near, fine_ends, weights[0], biases[0]))
    slot_sums = group_sum(after_first.reshape(N_DOM, GROUP * FINE_DEV, BLOCK * D), slot_ids)
    slot_counts = group_sum(jnp.ones(slot_ids.shape, jnp.float32), slot_ids)
    divisor = jnp.maximum(slot_counts, 1.0)
    coarse_start = rounded(slot_sums / divisor[:, :, None]).reshape(shape_coarse)
    coarse_in = coarse_halo(coarse_start)
    coarse_end = rounded(apply_layer(coarse_start, coarse_in, coarse_near, coarse_ends, weights[1], biases[1]))
    coarse_flat = coarse_end.reshape(N_DOM, SLOTS, BLOCK * D)
    lifted = jax.vmap(lambda table_in, ids_in: table_in[ids_in])(coarse_flat, slot_ids).reshape(shape_fine)
    middle = rounded(after_first + lifted)
    halo_second = fine_halo(middle, send_lists)
    final = apply_layer(middle, halo_second, fine_near, fine_ends, weights[2], biases[2])
    out_nodes = final.astype(jnp.bfloat16).reshape(NODES, D)
    grad_final = cotangent.reshape(shape_fine).astype(jnp.float32)
    grad_middle, grad_halo_second = pull_layer(middle, halo_second, fine_near, fine_ends, weights[2], biases[2], grad_final)
    grad_middle = fine_return(grad_halo_second, send_lists, grad_middle)
    grad_coarse_end = group_sum(grad_middle.reshape(N_DOM, GROUP * FINE_DEV, BLOCK * D), slot_ids).reshape(shape_coarse)
    grad_coarse, grad_coarse_halo = pull_layer(coarse_start, coarse_in, coarse_near, coarse_ends, weights[1], biases[1], grad_coarse_end)
    grad_coarse = coarse_return(grad_coarse_halo, grad_coarse)
    scaled = grad_coarse.reshape(N_DOM, SLOTS, BLOCK * D) / divisor[:, :, None]
    grad_first = grad_middle + jax.vmap(lambda table_in, ids_in: table_in[ids_in])(scaled, slot_ids).reshape(shape_fine)
    grad_start, grad_halo_first = pull_layer(start_state, halo_first, fine_near, fine_ends, weights[0], biases[0], grad_first)
    grad_start = fine_return(grad_halo_first, send_lists, grad_start)
    return (out_nodes, grad_start.reshape(NODES, D))
```

```python
import jax
import jax.numpy as jnp
from jax import lax
from jax.experimental import pallas as pl
from jax.experimental.pallas import tpu as pltpu
from jax.sharding import PartitionSpec as P

F32 = jnp.float32
BF16 = jnp.bfloat16
COUNT_ROWS = 16


def swapped(value, axis, mask):
    size = lax.axis_size(axis)
    return lax.ppermute(value, axis, [(source, source ^ mask) for source in range(size)])


def mm(a, b):
    return jnp.dot(a, b, preferred_element_type=F32)


def mm_t(a, b):
    return lax.dot_general(a, b, (((1,), (1,)), ((), ())), preferred_element_type=F32)


def sigmoid(x):
    return 0.5 * jnp.tanh(0.5 * x) + 0.5


def run(kernel, outs, scalars, *arrays, scratch=(), flops=0):
    in_specs = [pl.BlockSpec(memory_space=pltpu.SMEM)] + [pl.BlockSpec(memory_space=pltpu.VMEM)] * len(arrays)
    return pl.pallas_call(
        kernel,
        out_shape=[jax.ShapeDtypeStruct(shape, dtype) for shape, dtype in outs],
        in_specs=in_specs,
        out_specs=[pl.BlockSpec(memory_space=pltpu.VMEM)] * len(outs),
        scratch_shapes=list(scratch),
        compiler_params=pltpu.CompilerParams(vmem_limit_bytes=12 * 2**20),
        cost_estimate=pl.CostEstimate(flops=flops, bytes_accessed=2**20, transcendentals=0),
    )(scalars, *arrays)


def per_device(
    nodes,
    cotangent,
    send_blocks,
    neighbour_blocks,
    neighbour_nodes,
    pool_map,
    coarse_blocks,
    coarse_nodes,
    weights,
    biases,
):
    size, features = neighbour_nodes.shape[2], nodes.shape[1]
    blocks, degree = neighbour_blocks.shape
    xor_bits = (1, lax.axis_size("dom") // 2)
    rounds = len(xor_bits)
    group_axes = ("pair", "sub")
    slots = lax.axis_size(group_axes)
    edges = blocks * degree
    everyone = blocks + rounds
    tile = (size, features)

    at_near = rounds
    at_pool = at_near + edges
    at_coarse = at_pool + blocks
    at_me = at_coarse + degree
    scalars = jnp.concatenate(
        [
            send_blocks.reshape(-1),
            neighbour_blocks.reshape(-1),
            pool_map.reshape(-1),
            coarse_blocks.reshape(-1),
            lax.axis_index(group_axes).astype(jnp.int32)[None],
        ]
    )

    def exchange(pieces):
        return [swapped(piece, "dom", bit) for piece, bit in zip(pieces, xor_bits)]

    def spread(pieces):
        return [swapped(pieces[mask], group_axes, mask) for mask in range(1, slots)]

    def tables_into(ends_ref, count, pick_ref, put_ref):
        rows = lax.broadcasted_iota(jnp.int32, (size, size), 0)
        columns = lax.broadcasted_iota(jnp.int32, (size, size), 1)
        upright = jnp.transpose(ends_ref[...])
        for edge in range(count):
            put_ref[edge] = (rows == ends_ref[edge : edge + 1, :]).astype(BF16)
            pick_ref[edge] = (columns == upright[:, edge : edge + 1]).astype(BF16)

    def own_into(state, layer, w_ref, b_ref, recv_ref, node_ref, sender_ref):
        recv_ref[...] = mm(state, w_ref[layer, 0]) + b_ref[layer, 0:1, :]
        node_ref[...] = mm(state, w_ref[layer, 3]) + b_ref[layer, 1:2, :]
        sender_ref[...] = mm(state, w_ref[layer, 1]).astype(BF16)

    def forward_block(b, near_at, layer, s_ref, w_ref, recv_ref, node_ref, send_scr, pick_ref, slope_ref, node_slope_ref):
        rows = pl.ds(b * size, size)
        recv = recv_ref[rows, :]
        total = None
        for e in range(degree):
            edge = b * degree + e
            pre = recv + mm(pick_ref[edge], send_scr[s_ref[near_at + edge]])
            gate = sigmoid(pre)
            active = pre * gate
            slope_ref[edge] = (gate + active * (1.0 - gate)).astype(BF16)
            message = active.astype(BF16).astype(F32)
            total = message if total is None else total + message
        average = (mm(total.astype(BF16), w_ref[layer, 2]) * (1.0 / degree)).astype(BF16)
        hidden_pre = node_ref[rows, :] + mm(average, w_ref[layer, 4])
        gate = sigmoid(hidden_pre)
        hidden = hidden_pre * gate
        node_slope_ref[b] = (gate + hidden * (1.0 - gate)).astype(BF16)
        return mm(hidden.astype(BF16), w_ref[layer, 5])

    def backward_edges(grad, b, near_at, layer, s_ref, w_ref, put_ref, slope_ref, node_slope_ref, acc_scr):
        d_hidden = (mm_t(grad.astype(BF16), w_ref[layer, 5]) * node_slope_ref[b].astype(F32)).astype(BF16)
        d_average = (mm_t(d_hidden, w_ref[layer, 4]) * (1.0 / degree)).astype(BF16)
        d_active = mm_t(d_average, w_ref[layer, 2])
        total = None
        for e in range(degree):
            edge = b * degree + e
            d_pre = d_active * slope_ref[edge].astype(F32)
            total = d_pre if total is None else total + d_pre
            near = s_ref[near_at + edge]
            acc_scr[near] = acc_scr[near] + mm(put_ref[edge], d_pre.astype(BF16))
        return d_hidden, total.astype(BF16)

    def pooled_into(read, s_ref, out_refs, with_count):
        me = s_ref[at_me]
        for mask in range(slots):
            slot = me ^ mask
            total, count = None, None
            for b in range(blocks):
                hit = (s_ref[at_pool + b] == slot).astype(F32)
                part = read(b) * hit
                total = part if total is None else total + part
                count = hit if count is None else count + hit
            out_refs[mask][0:size, :] = total.astype(BF16)
            if with_count:
                out_refs[mask][size:, :] = jnp.full((COUNT_ROWS, features), count, F32).astype(BF16)

    def send_rows(b):
        return lax.dynamic_slice_in_dim(nodes, b * size, size, axis=0)

    halo = exchange([send_rows(send_blocks[0, r, 0]) for r in range(rounds)])

    def prepare(s_ref, ends_ref, coarse_ref, h_ref, w_ref, b_ref, pick, put, cpick, cput, recv, node, sender):
        tables_into(ends_ref, edges, pick, put)
        tables_into(coarse_ref, degree, cpick, cput)
        own_into(h_ref[...], 0, w_ref, b_ref, recv, node, sender)

    fine_own = [((blocks * size, features), F32), ((blocks * size, features), F32), ((blocks * size, features), BF16)]
    coarse_own = [(tile, F32), (tile, F32), (tile, BF16)]
    pick, put, coarse_pick, coarse_put, recv0, node0, sender0 = run(
        prepare,
        [((edges, size, size), BF16)] * 2 + [((degree, size, size), BF16)] * 2 + fine_own,
        scalars,
        neighbour_nodes.reshape(edges, size),
        coarse_nodes.reshape(degree, size),
        nodes,
        weights,
        biases,
    )

    slopes = [((edges,) + tile, BF16), ((blocks,) + tile, BF16)]
    pool_out = [((size + COUNT_ROWS, features), BF16)] * slots

    def first_layer(s_ref, g0, g1, h_ref, recv, node, sender, pick, w_ref, *rest):
        first_ref, slope_ref, node_slope_ref = rest[:3]
        sends, send_scr = rest[3:-1], rest[-1]
        for b in range(blocks):
            send_scr[b] = sender[pl.ds(b * size, size), :]
        for r, g in enumerate((g0, g1)):
            send_scr[blocks + r] = mm(g[...], w_ref[0, 1]).astype(BF16)
        for b in range(blocks):
            change = forward_block(b, at_near, 0, s_ref, w_ref, recv, node, send_scr, pick, slope_ref, node_slope_ref)
            first_ref[b] = (h_ref[pl.ds(b * size, size), :].astype(F32) + change).astype(BF16)
        pooled_into(lambda b: first_ref[b].astype(F32), s_ref, sends, True)

    first, slope0, node_slope0, *pool_sends = run(
        first_layer,
        [((blocks,) + tile, BF16)] + slopes + pool_out,
        scalars, halo[0], halo[1], nodes, recv0, node0, sender0, pick, weights,
        scratch=[pltpu.VMEM((everyone,) + tile, BF16)],
    )

    pool_in = spread(pool_sends)

    def coarse_begin(s_ref, *refs):
        parts, (start_ref, divisor_ref) = refs[:slots], refs[slots:]
        total = parts[0][...].astype(F32)
        for part in parts[1:]:
            total = total + part[...].astype(F32)
        divisor = jnp.maximum(total[size : size + 8, :], 1.0)
        divisor_ref[...] = divisor
        start_ref[...] = (total[:size, :] / divisor[0:1, :]).astype(BF16)

    coarse_start, divisor = run(
        coarse_begin, [(tile, BF16), ((8, features), F32)], scalars, pool_sends[0], *pool_in
    )
    coarse_halo = exchange([coarse_start] * rounds)

    def coarse_prepare(s_ref, h_ref, w_ref, b_ref, recv, node, sender):
        own_into(h_ref[...], 1, w_ref, b_ref, recv, node, sender)

    recv1, node1, sender1 = run(coarse_prepare, coarse_own, scalars, coarse_start, weights, biases)

    def coarse_layer(s_ref, g0, g1, h_ref, recv, node, sender, pick, w_ref, end_ref, slope_ref, node_slope_ref, send_scr):
        send_scr[0] = sender[...]
        for r, g in enumerate((g0, g1)):
            send_scr[1 + r] = mm(g[...], w_ref[1, 1]).astype(BF16)
        change = forward_block(0, at_coarse, 1, s_ref, w_ref, recv, node, send_scr, pick, slope_ref, node_slope_ref)
        end_ref[...] = (h_ref[...].astype(F32) + change).astype(BF16)

    coarse_end, slope1, node_slope1 = run(
        coarse_layer,
        [(tile, BF16), ((degree,) + tile, BF16), ((1,) + tile, BF16)],
        scalars, coarse_halo[0], coarse_halo[1], coarse_start, recv1, node1, sender1, coarse_pick, weights,
        scratch=[pltpu.VMEM((1 + rounds,) + tile, BF16)],
    )
    ends_in = spread([coarse_end] * slots)

    def lift(s_ref, *refs):
        parts, first_ref = refs[:slots], refs[slots]
        middle_ref, out0, out1, table = refs[slots + 1 :]
        me = s_ref[at_me]
        for mask in range(slots):
            table[me ^ mask] = parts[mask][...]
        for b in range(blocks):
            lifted = table[s_ref[at_pool + b]].astype(F32)
            middle_ref[b] = (first_ref[b].astype(F32) + lifted).astype(BF16)
        for r, out in enumerate((out0, out1)):
            out[...] = middle_ref[s_ref[r]]

    middle, *middle_sends = run(
        lift,
        [((blocks,) + tile, BF16)] + [(tile, BF16)] * rounds,
        scalars, coarse_end, *ends_in, first,
        scratch=[pltpu.VMEM((slots,) + tile, BF16)],
    )
    halo = exchange(middle_sends)

    def last_prepare(s_ref, h_ref, w_ref, b_ref, recv, node, sender):
        own_into(h_ref[...].reshape(blocks * size, features), 2, w_ref, b_ref, recv, node, sender)

    recv2, node2, sender2 = run(last_prepare, fine_own, scalars, middle, weights, biases)

    back_out = [(tile, BF16)] * rounds + [((blocks,) + tile, BF16)] * 3

    def backward_out(read, layer, s_ref, w_ref, put_ref, slope_ref, node_slope_ref, halo_refs, d_node, d_recv, d_send, acc_scr):
        acc_scr[...] = jnp.zeros_like(acc_scr)
        for b in range(blocks):
            d_node[b], d_recv[b] = backward_edges(
                read(b), b, at_near, layer, s_ref, w_ref, put_ref, slope_ref, node_slope_ref, acc_scr
            )
        for r, out in enumerate(halo_refs):
            out[...] = mm_t(acc_scr[blocks + r].astype(BF16), w_ref[layer, 1]).astype(BF16)
        d_send[...] = acc_scr[0:blocks].astype(BF16)

    def last_layer(s_ref, g0, g1, h_ref, recv, node, sender, pick, put, w_ref, cot_ref, out_ref, h0, h1, d_node, d_recv, d_send, send_scr, slope_scr, node_slope_scr, acc_scr):
        for b in range(blocks):
            send_scr[b] = sender[pl.ds(b * size, size), :]
        for r, g in enumerate((g0, g1)):
            send_scr[blocks + r] = mm(g[...], w_ref[2, 1]).astype(BF16)
        for b in range(blocks):
            change = forward_block(b, at_near, 2, s_ref, w_ref, recv, node, send_scr, pick, slope_scr, node_slope_scr)
            out_ref[pl.ds(b * size, size), :] = (h_ref[b].astype(F32) + change).astype(BF16)
        backward_out(
            lambda b: cot_ref[pl.ds(b * size, size), :],
            2, s_ref, w_ref, put, slope_scr, node_slope_scr, (h0, h1), d_node, d_recv, d_send, acc_scr,
        )

    out_nodes, *rest = run(
        last_layer,
        [((blocks * size, features), BF16)] + back_out,
        scalars, halo[0], halo[1], middle, recv2, node2, sender2, pick, put, weights, cotangent,
        scratch=[
            pltpu.VMEM((everyone,) + tile, BF16),
            pltpu.VMEM((edges,) + tile, BF16),
            pltpu.VMEM((blocks,) + tile, BF16),
            pltpu.VMEM((everyone,) + tile, F32),
        ],
    )
    halo_grads, (d_node, d_recv, d_send) = rest[:rounds], rest[rounds:]
    returned = exchange(halo_grads)

    def own_back(layer, b, grad, w_ref, d_node, d_recv, d_send):
        return (
            grad
            + mm_t(d_recv[b], w_ref[layer, 0])
            + mm_t(d_node[b], w_ref[layer, 3])
            + mm_t(d_send[b], w_ref[layer, 1])
        )

    def last_own(s_ref, cot_ref, d_node, d_recv, d_send, w_ref, grad_ref):
        for b in range(blocks):
            grad = cot_ref[pl.ds(b * size, size), :].astype(F32)
            grad_ref[b] = own_back(2, b, grad, w_ref, d_node, d_recv, d_send)

    (grad_own,) = run(
        last_own, [((blocks,) + tile, F32)], scalars, cotangent, d_node, d_recv, d_send, weights
    )

    def pool_grads(s_ref, r0, r1, own_ref, grad_ref, *sends):
        grad_ref[...] = own_ref[...]
        for r, arrived in enumerate((r0, r1)):
            grad_ref[s_ref[r]] = grad_ref[s_ref[r]] + arrived[...].astype(F32)
        pooled_into(lambda b: grad_ref[b], s_ref, sends, False)

    grad_middle, *grad_sends = run(
        pool_grads,
        [((blocks,) + tile, F32)] + [(tile, BF16)] * slots,
        scalars, returned[0], returned[1], grad_own,
    )
    grads_in = spread(grad_sends)

    def coarse_back(s_ref, *refs):
        parts = refs[:slots]
        put, slope_ref, node_slope_ref, w_ref, own_ref, h0, h1, acc_scr = refs[slots:]
        grad = parts[0][...].astype(F32)
        for part in parts[1:]:
            grad = grad + part[...].astype(F32)
        acc_scr[...] = jnp.zeros_like(acc_scr)
        d_node, d_recv = backward_edges(
            grad, 0, at_coarse, 1, s_ref, w_ref, put, slope_ref, node_slope_ref, acc_scr
        )
        for r, out in enumerate((h0, h1)):
            out[...] = mm_t(acc_scr[1 + r].astype(BF16), w_ref[1, 1]).astype(BF16)
        own_ref[...] = (
            grad
            + mm_t(d_recv, w_ref[1, 0])
            + mm_t(d_node, w_ref[1, 3])
            + mm_t(acc_scr[0].astype(BF16), w_ref[1, 1])
        )

    coarse_grad, *coarse_sends = run(
        coarse_back,
        [(tile, F32)] + [(tile, BF16)] * rounds,
        scalars, grad_sends[0], *grads_in, coarse_put, slope1, node_slope1, weights,
        scratch=[pltpu.VMEM((1 + rounds,) + tile, F32)],
    )
    coarse_returned = exchange(coarse_sends)

    def scale(s_ref, own_ref, r0, r1, divisor_ref, out_ref):
        total = own_ref[...] + r0[...].astype(F32) + r1[...].astype(F32)
        out_ref[...] = (total / divisor_ref[0:1, :]).astype(BF16)

    (scaled,) = run(scale, [(tile, BF16)], scalars, coarse_grad, *coarse_returned, divisor)
    scaled_in = spread([scaled] * slots)

    def first_back(s_ref, *refs):
        parts = refs[:slots]
        middle_ref, put, slope_ref, node_slope_ref, w_ref = refs[slots : slots + 5]
        grad_ref, h0, h1, d_node, d_recv, d_send, table, acc_scr = refs[slots + 5 :]
        me = s_ref[at_me]
        for mask in range(slots):
            table[me ^ mask] = parts[mask][...]
        for b in range(blocks):
            grad_ref[b] = middle_ref[b] + table[s_ref[at_pool + b]].astype(F32)
        backward_out(
            lambda b: grad_ref[b],
            0, s_ref, w_ref, put, slope_ref, node_slope_ref, (h0, h1), d_node, d_recv, d_send, acc_scr,
        )

    grad_first, *rest = run(
        first_back,
        [((blocks,) + tile, F32)] + back_out,
        scalars, scaled, *scaled_in, grad_middle, put, slope0, node_slope0, weights,
        scratch=[pltpu.VMEM((slots,) + tile, BF16), pltpu.VMEM((everyone,) + tile, F32)],
    )
    halo_grads, (d_node, d_recv, d_send) = rest[:rounds], rest[rounds:]
    returned = exchange(halo_grads)

    def first_own(s_ref, first_ref, d_node, d_recv, d_send, w_ref, grad_ref):
        for b in range(blocks):
            grad_ref[b] = own_back(0, b, first_ref[b], w_ref, d_node, d_recv, d_send)

    (grad_own,) = run(
        first_own, [((blocks,) + tile, F32)], scalars, grad_first, d_node, d_recv, d_send, weights
    )

    def finish(s_ref, r0, r1, own_ref, out_ref):
        out_ref[...] = own_ref[...]
        for r, arrived in enumerate((r0, r1)):
            out_ref[s_ref[r]] = out_ref[s_ref[r]] + arrived[...].astype(F32)

    (grad_nodes,) = run(finish, [((blocks,) + tile, F32)], scalars, returned[0], returned[1], grad_own)
    return (out_nodes, grad_nodes.reshape(-1, features))


def solution(mesh):
    split = ("groups", "dom", "pair", "sub")
    placed = (
        P(split, None),
        P(split, None),
        P(split, None, None),
        P(split, None),
        P(split, None, None),
        P(split),
        P(split, None),
        P(split, None, None),
        P(),
        P(),
    )
    return jax.shard_map(
        per_device,
        mesh=mesh,
        in_specs=placed,
        out_specs=(P(split, None), P(split, None)),
        check_vma=False,
    )
```

```python
import jax
import jax.numpy as jnp
from jax import lax
from jax.experimental import pallas as pl
from jax.experimental.pallas import tpu as pltpu
from jax.sharding import PartitionSpec as P

F32 = jnp.float32
BF16 = jnp.bfloat16
I32 = jnp.int32
COUNT_ROWS = 16
GROUP_AXES = ("pair", "sub")


def swapped(value, axis, mask):
    size = lax.axis_size(axis)
    return lax.ppermute(value, axis, [(source, source ^ mask) for source in range(size)])


def mm(a, b):
    return jnp.dot(a, b, preferred_element_type=F32)


def mm_t(a, b):
    return lax.dot_general(a, b, (((1,), (1,)), ((), ())), preferred_element_type=F32)


def sigmoid(x):
    return 0.5 * jnp.tanh(0.5 * x) + 0.5


def scalar(table, index):
    return table[index : index + 1, :][0, 0]


def run(kernel, outs, *arrays, scratch=(), flops=0, space=pltpu.VMEM):
    return pl.pallas_call(
        kernel,
        out_shape=[jax.ShapeDtypeStruct(shape, dtype) for shape, dtype in outs],
        in_specs=[pl.BlockSpec(memory_space=space)] * len(arrays),
        out_specs=[pl.BlockSpec(memory_space=pltpu.VMEM)] * len(outs),
        scratch_shapes=list(scratch),
        compiler_params=pltpu.CompilerParams(vmem_limit_bytes=12 * 2**20),
        cost_estimate=pl.CostEstimate(flops=flops, bytes_accessed=2**20, transcendentals=0),
    )(*arrays)


def per_device(
    nodes,
    cotangent,
    send_blocks,
    neighbour_blocks,
    neighbour_nodes,
    pool_map,
    coarse_blocks,
    coarse_nodes,
    weights,
    biases,
):
    size, features = neighbour_nodes.shape[2], nodes.shape[1]
    blocks, degree = neighbour_blocks.shape
    xor_bits = (1, lax.axis_size("dom") // 2)
    rounds = len(xor_bits)
    slots = lax.axis_size(GROUP_AXES)
    pair_size, sub_size = lax.axis_size("pair"), lax.axis_size("sub")
    edges = blocks * degree
    everyone = blocks + rounds
    tile = (size, features)
    fine = (blocks * size, features)
    tiles = (blocks,) + tile

    at_near = rounds
    at_pool = at_near + edges
    at_coarse = at_pool + blocks
    at_me = at_coarse + degree
    table_rows = -(-(at_me + 1) // 8) * 8

    def exchange(pieces):
        return [swapped(piece, "dom", bit) for piece, bit in zip(pieces, xor_bits)]

    def spread(pieces):
        return [swapped(pieces[mask], GROUP_AXES, mask) for mask in range(1, slots)]

    def rows_of(b):
        return pl.ds(b * size, size)

    def choose(send_ref, nodes_hbm, h_ref, out0, out1, send_smem, sems):
        copies = [
            pltpu.make_async_copy(send_ref, send_smem, sems.at[0]),
            pltpu.make_async_copy(nodes_hbm, h_ref, sems.at[1]),
        ]
        for copy in copies:
            copy.start()
        for copy in copies:
            copy.wait()
        for r, out in enumerate((out0, out1)):
            at = pl.multiple_of(send_smem[0, r, 0] * size, size)
            out[...] = h_ref[pl.ds(at, size), :]

    h0, *first_sends = run(
        choose,
        [(fine, BF16)] + [(tile, BF16)] * rounds,
        send_blocks,
        nodes,
        space=pltpu.HBM,
        scratch=[pltpu.SMEM(send_blocks.shape, I32), pltpu.SemaphoreType.DMA((2,))],
    )
    halo = exchange(first_sends)

    def tables_into(ends, count, pick_ref, put_ref):
        rows = lax.broadcasted_iota(I32, (size, size), 0)
        columns = lax.broadcasted_iota(I32, (size, size), 1)
        upright = jnp.transpose(ends)
        for edge in range(count):
            put_ref[edge] = (rows == ends[edge : edge + 1, :]).astype(BF16)
            pick_ref[edge] = (columns == upright[:, edge : edge + 1]).astype(BF16)

    def own_into(state, layer, w_ref, b_ref, recv_ref, node_ref, sender_ref):
        recv_ref[...] = mm(state, w_ref[layer, 0]) + b_ref[layer, 0:1, :]
        node_ref[...] = mm(state, w_ref[layer, 3]) + b_ref[layer, 1:2, :]
        sender_ref[...] = mm(state, w_ref[layer, 1]).astype(BF16)

    def layer_forward(count, near_at, layer, s_ref, w_ref, recv, node, send_scr, pick_ref, slope_ref, node_slope_ref, sum_scr):
        for b in range(count):
            receiver = recv[rows_of(b), :]
            total = None
            for e in range(degree):
                edge = b * degree + e
                pre = receiver + mm(pick_ref[edge], send_scr[scalar(s_ref, near_at + edge)])
                gate = sigmoid(pre)
                active = pre * gate
                slope_ref[edge] = (gate + active * (1.0 - gate)).astype(BF16)
                total = active if total is None else total + active
            sum_scr[rows_of(b), :] = total.astype(BF16)
        average = (mm(sum_scr[...], w_ref[layer, 2]) * (1.0 / degree)).astype(BF16)
        hidden_pre = node[...] + mm(average, w_ref[layer, 4])
        gate = sigmoid(hidden_pre)
        hidden = hidden_pre * gate
        node_slope_ref[...] = (gate + hidden * (1.0 - gate)).astype(BF16)
        return mm(hidden.astype(BF16), w_ref[layer, 5])

    def senders_into(own, halos, layer, w_ref, send_scr):
        count = send_scr.shape[0] - rounds
        for r, g in enumerate(halos):
            send_scr[count + r] = mm(g[...], w_ref[layer, 1]).astype(BF16)
        for b in range(count):
            send_scr[b] = own[rows_of(b), :]

    def layer_backward(grad, count, near_at, layer, s_ref, w_ref, put_ref, slope_ref, node_slope_ref, d_node, d_recv, act_scr, acc_scr):
        d_hidden = (mm_t(grad, w_ref[layer, 5]) * node_slope_ref[...].astype(F32)).astype(BF16)
        d_node[...] = d_hidden
        d_average = (mm_t(d_hidden, w_ref[layer, 4]) * (1.0 / degree)).astype(BF16)
        act_scr[...] = mm_t(d_average, w_ref[layer, 2])
        acc_scr[...] = jnp.zeros_like(acc_scr)
        for b in range(count):
            d_active = act_scr[rows_of(b), :]
            total = None
            for e in range(degree):
                edge = b * degree + e
                d_pre = d_active * slope_ref[edge].astype(F32)
                total = d_pre if total is None else total + d_pre
                near = scalar(s_ref, near_at + edge)
                acc_scr[near] = acc_scr[near] + mm(put_ref[edge], d_pre.astype(BF16))
            d_recv[rows_of(b), :] = total.astype(BF16)

    def halo_grads_into(outs, layer, w_ref, acc_scr):
        count = acc_scr.shape[0] - rounds
        for r, out in enumerate(outs):
            out[...] = mm_t(acc_scr[count + r].astype(BF16), w_ref[layer, 1]).astype(BF16)

    def own_back(grad, layer, w_ref, d_node, d_recv, d_send):
        return grad + mm_t(d_recv, w_ref[layer, 0]) + mm_t(d_node, w_ref[layer, 3]) + mm_t(d_send, w_ref[layer, 1])

    def pooled_into(read, s_ref, out_refs, with_count):
        me = scalar(s_ref, at_me)
        for mask in range(slots):
            slot = me ^ mask
            total, count = None, None
            for b in range(blocks):
                hit = (scalar(s_ref, at_pool + b) == slot).astype(F32)
                part = read(b) * hit
                total = part if total is None else total + part
                count = hit if count is None else count + hit
            out_refs[mask][0:size, :] = total.astype(BF16)
            if with_count:
                out_refs[mask][size:, :] = jnp.full((COUNT_ROWS, features), count, F32).astype(BF16)

    inputs = (
        send_blocks,
        neighbour_blocks,
        pool_map,
        coarse_blocks,
        neighbour_nodes.reshape(edges, size),
        coarse_nodes.reshape(degree, size),
        weights,
        biases,
        cotangent,
    )
    own_out = [(fine, F32), (fine, F32), (fine, BF16)]

    def prepare(send_in, near_in, pool_in, coarse_in, ends_in, cends_in, w_in, b_in, c_in, h_ref,
                s_ref, w_ref, b_ref, c_ref, pick, put, cpick, cput, recv, node, sender,
                send_s, near_s, pool_s, coarse_s, ends, cends, sems):
        pairs = (
            (send_in, send_s), (near_in, near_s), (pool_in, pool_s), (coarse_in, coarse_s),
            (ends_in, ends), (cends_in, cends), (w_in, w_ref), (b_in, b_ref), (c_in, c_ref),
        )
        copies = [pltpu.make_async_copy(source, target, sems.at[i]) for i, (source, target) in enumerate(pairs)]
        for copy in copies:
            copy.start()
        for copy in copies:
            copy.wait()

        def put_row(index, value):
            s_ref[index : index + 1, :] = jnp.full((1, features), value, I32)

        for r in range(rounds):
            put_row(r, send_s[0, r, 0])
        for b in range(blocks):
            for e in range(degree):
                put_row(at_near + b * degree + e, near_s[b, e])
            put_row(at_pool + b, pool_s[b])
        for e in range(degree):
            put_row(at_coarse + e, coarse_s[0, e])
        put_row(at_me, lax.axis_index("pair") * sub_size + lax.axis_index("sub"))
        own_into(h_ref[...], 0, w_ref, b_ref, recv, node, sender)
        tables_into(ends[...], edges, pick, put)
        tables_into(cends[...], degree, cpick, cput)

    hbm, vmem = pl.BlockSpec(memory_space=pltpu.HBM), pl.BlockSpec(memory_space=pltpu.VMEM)
    prepared = [
        ((table_rows, features), I32), (weights.shape, BF16), (biases.shape, F32), (fine, BF16),
        ((edges, size, size), BF16), ((edges, size, size), BF16),
        ((degree, size, size), BF16), ((degree, size, size), BF16),
    ] + own_out
    table, w, bias, cot, pick, put, coarse_pick, coarse_put, recv0, node0, sender0 = pl.pallas_call(
        prepare,
        out_shape=[jax.ShapeDtypeStruct(shape, dtype) for shape, dtype in prepared],
        in_specs=[hbm] * len(inputs) + [vmem],
        out_specs=[vmem] * len(prepared),
        scratch_shapes=[pltpu.SMEM(a.shape, I32) for a in inputs[:4]]
        + [pltpu.VMEM(a.shape, I32) for a in inputs[4:6]]
        + [pltpu.SemaphoreType.DMA((len(inputs),))],
        compiler_params=pltpu.CompilerParams(vmem_limit_bytes=12 * 2**20),
        cost_estimate=pl.CostEstimate(flops=0, bytes_accessed=2**22, transcendentals=0),
    )(*inputs, h0)

    slopes = [((edges,) + tile, BF16), (fine, BF16)]
    pool_out = [((size + COUNT_ROWS, features), BF16)] * slots
    layer_scratch = [pltpu.VMEM((everyone,) + tile, BF16), pltpu.VMEM(fine, BF16)]
    coarse_scratch = [pltpu.VMEM((1 + rounds,) + tile, BF16), pltpu.VMEM(tile, BF16)]

    def first_layer(s_ref, g0, g1, h_ref, recv, node, sender, pick, w_ref, *rest):
        first_ref, slope_ref, node_slope_ref = rest[:3]
        sends, (send_scr, sum_scr) = rest[3:-2], rest[-2:]
        senders_into(sender, (g0, g1), 0, w_ref, send_scr)
        change = layer_forward(
            blocks, at_near, 0, s_ref, w_ref, recv, node, send_scr, pick, slope_ref, node_slope_ref, sum_scr
        )
        first_ref[...] = (h_ref[...].astype(F32) + change).astype(BF16)
        pooled_into(lambda b: first_ref[rows_of(b), :].astype(F32), s_ref, sends, True)

    first, slope0, node_slope0, *pool_sends = run(
        first_layer,
        [(fine, BF16)] + slopes + pool_out,
        table, halo[0], halo[1], h0, recv0, node0, sender0, pick, w,
        scratch=layer_scratch,
    )

    pool_in = spread(pool_sends)

    def coarse_begin(*refs):
        parts, (start_ref, divisor_ref) = refs[:slots], refs[slots:]
        total = parts[0][...].astype(F32)
        for part in parts[1:]:
            total = total + part[...].astype(F32)
        divisor = jnp.maximum(total[size : size + 8, :], 1.0)
        divisor_ref[...] = divisor
        start_ref[...] = (total[:size, :] / divisor[0:1, :]).astype(BF16)

    coarse_start, divisor = run(coarse_begin, [(tile, BF16), ((8, features), F32)], pool_sends[0], *pool_in)
    coarse_halo = exchange([coarse_start] * rounds)

    def coarse_prepare(h_ref, w_ref, b_ref, recv, node, sender):
        own_into(h_ref[...], 1, w_ref, b_ref, recv, node, sender)

    recv1, node1, sender1 = run(coarse_prepare, [(tile, F32), (tile, F32), (tile, BF16)], coarse_start, w, bias)

    def coarse_layer(s_ref, g0, g1, h_ref, recv, node, sender, pick, w_ref, end_ref, slope_ref, node_slope_ref, send_scr, sum_scr):
        senders_into(sender, (g0, g1), 1, w_ref, send_scr)
        change = layer_forward(
            1, at_coarse, 1, s_ref, w_ref, recv, node, send_scr, pick, slope_ref, node_slope_ref, sum_scr
        )
        end_ref[...] = (h_ref[...].astype(F32) + change).astype(BF16)

    coarse_end, slope1, node_slope1 = run(
        coarse_layer,
        [(tile, BF16), ((degree,) + tile, BF16), (tile, BF16)],
        table, coarse_halo[0], coarse_halo[1], coarse_start, recv1, node1, sender1, coarse_pick, w,
        scratch=coarse_scratch,
    )
    ends_in = spread([coarse_end] * slots)

    def lift(s_ref, *refs):
        parts, first_ref = refs[:slots], refs[slots]
        middle_ref, out0, out1, lift_scr = refs[slots + 1 :]
        me = scalar(s_ref, at_me)
        for mask in range(slots):
            lift_scr[me ^ mask] = parts[mask][...]
        for b in range(blocks):
            lifted = lift_scr[scalar(s_ref, at_pool + b)].astype(F32)
            middle_ref[b] = (first_ref[rows_of(b), :].astype(F32) + lifted).astype(BF16)
        for r, out in enumerate((out0, out1)):
            out[...] = middle_ref[scalar(s_ref, r)]

    middle, *middle_sends = run(
        lift,
        [(tiles, BF16)] + [(tile, BF16)] * rounds,
        table, coarse_end, *ends_in, first,
        scratch=[pltpu.VMEM((slots,) + tile, BF16)],
    )
    middle = middle.reshape(fine)
    halo = exchange(middle_sends)

    def last_prepare(h_ref, w_ref, b_ref, recv, node, sender):
        own_into(h_ref[...], 2, w_ref, b_ref, recv, node, sender)

    recv2, node2, sender2 = run(last_prepare, own_out, middle, w, bias)

    back_out = [(tile, BF16)] * rounds + [(fine, BF16), (fine, BF16), (tiles, BF16)]
    back_scratch = [pltpu.VMEM(fine, F32), pltpu.VMEM((everyone,) + tile, F32)]

    def last_layer(s_ref, g0, g1, h_ref, recv, node, sender, pick, put, w_ref, cot_ref,
                   out_ref, r0, r1, d_node, d_recv, d_send,
                   send_scr, sum_scr, slope_scr, node_slope_scr, act_scr, acc_scr):
        senders_into(sender, (g0, g1), 2, w_ref, send_scr)
        change = layer_forward(
            blocks, at_near, 2, s_ref, w_ref, recv, node, send_scr, pick, slope_scr, node_slope_scr, sum_scr
        )
        out_ref[...] = (h_ref[...].astype(F32) + change).astype(BF16)
        layer_backward(
            cot_ref[...], blocks, at_near, 2, s_ref, w_ref, put, slope_scr, node_slope_scr, d_node, d_recv, act_scr, acc_scr
        )
        halo_grads_into((r0, r1), 2, w_ref, acc_scr)
        d_send[...] = acc_scr[0:blocks].astype(BF16)

    out_nodes, *rest = run(
        last_layer,
        [(fine, BF16)] + back_out,
        table, halo[0], halo[1], middle, recv2, node2, sender2, pick, put, w, cot,
        scratch=layer_scratch + [pltpu.VMEM((edges,) + tile, BF16), pltpu.VMEM(fine, BF16)] + back_scratch,
    )
    halo_grads, (d_node, d_recv, d_send) = rest[:rounds], rest[rounds:]
    returned = exchange(halo_grads)

    def last_own(cot_ref, d_node, d_recv, d_send, w_ref, grad_ref):
        grad_ref[...] = own_back(cot_ref[...].astype(F32), 2, w_ref, d_node[...], d_recv[...], d_send[...])

    (grad_own,) = run(last_own, [(fine, F32)], cot, d_node, d_recv, d_send.reshape(fine), w)

    def pool_grads(s_ref, r0, r1, own_ref, grad_ref, *sends):
        grad_ref[...] = own_ref[...]
        for r, arrived in enumerate((r0, r1)):
            at = scalar(s_ref, r)
            grad_ref[at] = grad_ref[at] + arrived[...].astype(F32)
        pooled_into(lambda b: grad_ref[b], s_ref, sends, False)

    grad_middle, *grad_sends = run(
        pool_grads,
        [(tiles, F32)] + [(tile, BF16)] * slots,
        table, returned[0], returned[1], grad_own.reshape(tiles),
    )
    grads_in = spread(grad_sends)

    def coarse_back(s_ref, *refs):
        parts = refs[:slots]
        put, slope_ref, node_slope_ref, w_ref, own_ref, r0, r1, d_node, d_recv, act_scr, acc_scr = refs[slots:]
        grad = parts[0][...].astype(F32)
        for part in parts[1:]:
            grad = grad + part[...].astype(F32)
        layer_backward(
            grad.astype(BF16), 1, at_coarse, 1, s_ref, w_ref, put, slope_ref, node_slope_ref, d_node, d_recv, act_scr, acc_scr
        )
        halo_grads_into((r0, r1), 1, w_ref, acc_scr)
        own_ref[...] = own_back(grad, 1, w_ref, d_node[...], d_recv[...], acc_scr[0].astype(BF16))

    coarse_grad, *coarse_sends = run(
        coarse_back,
        [(tile, F32)] + [(tile, BF16)] * rounds,
        table, grad_sends[0], *grads_in, coarse_put, slope1, node_slope1, w,
        scratch=[
            pltpu.VMEM(tile, BF16), pltpu.VMEM(tile, BF16), pltpu.VMEM(tile, F32), pltpu.VMEM((1 + rounds,) + tile, F32),
        ],
    )
    coarse_returned = exchange(coarse_sends)

    def scale(own_ref, r0, r1, divisor_ref, out_ref):
        total = own_ref[...] + r0[...].astype(F32) + r1[...].astype(F32)
        out_ref[...] = (total / divisor_ref[0:1, :]).astype(BF16)

    (scaled,) = run(scale, [(tile, BF16)], coarse_grad, *coarse_returned, divisor)
    scaled_in = spread([scaled] * slots)

    def first_back(s_ref, *refs):
        parts = refs[:slots]
        middle_ref, put, slope_ref, node_slope_ref, w_ref = refs[slots : slots + 5]
        grad_ref, r0, r1, d_node, d_recv, d_send, lift_scr, act_scr, acc_scr = refs[slots + 5 :]
        me = scalar(s_ref, at_me)
        for mask in range(slots):
            lift_scr[me ^ mask] = parts[mask][...]
        for b in range(blocks):
            lifted = lift_scr[scalar(s_ref, at_pool + b)].astype(F32)
            grad_ref[rows_of(b), :] = middle_ref[b] + lifted
        layer_backward(
            grad_ref[...].astype(BF16), blocks, at_near, 0, s_ref, w_ref, put, slope_ref, node_slope_ref, d_node, d_recv, act_scr, acc_scr
        )
        halo_grads_into((r0, r1), 0, w_ref, acc_scr)
        d_send[...] = acc_scr[0:blocks].astype(BF16)

    grad_first, *rest = run(
        first_back,
        [(fine, F32)] + back_out,
        table, scaled, *scaled_in, grad_middle, put, slope0, node_slope0, w,
        scratch=[pltpu.VMEM((slots,) + tile, BF16)] + back_scratch,
    )
    halo_grads, (d_node, d_recv, d_send) = rest[:rounds], rest[rounds:]
    returned = exchange(halo_grads)

    def first_own(first_ref, d_node, d_recv, d_send, w_ref, grad_ref):
        grad_ref[...] = own_back(first_ref[...], 0, w_ref, d_node[...], d_recv[...], d_send[...])

    (grad_own,) = run(first_own, [(fine, F32)], grad_first, d_node, d_recv, d_send.reshape(fine), w)

    def finish(s_ref, r0, r1, own_ref, out_ref):
        out_ref[...] = own_ref[...]
        for r, arrived in enumerate((r0, r1)):
            at = scalar(s_ref, r)
            out_ref[at] = out_ref[at] + arrived[...].astype(F32)

    (grad_nodes,) = run(finish, [(tiles, F32)], table, returned[0], returned[1], grad_own.reshape(tiles))
    return (out_nodes, grad_nodes.reshape(fine))


def solution(mesh):
    split = ("groups", "dom", "pair", "sub")
    placed = (
        P(split, None),
        P(split, None),
        P(split, None, None),
        P(split, None),
        P(split, None, None),
        P(split),
        P(split, None),
        P(split, None, None),
        P(),
        P(),
    )
    return jax.shard_map(
        per_device,
        mesh=mesh,
        in_specs=placed,
        out_specs=(P(split, None), P(split, None)),
        check_vma=False,
    )
```

```python
import jax
import jax.numpy as jnp
from jax import lax
from jax.experimental import pallas as pl
from jax.experimental.pallas import tpu as pltpu
from jax.sharding import PartitionSpec as P

F32 = jnp.float32
BF16 = jnp.bfloat16
I32 = jnp.int32
COUNT_ROWS = 16
GROUP_AXES = ("pair", "sub")
ORDER = (1, 0)


def swapped(value, axis, mask):
    size = lax.axis_size(axis)
    return lax.ppermute(value, axis, [(source, source ^ mask) for source in range(size)])


def mm(a, b):
    return jnp.dot(a, b, preferred_element_type=F32)


def mm_t(a, b):
    return lax.dot_general(a, b, (((1,), (1,)), ((), ())), preferred_element_type=F32)


def sigmoid(x):
    return 0.5 * jnp.tanh(0.5 * x) + 0.5


def scalar(table, index):
    return table[index : index + 1, :][0, 0]


def run(kernel, outs, *arrays, scratch=(), flops=0):
    return pl.pallas_call(
        kernel,
        out_shape=[jax.ShapeDtypeStruct(shape, dtype) for shape, dtype in outs],
        in_specs=[pl.BlockSpec(memory_space=pltpu.VMEM)] * len(arrays),
        out_specs=[pl.BlockSpec(memory_space=pltpu.VMEM)] * len(outs),
        scratch_shapes=list(scratch),
        compiler_params=pltpu.CompilerParams(vmem_limit_bytes=12 * 2**20),
        cost_estimate=pl.CostEstimate(flops=flops, bytes_accessed=2**20, transcendentals=0),
    )(*arrays)


def run_hbm(kernel, outs, far, *near, scratch=()):
    return pl.pallas_call(
        kernel,
        out_shape=[pltpu.VMEM(shape, dtype) for shape, dtype in outs],
        in_specs=[pl.BlockSpec(memory_space=pltpu.HBM)] * len(far) + [pl.BlockSpec(memory_space=pltpu.VMEM)] * len(near),
        out_specs=[pl.BlockSpec(memory_space=pltpu.VMEM)] * len(outs),
        scratch_shapes=list(scratch),
        compiler_params=pltpu.CompilerParams(vmem_limit_bytes=12 * 2**20),
        cost_estimate=pl.CostEstimate(flops=0, bytes_accessed=2**20, transcendentals=0),
    )(*[pltpu.with_memory_space_constraint(array, pltpu.HBM) for array in far], *near)


def per_device(
    nodes,
    cotangent,
    send_blocks,
    neighbour_blocks,
    neighbour_nodes,
    pool_map,
    coarse_blocks,
    coarse_nodes,
    weights,
    biases,
):
    size, features = neighbour_nodes.shape[2], nodes.shape[1]
    blocks, degree = neighbour_blocks.shape
    xor_bits = (1, lax.axis_size("dom") // 2)
    rounds = len(xor_bits)
    slots = lax.axis_size(GROUP_AXES)
    pair_size, sub_size = lax.axis_size("pair"), lax.axis_size("sub")
    edges = blocks * degree
    everyone = blocks + rounds
    tile = (size, features)
    fine = (blocks * size, features)
    tiles = (blocks,) + tile

    at_near = rounds
    at_pool = at_near + edges
    at_coarse = at_pool + blocks
    at_me = at_coarse + degree
    table_rows = -(-(at_me + 1) // 8) * 8

    masks = (0,) + tuple(range(slots - 1, 0, -1))
    same_masks = tuple(range(slots))

    def exchange(pieces):
        return [swapped(piece, "dom", xor_bits[r]) for r, piece in zip(ORDER, pieces)]

    def exchange_same(piece):
        return [swapped(piece, "dom", bit) for bit in xor_bits]

    def spread(pieces):
        return [swapped(piece, GROUP_AXES, mask) for mask, piece in zip(masks[1:], pieces[1:])]

    def spread_same(piece):
        return [swapped(piece, GROUP_AXES, mask) for mask in same_masks[1:]]

    def rows_of(b):
        return pl.ds(b * size, size)

    def fetch(pairs, sems):
        copies = [pltpu.make_async_copy(source, target, sems.at[i]) for i, (source, target) in enumerate(pairs)]
        for copy in copies:
            copy.start()
        for copy in copies:
            copy.wait()

    def choose(send_in, nodes_in, h_ref, out0, out1, send_scr, sems):
        fetch([(send_in, send_scr), (nodes_in, h_ref)], sems)
        for r, out in zip(ORDER, (out0, out1)):
            at = pl.multiple_of(send_scr[0:1, r : r + 1][0, 0] * size, size)
            out[...] = h_ref[pl.ds(at, size), :]

    sent = send_blocks.reshape(1, rounds)
    h0, *first_sends = run_hbm(
        choose,
        [(fine, BF16)] + [(tile, BF16)] * rounds,
        [sent, nodes],
        scratch=[pltpu.VMEM((1, rounds), I32), pltpu.SemaphoreType.DMA((2,))],
    )
    halo = exchange(first_sends)

    def tables_into(ends, count, pick_ref, put_ref):
        rows = lax.broadcasted_iota(I32, (size, size), 0)
        columns = lax.broadcasted_iota(I32, (size, size), 1)
        upright = jnp.transpose(ends)
        for edge in range(count):
            put_ref[edge] = (rows == ends[edge : edge + 1, :]).astype(BF16)
            pick_ref[edge] = (columns == upright[:, edge : edge + 1]).astype(BF16)

    def own_into(state, layer, w_ref, b_ref, recv_ref, node_ref, sender_ref):
        recv_ref[...] = mm(state, w_ref[layer, 0]) + b_ref[layer, 0:1, :]
        node_ref[...] = mm(state, w_ref[layer, 3]) + b_ref[layer, 1:2, :]
        sender_ref[...] = mm(state, w_ref[layer, 1]).astype(BF16)

    def layer_forward(count, near_at, layer, s_ref, w_ref, recv, node, send_scr, pick_ref, slope_ref, node_slope_ref, sum_scr):
        for b in range(count):
            receiver = recv[rows_of(b), :]
            total = None
            for e in range(degree):
                edge = b * degree + e
                pre = receiver + mm(pick_ref[edge], send_scr[scalar(s_ref, near_at + edge)])
                gate = sigmoid(pre)
                active = pre * gate
                slope_ref[edge] = (gate + active * (1.0 - gate)).astype(BF16)
                total = active if total is None else total + active
            sum_scr[rows_of(b), :] = total.astype(BF16)
        average = (mm(sum_scr[...], w_ref[layer, 2]) * (1.0 / degree)).astype(BF16)
        hidden_pre = node[...] + mm(average, w_ref[layer, 4])
        gate = sigmoid(hidden_pre)
        hidden = hidden_pre * gate
        node_slope_ref[...] = (gate + hidden * (1.0 - gate)).astype(BF16)
        return mm(hidden.astype(BF16), w_ref[layer, 5])

    def senders_into(own, halos, layer, w_ref, send_scr, order=ORDER):
        count = send_scr.shape[0] - rounds
        for r, g in zip(order, halos):
            send_scr[count + r] = mm(g[...], w_ref[layer, 1]).astype(BF16)
        for b in range(count):
            send_scr[b] = own[rows_of(b), :]

    def layer_backward(grad, count, near_at, layer, s_ref, w_ref, put_ref, slope_ref, node_slope_ref, d_node, d_recv, act_scr, acc_scr):
        d_hidden = (mm_t(grad, w_ref[layer, 5]) * node_slope_ref[...].astype(F32)).astype(BF16)
        d_node[...] = d_hidden
        d_average = (mm_t(d_hidden, w_ref[layer, 4]) * (1.0 / degree)).astype(BF16)
        act_scr[...] = mm_t(d_average, w_ref[layer, 2])
        acc_scr[...] = jnp.zeros_like(acc_scr)
        for b in range(count):
            d_active = act_scr[rows_of(b), :]
            total = None
            for e in range(degree):
                edge = b * degree + e
                d_pre = d_active * slope_ref[edge].astype(F32)
                total = d_pre if total is None else total + d_pre
                near = scalar(s_ref, near_at + edge)
                acc_scr[near] = acc_scr[near] + mm(put_ref[edge], d_pre.astype(BF16))
            d_recv[rows_of(b), :] = total.astype(BF16)

    def halo_grads_into(outs, layer, w_ref, acc_scr):
        count = acc_scr.shape[0] - rounds
        for r, out in zip(ORDER, outs):
            out[...] = mm_t(acc_scr[count + r].astype(BF16), w_ref[layer, 1]).astype(BF16)

    def own_back(grad, layer, w_ref, d_node, d_recv, d_send):
        return grad + mm_t(d_recv, w_ref[layer, 0]) + mm_t(d_node, w_ref[layer, 3]) + mm_t(d_send, w_ref[layer, 1])

    def pooled_into(read, s_ref, out_refs, with_count):
        me = scalar(s_ref, at_me)
        for mask, out in zip(masks, out_refs):
            slot = me ^ mask
            total, count = None, None
            for b in range(blocks):
                hit = (scalar(s_ref, at_pool + b) == slot).astype(F32)
                part = read(b) * hit
                total = part if total is None else total + part
                count = hit if count is None else count + hit
            out[0:size, :] = total.astype(BF16)
            if with_count:
                out[size:, :] = jnp.full((COUNT_ROWS, features), count, F32).astype(BF16)

    inputs = [
        sent,
        neighbour_blocks,
        pool_map.reshape(1, blocks),
        coarse_blocks,
        neighbour_nodes.reshape(edges, size),
        coarse_nodes.reshape(degree, size),
        weights,
        biases,
        cotangent,
    ]
    own_out = [(fine, F32), (fine, F32), (fine, BF16)]

    def prepare(*refs):
        sources, h_ref = refs[: len(inputs)], refs[len(inputs)]
        w_ref, b_ref, c_ref, s_ref, pick, put, cpick, cput, recv, node, sender, *kept, sems = refs[len(inputs) + 1 :]
        send_scr, near_scr, pool_scr, coarse_scr, ends, cends = kept
        fetch(list(zip(sources, kept + [w_ref, b_ref, c_ref])), sems)

        def put_row(index, ref, i, j):
            s_ref[index : index + 1, :] = jnp.broadcast_to(ref[i : i + 1, j : j + 1], (1, features))

        for r in range(rounds):
            put_row(r, send_scr, 0, r)
        for b in range(blocks):
            for e in range(degree):
                put_row(at_near + b * degree + e, near_scr, b, e)
            put_row(at_pool + b, pool_scr, 0, b)
        for e in range(degree):
            put_row(at_coarse + e, coarse_scr, 0, e)
        own = lax.axis_index("pair") * sub_size + lax.axis_index("sub")
        s_ref[at_me : at_me + 1, :] = jnp.full((1, features), own, I32)
        own_into(h_ref[...], 0, w_ref, b_ref, recv, node, sender)
        tables_into(ends[...], edges, pick, put)
        tables_into(cends[...], degree, cpick, cput)

    w, bias, cot, table, pick, put, coarse_pick, coarse_put, recv0, node0, sender0 = run_hbm(
        prepare,
        [
            (weights.shape, BF16), (biases.shape, F32), (fine, BF16),
            ((table_rows, features), I32),
            ((edges, size, size), BF16), ((edges, size, size), BF16),
            ((degree, size, size), BF16), ((degree, size, size), BF16),
        ] + own_out,
        inputs,
        h0,
        scratch=[pltpu.VMEM(a.shape, I32) for a in inputs[:6]] + [pltpu.SemaphoreType.DMA((len(inputs),))],
    )

    slopes = [((edges,) + tile, BF16), (fine, BF16)]
    pool_out = [((size + COUNT_ROWS, features), BF16)] * slots
    layer_scratch = [pltpu.VMEM((everyone,) + tile, BF16), pltpu.VMEM(fine, BF16)]
    coarse_scratch = [pltpu.VMEM((1 + rounds,) + tile, BF16), pltpu.VMEM(tile, BF16)]

    def first_layer(s_ref, g0, g1, h_ref, recv, node, sender, pick, w_ref, *rest):
        first_ref, slope_ref, node_slope_ref = rest[:3]
        sends, (send_scr, sum_scr) = rest[3:-2], rest[-2:]
        senders_into(sender, (g0, g1), 0, w_ref, send_scr)
        change = layer_forward(
            blocks, at_near, 0, s_ref, w_ref, recv, node, send_scr, pick, slope_ref, node_slope_ref, sum_scr
        )
        first_ref[...] = (h_ref[...].astype(F32) + change).astype(BF16)
        pooled_into(lambda b: first_ref[rows_of(b), :].astype(F32), s_ref, sends, True)

    first, slope0, node_slope0, *pool_sends = run(
        first_layer,
        [(fine, BF16)] + slopes + pool_out,
        table, halo[0], halo[1], h0, recv0, node0, sender0, pick, w,
        scratch=layer_scratch,
    )

    pool_in = spread(pool_sends)

    def coarse_begin(*refs):
        parts, (start_ref, divisor_ref) = refs[:slots], refs[slots:]
        total = parts[0][...].astype(F32)
        for part in parts[1:]:
            total = total + part[...].astype(F32)
        divisor = jnp.maximum(total[size : size + 8, :], 1.0)
        divisor_ref[...] = divisor
        start_ref[...] = (total[:size, :] / divisor[0:1, :]).astype(BF16)

    coarse_start, divisor = run(coarse_begin, [(tile, BF16), ((8, features), F32)], pool_sends[0], *pool_in)
    coarse_halo = exchange_same(coarse_start)

    def coarse_prepare(h_ref, w_ref, b_ref, recv, node, sender):
        own_into(h_ref[...], 1, w_ref, b_ref, recv, node, sender)

    recv1, node1, sender1 = run(coarse_prepare, [(tile, F32), (tile, F32), (tile, BF16)], coarse_start, w, bias)

    def coarse_layer(s_ref, g0, g1, h_ref, recv, node, sender, pick, w_ref, end_ref, slope_ref, node_slope_ref, send_scr, sum_scr):
        senders_into(sender, (g0, g1), 1, w_ref, send_scr, range(rounds))
        change = layer_forward(
            1, at_coarse, 1, s_ref, w_ref, recv, node, send_scr, pick, slope_ref, node_slope_ref, sum_scr
        )
        end_ref[...] = (h_ref[...].astype(F32) + change).astype(BF16)

    coarse_end, slope1, node_slope1 = run(
        coarse_layer,
        [(tile, BF16), ((degree,) + tile, BF16), (tile, BF16)],
        table, coarse_halo[0], coarse_halo[1], coarse_start, recv1, node1, sender1, coarse_pick, w,
        scratch=coarse_scratch,
    )
    ends_in = spread_same(coarse_end)

    def lift(s_ref, *refs):
        parts, first_ref = refs[:slots], refs[slots]
        middle_ref, out0, out1, lift_scr = refs[slots + 1 :]
        me = scalar(s_ref, at_me)
        for mask, part in zip(same_masks, parts):
            lift_scr[me ^ mask] = part[...]
        for b in range(blocks):
            lifted = lift_scr[scalar(s_ref, at_pool + b)].astype(F32)
            middle_ref[b] = (first_ref[rows_of(b), :].astype(F32) + lifted).astype(BF16)
        for r, out in zip(ORDER, (out0, out1)):
            out[...] = middle_ref[scalar(s_ref, r)]

    middle, *middle_sends = run(
        lift,
        [(tiles, BF16)] + [(tile, BF16)] * rounds,
        table, coarse_end, *ends_in, first,
        scratch=[pltpu.VMEM((slots,) + tile, BF16)],
    )
    middle = middle.reshape(fine)
    halo = exchange(middle_sends)

    def last_prepare(h_ref, w_ref, b_ref, recv, node, sender):
        own_into(h_ref[...], 2, w_ref, b_ref, recv, node, sender)

    recv2, node2, sender2 = run(last_prepare, own_out, middle, w, bias)

    back_out = [(tile, BF16)] * rounds + [(fine, BF16), (fine, BF16), (tiles, BF16)]
    back_scratch = [pltpu.VMEM(fine, F32), pltpu.VMEM((everyone,) + tile, F32)]

    def last_layer(s_ref, g0, g1, h_ref, recv, node, sender, pick, put, w_ref, cot_ref,
                   out_ref, r0, r1, d_node, d_recv, d_send,
                   send_scr, sum_scr, slope_scr, node_slope_scr, act_scr, acc_scr):
        senders_into(sender, (g0, g1), 2, w_ref, send_scr)
        change = layer_forward(
            blocks, at_near, 2, s_ref, w_ref, recv, node, send_scr, pick, slope_scr, node_slope_scr, sum_scr
        )
        out_ref[...] = (h_ref[...].astype(F32) + change).astype(BF16)
        layer_backward(
            cot_ref[...], blocks, at_near, 2, s_ref, w_ref, put, slope_scr, node_slope_scr, d_node, d_recv, act_scr, acc_scr
        )
        halo_grads_into((r0, r1), 2, w_ref, acc_scr)
        d_send[...] = acc_scr[0:blocks].astype(BF16)

    out_nodes, *rest = run(
        last_layer,
        [(fine, BF16)] + back_out,
        table, halo[0], halo[1], middle, recv2, node2, sender2, pick, put, w, cot,
        scratch=layer_scratch + [pltpu.VMEM((edges,) + tile, BF16), pltpu.VMEM(fine, BF16)] + back_scratch,
    )
    halo_grads, (d_node, d_recv, d_send) = rest[:rounds], rest[rounds:]
    returned = exchange(halo_grads)

    def last_own(cot_ref, d_node, d_recv, d_send, w_ref, grad_ref):
        grad_ref[...] = own_back(cot_ref[...].astype(F32), 2, w_ref, d_node[...], d_recv[...], d_send[...])

    (grad_own,) = run(last_own, [(fine, F32)], cot, d_node, d_recv, d_send.reshape(fine), w)

    def pool_grads(s_ref, r0, r1, own_ref, grad_ref, *sends):
        grad_ref[...] = own_ref[...]
        for r, arrived in zip(ORDER, (r0, r1)):
            at = scalar(s_ref, r)
            grad_ref[at] = grad_ref[at] + arrived[...].astype(F32)
        pooled_into(lambda b: grad_ref[b], s_ref, sends, False)

    grad_middle, *grad_sends = run(
        pool_grads,
        [(tiles, F32)] + [(tile, BF16)] * slots,
        table, returned[0], returned[1], grad_own.reshape(tiles),
    )
    grads_in = spread(grad_sends)

    def coarse_back(s_ref, *refs):
        parts = refs[:slots]
        put, slope_ref, node_slope_ref, w_ref, own_ref, r0, r1, d_node, d_recv, act_scr, acc_scr = refs[slots:]
        grad = parts[0][...].astype(F32)
        for part in parts[1:]:
            grad = grad + part[...].astype(F32)
        layer_backward(
            grad.astype(BF16), 1, at_coarse, 1, s_ref, w_ref, put, slope_ref, node_slope_ref, d_node, d_recv, act_scr, acc_scr
        )
        halo_grads_into((r0, r1), 1, w_ref, acc_scr)
        own_ref[...] = own_back(grad, 1, w_ref, d_node[...], d_recv[...], acc_scr[0].astype(BF16))

    coarse_grad, *coarse_sends = run(
        coarse_back,
        [(tile, F32)] + [(tile, BF16)] * rounds,
        table, grad_sends[0], *grads_in, coarse_put, slope1, node_slope1, w,
        scratch=[
            pltpu.VMEM(tile, BF16), pltpu.VMEM(tile, BF16), pltpu.VMEM(tile, F32), pltpu.VMEM((1 + rounds,) + tile, F32),
        ],
    )
    coarse_returned = exchange(coarse_sends)

    def scale(own_ref, r0, r1, divisor_ref, out_ref):
        total = own_ref[...] + r0[...].astype(F32) + r1[...].astype(F32)
        out_ref[...] = (total / divisor_ref[0:1, :]).astype(BF16)

    (scaled,) = run(scale, [(tile, BF16)], coarse_grad, *coarse_returned, divisor)
    scaled_in = spread_same(scaled)

    def first_back(s_ref, *refs):
        parts = refs[:slots]
        middle_ref, put, slope_ref, node_slope_ref, w_ref = refs[slots : slots + 5]
        grad_ref, r0, r1, d_node, d_recv, d_send, lift_scr, act_scr, acc_scr = refs[slots + 5 :]
        me = scalar(s_ref, at_me)
        for mask, part in zip(same_masks, parts):
            lift_scr[me ^ mask] = part[...]
        for b in range(blocks):
            lifted = lift_scr[scalar(s_ref, at_pool + b)].astype(F32)
            grad_ref[rows_of(b), :] = middle_ref[b] + lifted
        layer_backward(
            grad_ref[...].astype(BF16), blocks, at_near, 0, s_ref, w_ref, put, slope_ref, node_slope_ref, d_node, d_recv, act_scr, acc_scr
        )
        halo_grads_into((r0, r1), 0, w_ref, acc_scr)
        d_send[...] = acc_scr[0:blocks].astype(BF16)

    grad_first, *rest = run(
        first_back,
        [(fine, F32)] + back_out,
        table, scaled, *scaled_in, grad_middle, put, slope0, node_slope0, w,
        scratch=[pltpu.VMEM((slots,) + tile, BF16)] + back_scratch,
    )
    halo_grads, (d_node, d_recv, d_send) = rest[:rounds], rest[rounds:]
    returned = exchange(halo_grads)

    def first_own(first_ref, d_node, d_recv, d_send, w_ref, grad_ref):
        grad_ref[...] = own_back(first_ref[...], 0, w_ref, d_node[...], d_recv[...], d_send[...])

    (grad_own,) = run(first_own, [(fine, F32)], grad_first, d_node, d_recv, d_send.reshape(fine), w)

    def finish(s_ref, r0, r1, own_ref, out_ref):
        out_ref[...] = own_ref[...]
        for r, arrived in zip(ORDER, (r0, r1)):
            at = scalar(s_ref, r)
            out_ref[at] = out_ref[at] + arrived[...].astype(F32)

    (grad_nodes,) = run(finish, [(tiles, F32)], table, returned[0], returned[1], grad_own.reshape(tiles))
    return (out_nodes, grad_nodes.reshape(fine))


def solution(mesh):
    split = ("groups", "dom", "pair", "sub")
    placed = (
        P(split, None),
        P(split, None),
        P(split, None, None),
        P(split, None),
        P(split, None, None),
        P(split),
        P(split, None),
        P(split, None, None),
        P(),
        P(),
    )
    return jax.shard_map(
        per_device,
        mesh=mesh,
        in_specs=placed,
        out_specs=(P(split, None), P(split, None)),
        check_vma=False,
    )
```

```python
import jax
import jax.numpy as jnp
from jax import lax
from jax.experimental import pallas as pl
from jax.experimental.pallas import tpu as pltpu
from jax.sharding import PartitionSpec as P

F32 = jnp.float32
BF16 = jnp.bfloat16
I32 = jnp.int32
TAIL = 16
GROUP_AXES = ("pair", "sub")
ORDER = (1, 0)


def swapped(value, axis, mask):
    size = lax.axis_size(axis)
    return lax.ppermute(value, axis, [(source, source ^ mask) for source in range(size)])


def mm(a, b):
    return jnp.dot(a, b, preferred_element_type=F32)


def mm_t(a, b):
    return lax.dot_general(a, b, (((1,), (1,)), ((), ())), preferred_element_type=F32)


def sigmoid(x):
    return 0.5 * jnp.tanh(0.5 * x) + 0.5


def scalar(table, index):
    return table[index : index + 1, :][0, 0]


def run(kernel, outs, *arrays, scratch=(), flops=0):
    return pl.pallas_call(
        kernel,
        out_shape=[jax.ShapeDtypeStruct(shape, dtype) for shape, dtype in outs],
        in_specs=[pl.BlockSpec(memory_space=pltpu.VMEM)] * len(arrays),
        out_specs=[pl.BlockSpec(memory_space=pltpu.VMEM)] * len(outs),
        scratch_shapes=list(scratch),
        compiler_params=pltpu.CompilerParams(vmem_limit_bytes=12 * 2**20),
        cost_estimate=pl.CostEstimate(flops=flops, bytes_accessed=2**20, transcendentals=0),
    )(*arrays)


def run_hbm(kernel, outs, far, *near, scratch=()):
    return pl.pallas_call(
        kernel,
        out_shape=[pltpu.VMEM(shape, dtype) for shape, dtype in outs],
        in_specs=[pl.BlockSpec(memory_space=pltpu.HBM)] * len(far) + [pl.BlockSpec(memory_space=pltpu.VMEM)] * len(near),
        out_specs=[pl.BlockSpec(memory_space=pltpu.VMEM)] * len(outs),
        scratch_shapes=list(scratch),
        compiler_params=pltpu.CompilerParams(vmem_limit_bytes=12 * 2**20),
        cost_estimate=pl.CostEstimate(flops=0, bytes_accessed=2**20, transcendentals=0),
    )(*[pltpu.with_memory_space_constraint(array, pltpu.HBM) for array in far], *near)


def per_device(
    nodes,
    cotangent,
    send_blocks,
    neighbour_blocks,
    neighbour_nodes,
    pool_map,
    coarse_blocks,
    coarse_nodes,
    weights,
    biases,
):
    size, features = neighbour_nodes.shape[2], nodes.shape[1]
    blocks, degree = neighbour_blocks.shape
    xor_bits = (1, lax.axis_size("dom") // 2)
    rounds = len(xor_bits)
    slots = lax.axis_size(GROUP_AXES)
    pair_size, sub_size = lax.axis_size("pair"), lax.axis_size("sub")
    edges = blocks * degree
    far_size = rounds * size
    everyone = blocks + rounds
    tile = (size, features)
    fine = (blocks * size, features)
    tiles = (blocks,) + tile

    held = pair_size
    wide = (held * size, features)
    at_ends = TAIL // 2
    at_blocks = at_ends + degree
    at_near = rounds
    at_pool = at_near + edges
    at_pair = at_pool + blocks
    at_sub = at_pair + 1
    table_rows = -(-(at_sub + 1) // 8) * 8

    def exchange(pieces):
        return [swapped(piece, "dom", xor_bits[r]) for r, piece in zip(ORDER, pieces)]

    def exchange_same(piece):
        return [swapped(piece, "dom", bit) for bit in xor_bits]

    def reduced(pieces):
        arrived = [swapped(piece, "sub", mask) for mask, piece in enumerate(pieces) if mask > 0]
        (chip,) = run(add_parts, [(pieces[0].shape, BF16)], pieces[0], *arrived)
        return [chip] + [swapped(chip, "pair", mask) for mask in range(1, pair_size)]

    def add_parts(*refs):
        total = refs[0][...].astype(F32)
        for part in refs[1:-1]:
            total = total + part[...].astype(F32)
        refs[-1][...] = total.astype(BF16)

    def share(piece):
        return [piece] + [swapped(piece, "sub", mask) for mask in range(1, sub_size)]

    def rows_of(b):
        return pl.ds(b * size, size)

    def fetch(pairs, sems):
        copies = [pltpu.make_async_copy(source, target, sems.at[i]) for i, (source, target) in enumerate(pairs)]
        for copy in copies:
            copy.start()
        for copy in copies:
            copy.wait()

    def choose(send_in, nodes_in, h_ref, out0, out1, send_scr, sems):
        parts = [(nodes_in.at[rows_of(b)], h_ref.at[rows_of(b)]) for b in range(blocks)]
        fetch([(send_in, send_scr)] + parts, sems)
        for r, out in zip(ORDER, (out0, out1)):
            at = pl.multiple_of(send_scr[0:1, r : r + 1][0, 0] * size, size)
            out[...] = h_ref[pl.ds(at, size), :]

    sent = send_blocks.reshape(1, rounds)
    h0, *first_sends = run_hbm(
        choose,
        [(fine, BF16)] + [(tile, BF16)] * rounds,
        [sent, nodes],
        scratch=[pltpu.VMEM((1, rounds), I32), pltpu.SemaphoreType.DMA((1 + blocks,))],
    )
    halo = exchange(first_sends)

    def grids():
        return lax.broadcasted_iota(I32, (size, size), 0), lax.broadcasted_iota(I32, (size, size), 1)

    def own_into(state, layer, w_ref, b_ref, recv_ref, node_ref, sender_ref):
        recv_ref[...] = mm(state, w_ref[layer, 0]) + b_ref[layer, 0:1, :]
        node_ref[...] = mm(state, w_ref[layer, 3]) + b_ref[layer, 1:2, :]
        sender_ref[...] = mm(state, w_ref[layer, 1]).astype(BF16)

    def layer_forward(count, fold, pre_of, node, slope_ref, node_slope_ref, sum_scr):
        for b in range(count):
            total = None
            for e in range(degree):
                edge = b * degree + e
                pre = pre_of(b, e)
                gate = sigmoid(pre)
                active = pre * gate
                slope_ref[edge] = (gate + active * (1.0 - gate)).astype(BF16)
                total = active if total is None else total + active
            sum_scr[rows_of(b), :] = total.astype(BF16)
        hidden_pre = node[...] + mm(sum_scr[...], fold)
        gate = sigmoid(hidden_pre)
        hidden = hidden_pre * gate
        node_slope_ref[...] = (gate + hidden * (1.0 - gate)).astype(BF16)
        return hidden.astype(BF16)

    def senders_into(own, halos, layer, w_ref, send_scr):
        for r, g in zip(ORDER, halos):
            send_scr[blocks + r] = mm(g[...], w_ref[layer, 1]).astype(BF16)
        for b in range(blocks):
            send_scr[b] = own[rows_of(b), :]

    def fine_pre(s_ref, recv, pick, send_scr):
        def pre_of(b, e):
            edge = b * degree + e
            return recv[rows_of(b), :] + mm(pick[edge], send_scr[scalar(s_ref, at_near + edge)])

        return pre_of

    def node_backward(d_out, fold, node_slope_ref, d_node, act_scr):
        d_hidden = (d_out * node_slope_ref[...].astype(F32)).astype(BF16)
        d_node[...] = d_hidden
        act_scr[...] = mm_t(d_hidden, fold)

    def fine_backward(d_out, s_ref, fold, put_ref, slope_ref, node_slope_ref, d_node, d_recv, act_scr, acc_scr):
        node_backward(d_out, fold, node_slope_ref, d_node, act_scr)
        acc_scr[...] = jnp.zeros_like(acc_scr)
        for b in range(blocks):
            d_active = act_scr[rows_of(b), :]
            total = None
            for e in range(degree):
                edge = b * degree + e
                d_pre = d_active * slope_ref[edge].astype(F32)
                total = d_pre if total is None else total + d_pre
                near = scalar(s_ref, at_near + edge)
                acc_scr[near] = acc_scr[near] + mm(put_ref[edge], d_pre.astype(BF16))
            d_recv[rows_of(b), :] = total.astype(BF16)

    def halo_grads_into(outs, grads, layer, w_ref):
        for r, out in zip(ORDER, outs):
            own = jnp.concatenate([g[r * size : (r + 1) * size, :] for g in grads], axis=0)
            out[...] = mm_t(own.astype(BF16), w_ref[layer, 1]).astype(BF16)

    def own_back(grad, layer, w_ref, d_node, d_recv, d_send):
        return (
            grad
            + mm_t(d_recv, w_ref[layer, 0])
            + mm_t(d_node, w_ref[layer, 3])
            + mm_t(d_send.astype(BF16), w_ref[layer, 1])
        )

    def pooled_into(read, s_ref, out_refs, tail_ref):
        sub = scalar(s_ref, at_sub)
        rows = lax.broadcasted_iota(I32, (TAIL, features), 0)
        for sub_mask, out in enumerate(out_refs):
            tail = None if tail_ref is None else tail_ref[...]
            for q in range(held):
                slot = q * sub_size + (sub ^ sub_mask)
                total, count = None, None
                for b in range(blocks):
                    hit = (scalar(s_ref, at_pool + b) == slot).astype(F32)
                    part = read(b) * hit
                    total = part if total is None else total + part
                    count = hit if count is None else count + hit
                out[rows_of(q), :] = total.astype(BF16)
                if tail is not None:
                    tail = tail + jnp.where(rows == q, count, 0.0)
            if tail is not None:
                if sub_mask > 0:
                    tail = jnp.where(rows < at_ends, tail, 0.0)
                out[held * size :, :] = tail.astype(BF16)

    def lift_into(parts, s_ref, lift_scr):
        sub = scalar(s_ref, at_sub)
        for mask, part in enumerate(parts):
            for q in range(held):
                lift_scr[q * sub_size + (sub ^ mask)] = part[rows_of(q), :]

    inputs = [
        sent,
        neighbour_blocks,
        pool_map.reshape(1, blocks),
        coarse_blocks,
        neighbour_nodes.reshape(edges, size),
        coarse_nodes.reshape(degree, size),
        weights,
        biases,
        cotangent,
    ]
    own_out = [(fine, F32), (fine, F32), (fine, BF16)]

    def prepare(*refs):
        sources, h_ref = refs[: len(inputs)], refs[len(inputs)]
        ends, w_ref, b_ref, c_ref, s_ref, fold_ref, tail_ref, pick, recv, node, sender, *kept, sems = refs[len(inputs) + 1 :]
        send_scr, near_scr, pool_scr, coarse_scr, cends = kept
        fetch(list(zip(sources, kept[:4] + [ends, cends, w_ref, b_ref, c_ref])), sems)

        def put_row(index, ref, i, j):
            s_ref[index : index + 1, :] = jnp.broadcast_to(ref[i : i + 1, j : j + 1], (1, features))

        for r in range(rounds):
            put_row(r, send_scr, 0, r)
        for b in range(blocks):
            for e in range(degree):
                put_row(at_near + b * degree + e, near_scr, b, e)
            put_row(at_pool + b, pool_scr, 0, b)
        s_ref[at_pair : at_pair + 1, :] = jnp.full((1, features), lax.axis_index("pair"), I32)
        s_ref[at_sub : at_sub + 1, :] = jnp.full((1, features), lax.axis_index("sub"), I32)
        lanes = lax.broadcasted_iota(I32, (1, features), 1)
        listed = jnp.zeros((1, features), I32)
        for e in range(degree):
            listed = jnp.where(lanes == e, jnp.broadcast_to(coarse_scr[0:1, e : e + 1], (1, features)), listed)
        tail_ref[...] = jnp.zeros_like(tail_ref)
        tail_ref[at_ends : at_ends + degree, :] = cends[...].astype(F32)
        tail_ref[at_blocks : at_blocks + 1, :] = listed.astype(F32)
        own_into(h_ref[...], 0, w_ref, b_ref, recv, node, sender)
        columns = grids()[1]
        upright = jnp.transpose(ends[...])
        for edge in range(edges):
            pick[edge] = (columns == upright[:, edge : edge + 1]).astype(BF16)
        fold_ref[...] = (mm(w_ref[0, 2], w_ref[0, 4]) * (1.0 / degree)).astype(BF16)

    ends, w, bias, cot, table, fold0, tail, pick, recv0, node0, sender0 = run_hbm(
        prepare,
        [
            ((edges, size), I32), (weights.shape, BF16), (biases.shape, F32), (fine, BF16),
            ((table_rows, features), I32), (tile, BF16), ((TAIL, features), F32),
            ((edges, size, size), BF16),
        ] + own_out,
        inputs,
        h0,
        scratch=[pltpu.VMEM(a.shape, I32) for a in inputs[:4] + inputs[5:6]]
        + [pltpu.SemaphoreType.DMA((len(inputs),))],
    )

    slopes = [((edges,) + tile, BF16), (fine, BF16)]

    layer_scratch = [pltpu.VMEM((everyone,) + tile, BF16), pltpu.VMEM(fine, BF16)]

    def first_layer(s_ref, g0, g1, h_ref, recv, node, sender, pick, w_ref, fold_ref, tail_ref, *rest):
        first_ref, slope_ref, node_slope_ref, *sends, send_scr, sum_scr = rest
        senders_into(sender, (g0, g1), 0, w_ref, send_scr)
        pre_of = fine_pre(s_ref, recv, pick, send_scr)
        hidden = layer_forward(blocks, fold_ref[...], pre_of, node, slope_ref, node_slope_ref, sum_scr)
        first_ref[...] = (h_ref[...].astype(F32) + mm(hidden, w_ref[0, 5])).astype(BF16)
        pooled_into(lambda b: first_ref[rows_of(b), :].astype(F32), s_ref, sends, tail_ref)

    first, slope0, node_slope0, *pool_sends = run(
        first_layer,
        [(fine, BF16)] + slopes + [((held * size + TAIL, features), BF16)] * sub_size,
        table, halo[0], halo[1], h0, recv0, node0, sender0, pick, w, fold0, tail,
        scratch=layer_scratch,
    )

    pool_in = reduced(pool_sends)

    def coarse_begin(s_ref, *refs):
        parts, (start_ref, divisor_ref, tails_ref) = refs[:pair_size], refs[pair_size:]
        total = parts[0][...].astype(F32)
        for part in parts[1:]:
            total = total + part[...].astype(F32)
        divisor = jnp.maximum(total[held * size : held * size + at_ends, :], 1.0)
        divisor_ref[...] = divisor
        for q in range(held):
            start_ref[rows_of(q), :] = (total[q * size : (q + 1) * size, :] / divisor[q : q + 1, :]).astype(BF16)
        pair = scalar(s_ref, at_pair)
        for mask, part in enumerate(parts):
            tails_ref[pair ^ mask] = part[held * size :, :].astype(F32)

    coarse_start, divisor, tails = run(
        coarse_begin,
        [(wide, BF16), ((at_ends, features), F32), ((held, TAIL, features), F32)],
        table, *pool_in,
    )
    coarse_halo = exchange_same(coarse_start)

    def coarse_prepare(h_ref, w_ref, b_ref, tails_ref, ends, pre, node, fold_ref, far_pick, cput, put, recv, sender):
        own_into(h_ref[...], 1, w_ref, b_ref, recv, node, sender)
        for i, layer in enumerate((1, 2)):
            fold_ref[i] = (mm(w_ref[layer, 2], w_ref[layer, 4]) * (1.0 / degree)).astype(BF16)
        rows, columns = grids()
        for q in range(held):
            around = tails_ref[q].astype(I32)
            upright = jnp.transpose(tails_ref[q]).astype(I32)
            own = sender[rows_of(q), :]
            for e in range(degree):
                edge = q * degree + e
                at = at_ends + e
                near = jnp.broadcast_to(around[at_blocks : at_blocks + 1, e : e + 1], (1, size))
                to = rows == around[at : at + 1, :]
                hit = columns == upright[:, at : at + 1]
                picked = mm((hit & (near == 0)).astype(BF16), own)
                pre[edge] = recv[rows_of(q), :] + picked
                for r in range(rounds):
                    far_pick[rows_of(edge), r * size : (r + 1) * size] = (hit & (near == 1 + r)).astype(BF16)
                for r in range(1 + rounds):
                    cput[q, r * size : (r + 1) * size, e * size : (e + 1) * size] = (to & (near == r)).astype(BF16)
        for edge in range(edges):
            put[edge] = (rows == ends[edge : edge + 1, :]).astype(BF16)

    pre1, node1, fold, coarse_far, coarse_put, put = run(
        coarse_prepare,
        [
            ((held * degree,) + tile, F32), (wide, F32), ((2,) + tile, BF16),
            ((held * degree * size, far_size), BF16), ((held, size + far_size, degree * size), BF16),
            ((edges, size, size), BF16),
        ],
        coarse_start, w, bias, tails, ends,
        scratch=[pltpu.VMEM(wide, F32), pltpu.VMEM(wide, BF16)],
    )

    def coarse_layer(g0, g1, h_ref, pre, node, far_pick, w_ref, fold_ref, end_ref, slope_ref, node_slope_ref, sum_scr):
        arrived = [mm(g[...], w_ref[1, 1]).astype(BF16) for g in (g0, g1)]
        picked = []
        for q in range(held):
            senders = jnp.concatenate([a[q * size : (q + 1) * size, :] for a in arrived], axis=0)
            width = degree * size
            picked.append(mm(far_pick[q * width : (q + 1) * width, :], senders))

        def pre_of(q, e):
            return pre[q * degree + e] + picked[q][e * size : (e + 1) * size, :]

        hidden = layer_forward(held, fold_ref[0], pre_of, node, slope_ref, node_slope_ref, sum_scr)
        end_ref[...] = (h_ref[...].astype(F32) + mm(hidden, w_ref[1, 5])).astype(BF16)

    coarse_end, slope1, node_slope1 = run(
        coarse_layer,
        [(wide, BF16), ((held * degree,) + tile, BF16), (wide, BF16)],
        coarse_halo[0], coarse_halo[1], coarse_start, pre1, node1, coarse_far, w, fold,
        scratch=[pltpu.VMEM(wide, BF16)],
    )
    coarse_ends = share(coarse_end)

    def lift(s_ref, *refs):
        parts, first_ref = refs[:sub_size], refs[sub_size]
        middle_ref, out0, out1, lift_scr = refs[sub_size + 1 :]
        lift_into(parts, s_ref, lift_scr)
        for b in range(blocks):
            lifted = lift_scr[scalar(s_ref, at_pool + b)].astype(F32)
            middle_ref[b] = (first_ref[rows_of(b), :].astype(F32) + lifted).astype(BF16)
        for r, out in zip(ORDER, (out0, out1)):
            out[...] = middle_ref[scalar(s_ref, r)]

    middle, *middle_sends = run(
        lift,
        [(tiles, BF16)] + [(tile, BF16)] * rounds,
        table, *coarse_ends, first,
        scratch=[pltpu.VMEM((slots,) + tile, BF16)],
    )
    middle = middle.reshape(fine)
    halo = exchange(middle_sends)

    def last_prepare(h_ref, w_ref, b_ref, cot_ref, recv, node, sender, d_out):
        own_into(h_ref[...], 2, w_ref, b_ref, recv, node, sender)
        d_out[...] = mm_t(cot_ref[...], w_ref[2, 5])

    recv2, node2, sender2, d_out2 = run(last_prepare, own_out + [(fine, F32)], middle, w, bias, cot)

    back_out = [(tile, BF16)] * rounds + [(fine, BF16), (fine, BF16), (tiles, BF16)]
    back_scratch = [pltpu.VMEM(fine, F32), pltpu.VMEM((everyone,) + tile, F32)]

    def last_layer(s_ref, g0, g1, recv, node, sender, pick, put, w_ref, fold_ref, d_out,
                   r0, r1, d_node, d_recv, d_send, hidden_ref,
                   send_scr, sum_scr, slope_scr, node_slope_scr, act_scr, acc_scr):
        senders_into(sender, (g0, g1), 2, w_ref, send_scr)
        fold = fold_ref[1]
        pre_of = fine_pre(s_ref, recv, pick, send_scr)
        hidden_ref[...] = layer_forward(blocks, fold, pre_of, node, slope_scr, node_slope_scr, sum_scr)
        fine_backward(d_out[...], s_ref, fold, put, slope_scr, node_slope_scr, d_node, d_recv, act_scr, acc_scr)
        halo_grads_into((r0, r1), [acc_scr[blocks:].reshape(far_size, features)], 2, w_ref)
        d_send[...] = acc_scr[0:blocks].astype(BF16)

    *halo_grads, d_node, d_recv, d_send, hidden2 = run(
        last_layer,
        back_out + [(fine, BF16)],
        table, halo[0], halo[1], recv2, node2, sender2, pick, put, w, fold, d_out2,
        scratch=layer_scratch + [pltpu.VMEM((edges,) + tile, BF16), pltpu.VMEM(fine, BF16)] + back_scratch,
    )
    returned = exchange(halo_grads)

    def last_own(cot_ref, d_node, d_recv, d_send, h_ref, hidden_ref, w_ref, grad_ref, out_ref):
        grad_ref[...] = own_back(cot_ref[...].astype(F32), 2, w_ref, d_node[...], d_recv[...], d_send[...])
        out_ref[...] = (h_ref[...].astype(F32) + mm(hidden_ref[...], w_ref[2, 5])).astype(BF16)

    grad_own, out_nodes = run(
        last_own, [(fine, F32), (fine, BF16)], cot, d_node, d_recv, d_send.reshape(fine), middle, hidden2, w
    )

    def pool_grads(s_ref, r0, r1, own_ref, grad_ref, *sends):
        grad_ref[...] = own_ref[...]
        for r, arrived in zip(ORDER, (r0, r1)):
            at = scalar(s_ref, r)
            grad_ref[at] = grad_ref[at] + arrived[...].astype(F32)
        pooled_into(lambda b: grad_ref[b], s_ref, sends, None)

    grad_middle, *grad_sends = run(
        pool_grads,
        [(tiles, F32)] + [(wide, BF16)] * sub_size,
        table, returned[0], returned[1], grad_own.reshape(tiles),
    )
    grads_in = reduced(grad_sends)

    def coarse_back(*refs):
        parts = refs[:pair_size]
        put, slope_ref, node_slope_ref, w_ref, fold_ref, r0, r1, grad_ref, d_node, d_pre, act_scr = refs[pair_size:]
        grad = parts[0][...].astype(F32)
        for part in parts[1:]:
            grad = grad + part[...].astype(F32)
        grad_ref[...] = grad
        d_out = mm_t(grad.astype(BF16), w_ref[1, 5])
        node_backward(d_out, fold_ref[0], node_slope_ref, d_node, act_scr)
        for q in range(held):
            for e in range(degree):
                edge = q * degree + e
                d_pre[rows_of(edge), :] = (act_scr[rows_of(q), :] * slope_ref[edge].astype(F32)).astype(BF16)
        width = degree * size
        grads = [mm(put[q, size:, :], d_pre[q * width : (q + 1) * width, :]) for q in range(held)]
        halo_grads_into((r0, r1), grads, 1, w_ref)

    *coarse_sends, coarse_grad, d_node, d_pre = run(
        coarse_back,
        [(wide, BF16)] * rounds + [(wide, F32), (wide, BF16), ((held * degree * size, features), BF16)],
        *grads_in, coarse_put, slope1, node_slope1, w, fold,
        scratch=[pltpu.VMEM(wide, F32)],
    )
    coarse_returned = exchange(coarse_sends)

    def coarse_own(grad_ref, put, d_node, d_pre, w_ref, own_ref):
        width = degree * size
        d_send = [mm(put[q, 0:size, :], d_pre[q * width : (q + 1) * width, :]) for q in range(held)]
        d_recv = []
        for q in range(held):
            total = None
            for e in range(degree):
                part = d_pre[rows_of(q * degree + e), :].astype(F32)
                total = part if total is None else total + part
            d_recv.append(total.astype(BF16))
        own_ref[...] = own_back(
            grad_ref[...], 1, w_ref, d_node[...], jnp.concatenate(d_recv, axis=0), jnp.concatenate(d_send, axis=0)
        )

    (coarse_grad,) = run(coarse_own, [(wide, F32)], coarse_grad, coarse_put, d_node, d_pre, w)

    def scale(own_ref, r0, r1, divisor_ref, out_ref):
        for q in range(held):
            rows = rows_of(q)
            total = own_ref[rows, :] + r0[rows, :].astype(F32) + r1[rows, :].astype(F32)
            out_ref[rows, :] = (total / divisor_ref[q : q + 1, :]).astype(BF16)

    (scaled,) = run(scale, [(wide, BF16)], coarse_grad, *coarse_returned, divisor)
    scaled_parts = share(scaled)

    def first_back(s_ref, *refs):
        parts = refs[:sub_size]
        middle_ref, put, slope_ref, node_slope_ref, w_ref, fold_ref = refs[sub_size : sub_size + 6]
        r0, r1, d_node, d_recv, d_send, grad_ref, lift_scr, act_scr, acc_scr = refs[sub_size + 6 :]
        lift_into(parts, s_ref, lift_scr)
        for b in range(blocks):
            lifted = lift_scr[scalar(s_ref, at_pool + b)].astype(F32)
            grad_ref[rows_of(b), :] = middle_ref[b] + lifted
        d_out = mm_t(grad_ref[...].astype(BF16), w_ref[0, 5])
        fine_backward(d_out, s_ref, fold_ref[...], put, slope_ref, node_slope_ref, d_node, d_recv, act_scr, acc_scr)
        halo_grads_into((r0, r1), [acc_scr[blocks:].reshape(far_size, features)], 0, w_ref)
        d_send[...] = acc_scr[0:blocks].astype(BF16)

    *halo_grads, d_node, d_recv, d_send, grad_first = run(
        first_back,
        back_out + [(fine, F32)],
        table, *scaled_parts, grad_middle, put, slope0, node_slope0, w, fold0,
        scratch=[pltpu.VMEM((slots,) + tile, BF16)] + back_scratch,
    )
    returned = exchange(halo_grads)

    def first_own(first_ref, d_node, d_recv, d_send, w_ref, grad_ref):
        grad_ref[...] = own_back(first_ref[...], 0, w_ref, d_node[...], d_recv[...], d_send[...])

    (grad_own,) = run(first_own, [(fine, F32)], grad_first, d_node, d_recv, d_send.reshape(fine), w)

    def finish(s_ref, r0, r1, own_ref, out_ref):
        out_ref[...] = own_ref[...]
        for r, arrived in zip(ORDER, (r0, r1)):
            at = scalar(s_ref, r)
            out_ref[at] = out_ref[at] + arrived[...].astype(F32)

    (grad_nodes,) = run(finish, [(tiles, F32)], table, returned[0], returned[1], grad_own.reshape(tiles))
    return (out_nodes, grad_nodes.reshape(fine))


def solution(mesh):
    split = ("groups", "dom", "pair", "sub")
    placed = (
        P(split, None),
        P(split, None),
        P(split, None, None),
        P(split, None),
        P(split, None, None),
        P(split),
        P(split, None),
        P(split, None, None),
        P(),
        P(),
    )
    return jax.shard_map(
        per_device,
        mesh=mesh,
        in_specs=placed,
        out_specs=(P(split, None), P(split, None)),
        check_vma=False,
    )
```

```python
import jax
import jax.numpy as jnp
from jax import lax
from jax.experimental import pallas as pl
from jax.experimental.pallas import tpu as pltpu
from jax.sharding import PartitionSpec as P

F32 = jnp.float32
BF16 = jnp.bfloat16
I32 = jnp.int32
TAIL = 16
GROUP_AXES = ("pair", "sub")
ORDER = (1, 0)


def swapped(value, axis, mask):
    size = lax.axis_size(axis)
    return lax.ppermute(value, axis, [(source, source ^ mask) for source in range(size)])


def mm(a, b):
    return jnp.dot(a, b, preferred_element_type=F32)


def mm_t(a, b):
    return lax.dot_general(a, b, (((1,), (1,)), ((), ())), preferred_element_type=F32)


def scalar(table, index):
    return table[index : index + 1, :][0, 0]


def run(kernel, outs, *arrays, scratch=(), flops=0):
    return pl.pallas_call(
        kernel,
        out_shape=[jax.ShapeDtypeStruct(shape, dtype) for shape, dtype in outs],
        in_specs=[pl.BlockSpec(memory_space=pltpu.VMEM)] * len(arrays),
        out_specs=[pl.BlockSpec(memory_space=pltpu.VMEM)] * len(outs),
        scratch_shapes=list(scratch),
        compiler_params=pltpu.CompilerParams(vmem_limit_bytes=12 * 2**20),
        cost_estimate=pl.CostEstimate(flops=flops, bytes_accessed=2**20, transcendentals=0),
    )(*arrays)


def run_hbm(kernel, outs, far, *near, scratch=()):
    return pl.pallas_call(
        kernel,
        out_shape=[pltpu.VMEM(shape, dtype) for shape, dtype in outs],
        in_specs=[pl.BlockSpec(memory_space=pltpu.HBM)] * len(far) + [pl.BlockSpec(memory_space=pltpu.VMEM)] * len(near),
        out_specs=[pl.BlockSpec(memory_space=pltpu.VMEM)] * len(outs),
        scratch_shapes=list(scratch),
        compiler_params=pltpu.CompilerParams(vmem_limit_bytes=12 * 2**20),
        cost_estimate=pl.CostEstimate(flops=0, bytes_accessed=2**20, transcendentals=0),
    )(*[pltpu.with_memory_space_constraint(array, pltpu.HBM) for array in far], *near)


def per_device(
    nodes,
    cotangent,
    send_blocks,
    neighbour_blocks,
    neighbour_nodes,
    pool_map,
    coarse_blocks,
    coarse_nodes,
    weights,
    biases,
):
    size, features = neighbour_nodes.shape[2], nodes.shape[1]
    blocks, degree = neighbour_blocks.shape
    xor_bits = (1, lax.axis_size("dom") // 2)
    rounds = len(xor_bits)
    slots = lax.axis_size(GROUP_AXES)
    pair_size, sub_size = lax.axis_size("pair"), lax.axis_size("sub")
    edges = blocks * degree
    far_size = rounds * size
    everyone = blocks + rounds
    tile = (size, features)
    fine = (blocks * size, features)
    tiles = (blocks,) + tile

    held = pair_size
    wide = (held * size, features)
    at_listed = degree
    doms = 1 + rounds
    at_info = held * size + TAIL
    pool_rows = at_info + doms * TAIL
    at_first = held * size
    halo_rows = at_first + size + TAIL
    at_near = rounds
    at_pool = at_near + edges
    at_pair = at_pool + blocks
    at_sub = at_pair + 1
    at_sent = at_sub + 1
    table_rows = -(-(at_sent + rounds) // 8) * 8

    def exchange(pieces):
        return [swapped(piece, "dom", xor_bits[r]) for r, piece in zip(ORDER, pieces)]

    def reduced(pieces):
        arrived = [swapped(piece, "sub", mask) for mask, piece in enumerate(pieces) if mask > 0]
        (chip,) = run(add_parts, [(pieces[0].shape, BF16)], pieces[0], *arrived)
        return [chip] + [swapped(chip, "pair", mask) for mask in range(1, pair_size)]

    def add_parts(*refs):
        own, out = refs[0], refs[-1]
        shared = refs[1].shape[0] if len(refs) > 2 else own.shape[0]
        total = own[0:shared, :].astype(F32)
        for part in refs[1:-1]:
            total = total + part[...].astype(F32)
        out[0:shared, :] = total.astype(BF16)
        if shared < own.shape[0]:
            out[shared:, :] = own[shared:, :]

    def share(piece):
        return [piece] + [swapped(piece, "sub", mask) for mask in range(1, sub_size)]

    def rows_of(b):
        return pl.ds(b * size, size)

    def fetch(pairs, sems):
        copies = [pltpu.make_async_copy(source, target, sems.at[i]) for i, (source, target) in enumerate(pairs)]
        for copy in copies:
            copy.start()
        for copy in copies:
            copy.wait()

    def choose(send_in, ends_in, listed_in, nodes_in, h_ref, info_ref, out0, out1, send_scr, ends_scr, listed_scr, sems):
        parts = [(nodes_in.at[rows_of(b)], h_ref.at[rows_of(b)]) for b in range(blocks)]
        fetch([(send_in, send_scr), (ends_in, ends_scr), (listed_in, listed_scr)] + parts, sems)
        lanes = lax.broadcasted_iota(I32, (1, features), 1)
        listed = jnp.zeros((1, features), I32)
        for e in range(degree):
            listed = jnp.where(lanes == e, jnp.broadcast_to(listed_scr[0:1, e : e + 1], (1, features)), listed)
        rest = jnp.zeros((TAIL - degree - 1, features), F32)
        info = jnp.concatenate([ends_scr[...].astype(F32), listed.astype(F32), rest], axis=0).astype(BF16)
        info_ref[...] = info
        for r, out in zip(ORDER, (out0, out1)):
            at = pl.multiple_of(send_scr[0:1, r : r + 1][0, 0] * size, size)
            out[0:size, :] = h_ref[pl.ds(at, size), :]
            out[size:, :] = info

    sent = send_blocks.reshape(1, rounds)
    coarse_ends = coarse_nodes.reshape(degree, size)
    h0, info, *first_sends = run_hbm(
        choose,
        [(fine, BF16), ((TAIL, features), BF16)] + [((size + TAIL, features), BF16)] * rounds,
        [sent, coarse_ends, coarse_blocks, nodes],
        scratch=[pltpu.VMEM(a.shape, I32) for a in (sent, coarse_ends, coarse_blocks)]
        + [pltpu.SemaphoreType.DMA((3 + blocks,))],
    )
    halo = exchange(first_sends)

    def grids():
        return lax.broadcasted_iota(I32, (size, size), 0), lax.broadcasted_iota(I32, (size, size), 1)

    def own_into(state, layer, w_ref, b_ref, recv_ref, node_ref, sender_ref):
        recv_ref[...] = 0.5 * (mm(state, w_ref[layer, 0]) + b_ref[layer, 0:1, :])
        node_ref[...] = 0.5 * (mm(state, w_ref[layer, 3]) + b_ref[layer, 1:2, :])
        sender_ref[...] = (0.5 * mm(state, w_ref[layer, 1])).astype(BF16)

    def layer_forward(count, fold, pre_of, node, slope_ref, node_slope_ref, sum_scr):
        for b in range(count):
            total = None
            for e in range(degree):
                edge = b * degree + e
                half = pre_of(b, e)
                up = 1.0 + jnp.tanh(half)
                active = half * up
                if edge < slope_ref.shape[0]:
                    slope_ref[edge] = (up + active * (2.0 - up)).astype(BF16)
                total = active if total is None else total + active
            sum_scr[rows_of(b), :] = total.astype(BF16)
        half = node + mm(sum_scr[...], fold)
        up = 1.0 + jnp.tanh(half)
        hidden = half * up
        kept = node_slope_ref.shape[0]
        node_slope_ref[...] = (0.5 * (up + hidden * (2.0 - up))).astype(BF16)[0:kept, :]
        return hidden.astype(BF16)

    def senders_into(own, halos, layer, w_ref, send_scr):
        for r, g in zip(ORDER, halos):
            send_scr[blocks + r] = (0.5 * mm(g, w_ref[layer, 1])).astype(BF16)
        for b in range(blocks):
            send_scr[b] = own[rows_of(b), :]

    def fine_pre(s_ref, recv, pick, send_scr):
        def pre_of(b, e):
            edge = b * degree + e
            return recv[rows_of(b), :] + mm(pick[edge], send_scr[scalar(s_ref, at_near + edge)])

        return pre_of

    def node_backward(d_out, fold, node_slope_ref, d_node, act_scr):
        d_hidden = (d_out * node_slope_ref[...].astype(F32)).astype(BF16)
        d_node[...] = d_hidden
        act_scr[...] = mm_t(d_hidden, fold)

    def fine_backward(d_out, s_ref, fold, put_ref, slope_ref, node_slope_ref, d_node, d_recv, act_scr, acc_scr):
        node_backward(d_out, fold, node_slope_ref, d_node, act_scr)
        acc_scr[...] = jnp.zeros_like(acc_scr)
        for b in range(blocks):
            d_active = act_scr[rows_of(b), :]
            total = None
            for e in range(degree):
                edge = b * degree + e
                d_pre = d_active * slope_ref[edge].astype(F32)
                total = d_pre if total is None else total + d_pre
                near = scalar(s_ref, at_near + edge)
                acc_scr[near] = acc_scr[near] + mm(put_ref[edge], d_pre.astype(BF16))
            d_recv[rows_of(b), :] = total.astype(BF16)

    def halo_grads_into(outs, grads, layer, w_ref):
        for r, out in zip(ORDER, outs):
            own = jnp.concatenate([g[r * size : (r + 1) * size, :] for g in grads], axis=0)
            out[...] = mm_t(own.astype(BF16), w_ref[layer, 1]).astype(BF16)

    def own_back(grad, layer, w_ref, d_node, d_recv, d_send):
        return (
            grad
            + mm_t(d_recv, w_ref[layer, 0])
            + mm_t(d_node, w_ref[layer, 3])
            + mm_t(d_send.astype(BF16), w_ref[layer, 1])
        )

    def pooled_into(read, s_ref, out_refs, with_count):
        sub = scalar(s_ref, at_sub)
        rows = lax.broadcasted_iota(I32, (TAIL, features), 0)
        for sub_mask, out in enumerate(out_refs):
            counts = jnp.zeros((TAIL, features), F32)
            for q in range(held):
                slot = q * sub_size + (sub ^ sub_mask)
                total, count = None, None
                for b in range(blocks):
                    hit = (scalar(s_ref, at_pool + b) == slot).astype(F32)
                    part = read(b) * hit
                    total = part if total is None else total + part
                    count = hit if count is None else count + hit
                out[rows_of(q), :] = total.astype(BF16)
                counts = counts + jnp.where(rows == q, count, 0.0)
            if with_count:
                out[held * size : at_info, :] = counts.astype(BF16)

    def lift_into(parts, s_ref, lift_scr):
        sub = scalar(s_ref, at_sub)
        for mask, part in enumerate(parts):
            for q in range(held):
                for v in range(part.shape[0] // (held * size)):
                    lift_scr[v * slots + q * sub_size + (sub ^ mask)] = part[rows_of(v * held + q), :]

    inputs = [
        sent,
        neighbour_blocks,
        pool_map.reshape(1, blocks),
        neighbour_nodes.reshape(edges, size),
        weights,
        biases,
        cotangent,
    ]
    own_out = [(fine, F32), (fine, F32), (fine, BF16)]

    def prepare(*refs):
        sources, h_ref = refs[: len(inputs)], refs[len(inputs)]
        ends, w_ref, b_ref, c_ref, s_ref, fold_ref, pick, recv, node, sender, *kept, sems = refs[len(inputs) + 1 :]
        send_scr, near_scr, pool_scr = kept
        fetch(list(zip(sources, kept + [ends, w_ref, b_ref, c_ref])), sems)

        def put_row(index, ref, i, j):
            s_ref[index : index + 1, :] = jnp.broadcast_to(ref[i : i + 1, j : j + 1], (1, features))

        for r in range(rounds):
            put_row(r, send_scr, 0, r)
        for b in range(blocks):
            for e in range(degree):
                put_row(at_near + b * degree + e, near_scr, b, e)
            put_row(at_pool + b, pool_scr, 0, b)
        s_ref[at_pair : at_pair + 1, :] = jnp.full((1, features), lax.axis_index("pair"), I32)
        s_ref[at_sub : at_sub + 1, :] = jnp.full((1, features), lax.axis_index("sub"), I32)
        for r in range(rounds):
            slot = jnp.zeros((1, features), I32)
            for b in range(blocks):
                slot = jnp.where(s_ref[r : r + 1, :] == b, s_ref[at_pool + b : at_pool + b + 1, :], slot)
            s_ref[at_sent + r : at_sent + r + 1, :] = slot
        own_into(h_ref[...], 0, w_ref, b_ref, recv, node, sender)
        columns = grids()[1]
        upright = jnp.transpose(ends[...])
        for edge in range(edges):
            pick[edge] = (columns == upright[:, edge : edge + 1]).astype(BF16)
        fold_ref[...] = (mm(w_ref[0, 2], w_ref[0, 4]) * (0.5 / degree)).astype(BF16)

    ends, w, bias, cot, table, fold0, pick, recv0, node0, sender0 = run_hbm(
        prepare,
        [
            ((edges, size), I32), (weights.shape, BF16), (biases.shape, F32), (fine, BF16),
            ((table_rows, features), I32), (tile, BF16),
            ((edges, size, size), BF16),
        ] + own_out,
        inputs,
        h0,
        scratch=[pltpu.VMEM(a.shape, I32) for a in inputs[:3]]
        + [pltpu.SemaphoreType.DMA((len(inputs),))],
    )

    slopes = [((edges,) + tile, BF16), (fine, BF16)]

    layer_scratch = [pltpu.VMEM((everyone,) + tile, BF16), pltpu.VMEM(fine, BF16)]

    def first_layer(s_ref, g0, g1, h_ref, recv, node, sender, pick, w_ref, fold_ref, info_ref, *rest):
        first_ref, slope_ref, node_slope_ref, *sends, send_scr, sum_scr = rest
        senders_into(sender, (g0[0:size, :], g1[0:size, :]), 0, w_ref, send_scr)
        pre_of = fine_pre(s_ref, recv, pick, send_scr)
        hidden = layer_forward(blocks, fold_ref[...], pre_of, node[...], slope_ref, node_slope_ref, sum_scr)
        first_ref[...] = (h_ref[...].astype(F32) + mm(hidden, w_ref[0, 5])).astype(BF16)
        pooled_into(lambda b: first_ref[rows_of(b), :].astype(F32), s_ref, sends, True)
        sends[0][at_info : at_info + TAIL, :] = info_ref[...]
        for r, g in zip(ORDER, (g0, g1)):
            sends[0][at_info + (1 + r) * TAIL : at_info + (2 + r) * TAIL, :] = g[size:, :]

    first, slope0, node_slope0, *pool_sends = run(
        first_layer,
        [(fine, BF16)] + slopes + [((pool_rows, features), BF16)] + [((at_info, features), BF16)] * (sub_size - 1),
        table, halo[0], halo[1], h0, recv0, node0, sender0, pick, w, fold0, info,
        scratch=layer_scratch,
    )

    pool_in = reduced(pool_sends)

    def coarse_begin(s_ref, first_ref, *refs):
        parts, (start_ref, divisor_ref, infos_ref, other, out0, out1) = refs[:pair_size], refs[pair_size:]
        total = parts[0][0:at_info, :].astype(F32)
        for part in parts[1:]:
            total = total + part[0:at_info, :].astype(F32)
        divisor = jnp.maximum(total[held * size : held * size + 8, :], 1.0)
        divisor_ref[...] = divisor
        for q in range(held):
            start = (total[q * size : (q + 1) * size, :] / divisor[q : q + 1, :]).astype(BF16)
            for out in (start_ref, other, out0, out1):
                out[rows_of(q), :] = start
        for r, out in zip(ORDER, (out0, out1)):
            at = pl.multiple_of(scalar(s_ref, r) * size, size)
            out[at_first : at_first + size, :] = first_ref[pl.ds(at, size), :]
            slot = s_ref[at_sent + r : at_sent + r + 1, :].astype(F32)
            out[at_first + size :, :] = jnp.broadcast_to(slot, (TAIL, features)).astype(BF16)
        pair = scalar(s_ref, at_pair)
        for mask, part in enumerate(parts):
            for v in range(doms):
                at = at_info + v * TAIL
                infos_ref[v * held + (pair ^ mask)] = part[at : at + TAIL, :].astype(F32)

    coarse_start, divisor, infos, other_send, *halo_sends = run(
        coarse_begin,
        [(wide, BF16), ((8, features), F32), ((doms * held, TAIL, features), F32), (wide, BF16)]
        + [((halo_rows, features), BF16)] * rounds,
        table, first, *pool_in,
    )
    other = swapped(other_send, "dom", xor_bits[0] ^ xor_bits[1])
    coarse_halo = exchange(halo_sends)

    def coarse_prepare(h_ref, w_ref, b_ref, cot_ref, infos_ref, ends, pre, node, fold_ref, far_pick, cput, put, d_out, recv, sender):
        own_into(h_ref[...], 1, w_ref, b_ref, recv, node, sender)
        for i, layer in enumerate((1, 2)):
            fold_ref[i] = (mm(w_ref[layer, 2], w_ref[layer, 4]) * (0.5 / degree)).astype(BF16)
        d_out[...] = mm_t(cot_ref[...], w_ref[2, 5])
        rows, columns = grids()
        for v in range(doms):
            for q in range(held):
                tile_at = v * held + q
                around = infos_ref[tile_at].astype(I32)
                upright = jnp.transpose(infos_ref[tile_at]).astype(I32)
                own = sender[rows_of(q), :]
                for e in range(degree):
                    edge = tile_at * degree + e
                    near = jnp.broadcast_to(around[at_listed : at_listed + 1, e : e + 1], (1, size))
                    hit = columns == upright[:, e : e + 1]
                    picked = mm((hit & (near == v)).astype(BF16), own)
                    pre[edge] = picked + recv[rows_of(q), :] if v == 0 else picked
                    for i, source in enumerate([n for n in range(doms) if n != v]):
                        far_pick[rows_of(edge), i * size : (i + 1) * size] = (hit & (near == source)).astype(BF16)
                    if v == 0:
                        to = rows == around[e : e + 1, :]
                        for r in range(doms):
                            cput[q, r * size : (r + 1) * size, e * size : (e + 1) * size] = (to & (near == r)).astype(BF16)
        for edge in range(edges):
            put[edge] = (rows == ends[edge : edge + 1, :]).astype(BF16)

    coarse_edges = doms * held * degree
    pre1, node1, fold, coarse_far, coarse_put, put, d_out2 = run(
        coarse_prepare,
        [
            ((coarse_edges,) + tile, F32), (wide, F32), ((2,) + tile, BF16),
            ((coarse_edges * size, far_size), BF16), ((held, size + far_size, degree * size), BF16),
            ((edges, size, size), BF16), (fine, F32),
        ],
        coarse_start, w, bias, cot, infos, ends,
        scratch=[pltpu.VMEM(wide, F32), pltpu.VMEM(wide, BF16)],
    )

    def coarse_layer(other_ref, g0, g1, h_ref, pre, node, far_pick, w_ref, b_ref, fold_ref, end_ref, slope_ref, node_slope_ref, slots_ref, sum_scr):
        halos = [g[0:at_first, :] for _, g in sorted(zip(ORDER, (g0, g1)))]
        states = [h_ref[...]] + halos
        third = (0.5 * mm(other_ref[...], w_ref[1, 1])).astype(BF16)
        arrived = [(0.5 * mm(g, w_ref[1, 1])).astype(BF16) for g in halos]
        recvs = [None] + [0.5 * (mm(g, w_ref[1, 0]) + b_ref[1, 0:1, :]) for g in halos]
        nodes_all = [node[...]] + [0.5 * (mm(g, w_ref[1, 3]) + b_ref[1, 1:2, :]) for g in halos]
        sources = [arrived, [arrived[0], third], [arrived[1], third]]
        width = degree * size
        picked = []
        for v in range(doms):
            for q in range(held):
                at = (v * held + q) * width
                senders = jnp.concatenate([a[q * size : (q + 1) * size, :] for a in sources[v]], axis=0)
                picked.append(mm(far_pick[at : at + width, :], senders))

        def pre_of(b, e):
            v, q = divmod(b, held)
            value = pre[b * degree + e] + picked[b][e * size : (e + 1) * size, :]
            return value if v == 0 else value + recvs[v][q * size : (q + 1) * size, :]

        hidden = layer_forward(
            doms * held, fold_ref[0], pre_of, jnp.concatenate(nodes_all, axis=0), slope_ref, node_slope_ref, sum_scr
        )
        state = jnp.concatenate(states, axis=0).astype(F32)
        end_ref[...] = (state + mm(hidden, w_ref[1, 5])).astype(BF16)
        for r, g in zip(ORDER, (g0, g1)):
            slots_ref[r * 8 : (r + 1) * 8, :] = g[at_first + size :, :].astype(F32).astype(I32)[0:8, :]

    coarse_end, slope1, node_slope1, halo_slots = run(
        coarse_layer,
        [((doms * held * size, features), BF16), ((held * degree,) + tile, BF16), (wide, BF16), ((rounds * 8, features), I32)],
        other, coarse_halo[0], coarse_halo[1], coarse_start, pre1, node1, coarse_far, w, bias, fold,
        scratch=[pltpu.VMEM((doms * held * size, features), BF16)],
    )
    coarse_ends = share(coarse_end)

    back_out = [(tile, BF16)] * rounds + [(fine, BF16), (fine, BF16), (tiles, BF16)]
    back_scratch = [pltpu.VMEM(fine, F32), pltpu.VMEM((everyone,) + tile, F32)]

    def last_layer(s_ref, slots_ref, g0, g1, *refs):
        parts = refs[:sub_size]
        first_ref, pick, put, w_ref, b_ref, fold_ref, d_out = refs[sub_size : sub_size + 7]
        (r0, r1, d_node, d_recv, d_send, hidden_ref, middle_ref,
         lift_scr, recv, node, sender, send_scr, sum_scr, slope_scr, node_slope_scr, act_scr, acc_scr) = refs[sub_size + 7 :]
        lift_into(parts, s_ref, lift_scr)
        for b in range(blocks):
            lifted = lift_scr[scalar(s_ref, at_pool + b)].astype(F32)
            middle_ref[rows_of(b), :] = (first_ref[rows_of(b), :].astype(F32) + lifted).astype(BF16)
        halos = []
        for r, g in zip(ORDER, (g0, g1)):
            lifted = lift_scr[(1 + r) * slots + scalar(slots_ref, r * 8)].astype(F32)
            halos.append((g[at_first : at_first + size, :].astype(F32) + lifted).astype(BF16))
        own_into(middle_ref[...], 2, w_ref, b_ref, recv, node, sender)
        senders_into(sender, halos, 2, w_ref, send_scr)
        fold = fold_ref[1]
        pre_of = fine_pre(s_ref, recv, pick, send_scr)
        hidden_ref[...] = layer_forward(blocks, fold, pre_of, node[...], slope_scr, node_slope_scr, sum_scr)
        fine_backward(d_out[...], s_ref, fold, put, slope_scr, node_slope_scr, d_node, d_recv, act_scr, acc_scr)
        halo_grads_into((r0, r1), [acc_scr[blocks:].reshape(far_size, features)], 2, w_ref)
        d_send[...] = acc_scr[0:blocks].astype(BF16)

    *halo_grads, d_node, d_recv, d_send, hidden2, middle = run(
        last_layer,
        back_out + [(fine, BF16), (fine, BF16)],
        table, halo_slots, *coarse_halo, *coarse_ends, first, pick, put, w, bias, fold, d_out2,
        scratch=[pltpu.VMEM((doms * slots,) + tile, BF16)]
        + [pltpu.VMEM(fine, F32), pltpu.VMEM(fine, F32), pltpu.VMEM(fine, BF16)]
        + layer_scratch + [pltpu.VMEM((edges,) + tile, BF16), pltpu.VMEM(fine, BF16)] + back_scratch,
    )
    returned = exchange(halo_grads)

    def last_own(cot_ref, d_node, d_recv, d_send, h_ref, hidden_ref, w_ref, grad_ref, out_ref):
        grad_ref[...] = own_back(cot_ref[...].astype(F32), 2, w_ref, d_node[...], d_recv[...], d_send[...])
        out_ref[...] = (h_ref[...].astype(F32) + mm(hidden_ref[...], w_ref[2, 5])).astype(BF16)

    grad_own, out_nodes = run(
        last_own, [(fine, F32), (fine, BF16)], cot, d_node, d_recv, d_send.reshape(fine), middle, hidden2, w
    )

    def pool_grads(s_ref, r0, r1, own_ref, grad_ref, *sends):
        grad_ref[...] = own_ref[...]
        for r, arrived in zip(ORDER, (r0, r1)):
            at = scalar(s_ref, r)
            grad_ref[at] = grad_ref[at] + arrived[...].astype(F32)
        pooled_into(lambda b: grad_ref[b], s_ref, sends, False)

    grad_middle, *grad_sends = run(
        pool_grads,
        [(tiles, F32)] + [(wide, BF16)] * sub_size,
        table, returned[0], returned[1], grad_own.reshape(tiles),
    )
    grads_in = reduced(grad_sends)

    def coarse_back(*refs):
        parts = refs[:pair_size]
        put, slope_ref, node_slope_ref, w_ref, fold_ref, r0, r1, grad_ref, d_node, d_pre, act_scr = refs[pair_size:]
        grad = parts[0][...].astype(F32)
        for part in parts[1:]:
            grad = grad + part[...].astype(F32)
        grad_ref[...] = grad
        d_out = mm_t(grad.astype(BF16), w_ref[1, 5])
        node_backward(d_out, fold_ref[0], node_slope_ref, d_node, act_scr)
        for q in range(held):
            for e in range(degree):
                edge = q * degree + e
                d_pre[rows_of(edge), :] = (act_scr[rows_of(q), :] * slope_ref[edge].astype(F32)).astype(BF16)
        width = degree * size
        grads = [mm(put[q, size:, :], d_pre[q * width : (q + 1) * width, :]) for q in range(held)]
        halo_grads_into((r0, r1), grads, 1, w_ref)

    *coarse_sends, coarse_grad, d_node, d_pre = run(
        coarse_back,
        [(wide, BF16)] * rounds + [(wide, F32), (wide, BF16), ((held * degree * size, features), BF16)],
        *grads_in, coarse_put, slope1, node_slope1, w, fold,
        scratch=[pltpu.VMEM(wide, F32)],
    )
    coarse_returned = exchange(coarse_sends)

    def coarse_own(grad_ref, put, d_node, d_pre, w_ref, own_ref):
        width = degree * size
        d_send = [mm(put[q, 0:size, :], d_pre[q * width : (q + 1) * width, :]) for q in range(held)]
        d_recv = []
        for q in range(held):
            total = None
            for e in range(degree):
                part = d_pre[rows_of(q * degree + e), :].astype(F32)
                total = part if total is None else total + part
            d_recv.append(total.astype(BF16))
        own_ref[...] = own_back(
            grad_ref[...], 1, w_ref, d_node[...], jnp.concatenate(d_recv, axis=0), jnp.concatenate(d_send, axis=0)
        )

    (coarse_grad,) = run(coarse_own, [(wide, F32)], coarse_grad, coarse_put, d_node, d_pre, w)

    def scale(own_ref, r0, r1, divisor_ref, out_ref):
        for q in range(held):
            rows = rows_of(q)
            total = own_ref[rows, :] + r0[rows, :].astype(F32) + r1[rows, :].astype(F32)
            out_ref[rows, :] = (total / divisor_ref[q : q + 1, :]).astype(BF16)

    (scaled,) = run(scale, [(wide, BF16)], coarse_grad, *coarse_returned, divisor)
    scaled_parts = share(scaled)

    def first_back(s_ref, *refs):
        parts = refs[:sub_size]
        middle_ref, put, slope_ref, node_slope_ref, w_ref, fold_ref = refs[sub_size : sub_size + 6]
        r0, r1, d_node, d_recv, d_send, grad_ref, lift_scr, act_scr, acc_scr = refs[sub_size + 6 :]
        lift_into(parts, s_ref, lift_scr)
        for b in range(blocks):
            lifted = lift_scr[scalar(s_ref, at_pool + b)].astype(F32)
            grad_ref[rows_of(b), :] = middle_ref[b] + lifted
        d_out = mm_t(grad_ref[...].astype(BF16), w_ref[0, 5])
        fine_backward(d_out, s_ref, fold_ref[...], put, slope_ref, node_slope_ref, d_node, d_recv, act_scr, acc_scr)
        halo_grads_into((r0, r1), [acc_scr[blocks:].reshape(far_size, features)], 0, w_ref)
        d_send[...] = acc_scr[0:blocks].astype(BF16)

    *halo_grads, d_node, d_recv, d_send, grad_first = run(
        first_back,
        back_out + [(fine, F32)],
        table, *scaled_parts, grad_middle, put, slope0, node_slope0, w, fold0,
        scratch=[pltpu.VMEM((slots,) + tile, BF16)] + back_scratch,
    )
    returned = exchange(halo_grads)

    def first_own(first_ref, d_node, d_recv, d_send, w_ref, grad_ref):
        grad_ref[...] = own_back(first_ref[...], 0, w_ref, d_node[...], d_recv[...], d_send[...])

    (grad_own,) = run(first_own, [(fine, F32)], grad_first, d_node, d_recv, d_send.reshape(fine), w)

    def finish(s_ref, r0, r1, own_ref, out_ref):
        out_ref[...] = own_ref[...]
        for r, arrived in zip(ORDER, (r0, r1)):
            at = scalar(s_ref, r)
            out_ref[at] = out_ref[at] + arrived[...].astype(F32)

    (grad_nodes,) = run(finish, [(tiles, F32)], table, returned[0], returned[1], grad_own.reshape(tiles))
    return (out_nodes, grad_nodes.reshape(fine))


def solution(mesh):
    split = ("groups", "dom", "pair", "sub")
    placed = (
        P(split, None),
        P(split, None),
        P(split, None, None),
        P(split, None),
        P(split, None, None),
        P(split),
        P(split, None),
        P(split, None, None),
        P(),
        P(),
    )
    return jax.shard_map(
        per_device,
        mesh=mesh,
        in_specs=placed,
        out_specs=(P(split, None), P(split, None)),
        check_vma=False,
    )
```

```python
import jax
import jax.numpy as jnp
from jax import lax
from jax.experimental import pallas as pl
from jax.experimental.pallas import tpu as pltpu
from jax.sharding import PartitionSpec as P

F32 = jnp.float32
BF16 = jnp.bfloat16
I32 = jnp.int32
TAIL = 16
GROUP_AXES = ("pair", "sub")
ORDER = (1, 0)


def swapped(value, axis, mask):
    size = lax.axis_size(axis)
    return lax.ppermute(value, axis, [(source, source ^ mask) for source in range(size)])


def mm(a, b):
    return jnp.dot(a, b, preferred_element_type=F32)


def mm_t(a, b):
    return lax.dot_general(a, b, (((1,), (1,)), ((), ())), preferred_element_type=F32)


def scalar(table, index):
    return table[index : index + 1, :][0, 0]


def run(kernel, outs, *arrays, scratch=(), flops=0):
    return pl.pallas_call(
        kernel,
        out_shape=[jax.ShapeDtypeStruct(shape, dtype) for shape, dtype in outs],
        in_specs=[pl.BlockSpec(memory_space=pltpu.VMEM)] * len(arrays),
        out_specs=[pl.BlockSpec(memory_space=pltpu.VMEM)] * len(outs),
        scratch_shapes=list(scratch),
        compiler_params=pltpu.CompilerParams(vmem_limit_bytes=12 * 2**20),
        cost_estimate=pl.CostEstimate(flops=flops, bytes_accessed=2**20, transcendentals=0),
    )(*arrays)


def run_hbm(kernel, outs, far, *near, scratch=()):
    return pl.pallas_call(
        kernel,
        out_shape=[pltpu.VMEM(shape, dtype) for shape, dtype in outs],
        in_specs=[pl.BlockSpec(memory_space=pltpu.HBM)] * len(far) + [pl.BlockSpec(memory_space=pltpu.VMEM)] * len(near),
        out_specs=[pl.BlockSpec(memory_space=pltpu.VMEM)] * len(outs),
        scratch_shapes=list(scratch),
        compiler_params=pltpu.CompilerParams(vmem_limit_bytes=12 * 2**20),
        cost_estimate=pl.CostEstimate(flops=0, bytes_accessed=2**20, transcendentals=0),
    )(*[pltpu.with_memory_space_constraint(array, pltpu.HBM) for array in far], *near)


def per_device(
    nodes,
    cotangent,
    send_blocks,
    neighbour_blocks,
    neighbour_nodes,
    pool_map,
    coarse_blocks,
    coarse_nodes,
    weights,
    biases,
):
    size, features = neighbour_nodes.shape[2], nodes.shape[1]
    blocks, degree = neighbour_blocks.shape
    xor_bits = (1, lax.axis_size("dom") // 2)
    rounds = len(xor_bits)
    slots = lax.axis_size(GROUP_AXES)
    pair_size, sub_size = lax.axis_size("pair"), lax.axis_size("sub")
    edges = blocks * degree
    far_size = rounds * size
    everyone = blocks + rounds
    tile = (size, features)
    fine = (blocks * size, features)
    tiles = (blocks,) + tile

    held = pair_size
    wide = (held * size, features)
    doms = 1 + rounds
    listed_rows = degree + 1
    at_last = doms * listed_rows
    at_tail = held * size
    pool_rows = at_tail + TAIL
    halo_rows = at_tail + size

    at_near = rounds
    at_pool = at_near + edges
    at_pair = at_pool + blocks
    at_sub = at_pair + 1
    table_rows = -(-(at_sub + 1) // 8) * 8

    def exchange(pieces):
        return [swapped(piece, "dom", xor_bits[r]) for r, piece in zip(ORDER, pieces)]

    def reduced(pieces):
        arrived = [swapped(piece, "sub", mask) for mask, piece in enumerate(pieces) if mask > 0]
        (chip,) = run(add_parts, [(pieces[0].shape, BF16)], pieces[0], *arrived)
        return [chip] + [swapped(chip, "pair", mask) for mask in range(1, pair_size)]

    def add_parts(*refs):
        total = refs[0][...].astype(F32)
        for part in refs[1:-1]:
            total = total + part[...].astype(F32)
        refs[-1][...] = total.astype(BF16)

    def share(piece):
        return [piece] + [swapped(piece, "sub", mask) for mask in range(1, sub_size)]

    def rows_of(b):
        return pl.ds(b * size, size)

    def fetch(pairs, sems):
        copies = [pltpu.make_async_copy(source, target, sems.at[i]) for i, (source, target) in enumerate(pairs)]
        for copy in copies:
            copy.start()
        for copy in copies:
            copy.wait()

    def choose(send_in, ends_in, listed_in, pool_in, nodes_in, h_ref, info_ref, out0, out1,
               send_scr, ends_scr, listed_scr, pool_scr, sems):
        parts = [(nodes_in.at[rows_of(b)], h_ref.at[rows_of(b)]) for b in range(blocks)]
        fetch([(send_in, send_scr), (ends_in, ends_scr), (listed_in, listed_scr), (pool_in, pool_scr)] + parts, sems)
        lanes = lax.broadcasted_iota(I32, (1, features), 1)
        listed = jnp.zeros((1, features), I32)
        for e in range(degree):
            listed = jnp.where(lanes == e, jnp.broadcast_to(listed_scr[0:1, e : e + 1], (1, features)), listed)
        listed = [ends_scr[...].astype(F32), listed.astype(F32)]

        def tail_of(v, last):
            before = [jnp.zeros((v * listed_rows, features), F32)] if v else []
            left = TAIL - 1 - (v + 1) * listed_rows
            after = [jnp.zeros((left, features), F32)] if left else []
            return jnp.concatenate(before + listed + after + [last.astype(F32)], axis=0).astype(BF16)

        info_ref[...] = tail_of(0, jnp.zeros((1, features), I32))
        for r, out in zip(ORDER, (out0, out1)):
            chosen = send_scr[0:1, r : r + 1]
            at = pl.multiple_of(chosen[0, 0] * size, size)
            out[0:size, :] = h_ref[pl.ds(at, size), :]
            slot = jnp.zeros((1, 1), I32)
            for b in range(blocks):
                slot = jnp.where(chosen == b, pool_scr[0:1, b : b + 1], slot)
            out[size:, :] = tail_of(1 + r, jnp.broadcast_to(slot, (1, features)))

    sent = send_blocks.reshape(1, rounds)
    coarse_ends = coarse_nodes.reshape(degree, size)
    pools = pool_map.reshape(1, blocks)
    h0, info, *first_sends = run_hbm(
        choose,
        [(fine, BF16), ((TAIL, features), BF16)] + [((size + TAIL, features), BF16)] * rounds,
        [sent, coarse_ends, coarse_blocks, pools, nodes],
        scratch=[pltpu.VMEM(a.shape, I32) for a in (sent, coarse_ends, coarse_blocks, pools)]
        + [pltpu.SemaphoreType.DMA((4 + blocks,))],
    )
    halo = exchange(first_sends)

    def grids():
        return lax.broadcasted_iota(I32, (size, size), 0), lax.broadcasted_iota(I32, (size, size), 1)

    def own_into(state, layer, w_ref, b_ref, recv_ref, node_ref, sender_ref):
        recv_ref[...] = 0.5 * (mm(state, w_ref[layer, 0]) + b_ref[layer, 0:1, :])
        node_ref[...] = 0.5 * (mm(state, w_ref[layer, 3]) + b_ref[layer, 1:2, :])
        sender_ref[...] = (0.5 * mm(state, w_ref[layer, 1])).astype(BF16)

    def layer_forward(count, fold, pre_of, node, slope_ref, node_slope_ref, sum_scr):
        for b in range(count):
            total = None
            for e in range(degree):
                edge = b * degree + e
                half = pre_of(b, e)
                up = 1.0 + jnp.tanh(half)
                active = half * up
                if edge < slope_ref.shape[0]:
                    slope_ref[edge] = (up + active * (2.0 - up)).astype(BF16)
                total = active if total is None else total + active
            sum_scr[rows_of(b), :] = total.astype(BF16)
        half = node + mm(sum_scr[...], fold)
        up = 1.0 + jnp.tanh(half)
        hidden = half * up
        kept = node_slope_ref.shape[0]
        node_slope_ref[...] = (0.5 * (up + hidden * (2.0 - up))).astype(BF16)[0:kept, :]
        return hidden.astype(BF16)

    def senders_into(own, halos, layer, w_ref, send_scr):
        for r, g in zip(ORDER, halos):
            send_scr[blocks + r] = (0.5 * mm(g, w_ref[layer, 1])).astype(BF16)
        for b in range(blocks):
            send_scr[b] = own[rows_of(b), :]

    def fine_pre(s_ref, recv, pick, send_scr):
        def pre_of(b, e):
            edge = b * degree + e
            return recv[rows_of(b), :] + mm(pick[edge], send_scr[scalar(s_ref, at_near + edge)])

        return pre_of

    def node_backward(d_out, fold, node_slope_ref, d_node, act_scr):
        d_hidden = (d_out * node_slope_ref[...].astype(F32)).astype(BF16)
        d_node[...] = d_hidden
        act_scr[...] = mm_t(d_hidden, fold)

    def fine_backward(d_out, s_ref, fold, put_ref, slope_ref, node_slope_ref, d_node, d_recv, act_scr, acc_scr):
        node_backward(d_out, fold, node_slope_ref, d_node, act_scr)
        acc_scr[...] = jnp.zeros_like(acc_scr)
        for b in range(blocks):
            d_active = act_scr[rows_of(b), :]
            total = None
            for e in range(degree):
                edge = b * degree + e
                d_pre = d_active * slope_ref[edge].astype(F32)
                total = d_pre if total is None else total + d_pre
                near = scalar(s_ref, at_near + edge)
                acc_scr[near] = acc_scr[near] + mm(put_ref[edge], d_pre.astype(BF16))
            d_recv[rows_of(b), :] = total.astype(BF16)

    def halo_grads_into(outs, grads, layer, w_ref):
        for r, out in zip(ORDER, outs):
            own = jnp.concatenate([g[r * size : (r + 1) * size, :] for g in grads], axis=0)
            out[...] = mm_t(own.astype(BF16), w_ref[layer, 1]).astype(BF16)

    def own_back(grad, layer, w_ref, d_node, d_recv, d_send):
        return (
            grad
            + mm_t(d_recv, w_ref[layer, 0])
            + mm_t(d_node, w_ref[layer, 3])
            + mm_t(d_send.astype(BF16), w_ref[layer, 1])
        )

    def pooled_into(read, s_ref, out_refs, tail=None):
        sub = scalar(s_ref, at_sub)
        lanes = lax.broadcasted_iota(I32, (1, features), 1)
        for sub_mask, out in enumerate(out_refs):
            counts = jnp.zeros((1, features), F32)
            for q in range(held):
                slot = q * sub_size + (sub ^ sub_mask)
                total, count = None, None
                for b in range(blocks):
                    hit = (scalar(s_ref, at_pool + b) == slot).astype(F32)
                    part = read(b) * hit
                    total = part if total is None else total + part
                    count = hit if count is None else count + hit
                out[rows_of(q), :] = total.astype(BF16)
                counts = counts + jnp.where(lanes == q, count, 0.0)
            if tail is not None:
                last = lax.broadcasted_iota(I32, (TAIL, features), 0) == at_last
                kept = tail if sub_mask == 0 else jnp.zeros_like(tail)
                out[at_tail:, :] = jnp.where(last, jnp.broadcast_to(counts, tail.shape), kept).astype(BF16)

    def lift_into(parts, s_ref, lift_scr):
        sub = scalar(s_ref, at_sub)
        for mask, part in enumerate(parts):
            for q in range(held):
                for v in range(part.shape[0] // (held * size)):
                    lift_scr[v * slots + q * sub_size + (sub ^ mask)] = part[rows_of(v * held + q), :]

    inputs = [
        sent,
        neighbour_blocks,
        pools,
        neighbour_nodes.reshape(edges, size),
        weights,
        biases,
        cotangent,
    ]
    own_out = [(fine, F32), (fine, F32), (fine, BF16)]

    def prepare(*refs):
        sources, h_ref = refs[: len(inputs)], refs[len(inputs)]
        ends, w_ref, b_ref, c_ref, s_ref, fold_ref, pick, recv, node, sender, *kept, sems = refs[len(inputs) + 1 :]
        send_scr, near_scr, pool_scr = kept
        fetch(list(zip(sources, kept + [ends, w_ref, b_ref, c_ref])), sems)

        def put_row(index, ref, i, j):
            s_ref[index : index + 1, :] = jnp.broadcast_to(ref[i : i + 1, j : j + 1], (1, features))

        for r in range(rounds):
            put_row(r, send_scr, 0, r)
        for b in range(blocks):
            for e in range(degree):
                put_row(at_near + b * degree + e, near_scr, b, e)
            put_row(at_pool + b, pool_scr, 0, b)
        s_ref[at_pair : at_pair + 1, :] = jnp.full((1, features), lax.axis_index("pair"), I32)
        s_ref[at_sub : at_sub + 1, :] = jnp.full((1, features), lax.axis_index("sub"), I32)
        own_into(h_ref[...], 0, w_ref, b_ref, recv, node, sender)
        columns = grids()[1]
        upright = jnp.transpose(ends[...])
        for edge in range(edges):
            pick[edge] = (columns == upright[:, edge : edge + 1]).astype(BF16)
        fold_ref[...] = (mm(w_ref[0, 2], w_ref[0, 4]) * (0.5 / degree)).astype(BF16)

    ends, w, bias, cot, table, fold0, pick, recv0, node0, sender0 = run_hbm(
        prepare,
        [
            ((edges, size), I32), (weights.shape, BF16), (biases.shape, F32), (fine, BF16),
            ((table_rows, features), I32), (tile, BF16),
            ((edges, size, size), BF16),
        ] + own_out,
        inputs,
        h0,
        scratch=[pltpu.VMEM(a.shape, I32) for a in inputs[:3]]
        + [pltpu.SemaphoreType.DMA((len(inputs),))],
    )

    slopes = [((edges,) + tile, BF16), (fine, BF16)]

    layer_scratch = [pltpu.VMEM((everyone,) + tile, BF16), pltpu.VMEM(fine, BF16)]

    def first_layer(s_ref, g0, g1, h_ref, recv, node, sender, pick, w_ref, fold_ref, info_ref, *rest):
        first_ref, slope_ref, node_slope_ref, slots_ref, *sends, send_scr, sum_scr = rest
        senders_into(sender, (g0[0:size, :], g1[0:size, :]), 0, w_ref, send_scr)
        pre_of = fine_pre(s_ref, recv, pick, send_scr)
        hidden = layer_forward(blocks, fold_ref[...], pre_of, node[...], slope_ref, node_slope_ref, sum_scr)
        first_ref[...] = (h_ref[...].astype(F32) + mm(hidden, w_ref[0, 5])).astype(BF16)
        tail = info_ref[...].astype(F32) + g0[size:, :].astype(F32) + g1[size:, :].astype(F32)
        pooled_into(lambda b: first_ref[rows_of(b), :].astype(F32), s_ref, sends, tail)
        for r, g in zip(ORDER, (g0, g1)):
            last = g[size:, :].astype(F32).astype(I32)[at_last : at_last + 1, :]
            slots_ref[r : r + 1, :] = last

    first, slope0, node_slope0, halo_slots, *pool_sends = run(
        first_layer,
        [(fine, BF16)] + slopes + [((8, features), I32)] + [((pool_rows, features), BF16)] * sub_size,
        table, halo[0], halo[1], h0, recv0, node0, sender0, pick, w, fold0, info,
        scratch=layer_scratch,
    )

    pool_in = reduced(pool_sends)

    def coarse_begin(s_ref, first_ref, *refs):
        parts, (start_ref, divisor_ref, infos_ref, other, out0, out1) = refs[:pair_size], refs[pair_size:]
        total = parts[0][0:at_tail, :].astype(F32)
        tails = [part[at_tail:, :].astype(F32) for part in parts]
        counts = tails[0][at_last : at_last + 1, :]
        for part, tail in zip(parts[1:], tails[1:]):
            total = total + part[0:at_tail, :].astype(F32)
            counts = counts + tail[at_last : at_last + 1, :]
        for q in range(held):
            divisor_ref[q : q + 1, :] = jnp.broadcast_to(jnp.maximum(counts[:, q : q + 1], 1.0), (1, features))
        for q in range(held):
            start = (total[q * size : (q + 1) * size, :] / divisor_ref[q : q + 1, :]).astype(BF16)
            for out in (start_ref, other, out0, out1):
                out[rows_of(q), :] = start
        for r, out in zip(ORDER, (out0, out1)):
            at = pl.multiple_of(scalar(s_ref, r) * size, size)
            out[at_tail:, :] = first_ref[pl.ds(at, size), :]
        pair = scalar(s_ref, at_pair)
        for mask, tail in enumerate(tails):
            infos_ref[pair ^ mask] = tail

    coarse_start, divisor, infos, other_send, *halo_sends = run(
        coarse_begin,
        [(wide, BF16), ((8, features), F32), ((held, TAIL, features), F32), (wide, BF16)]
        + [((halo_rows, features), BF16)] * rounds,
        table, first, *pool_in,
    )
    other = swapped(other_send, "dom", xor_bits[0] ^ xor_bits[1])
    coarse_halo = exchange(halo_sends)

    def coarse_prepare(h_ref, w_ref, b_ref, cot_ref, infos_ref, ends, pre, node, fold_ref, far_pick, cput, put, d_out, recv, sender):
        own_into(h_ref[...], 1, w_ref, b_ref, recv, node, sender)
        for i, layer in enumerate((1, 2)):
            fold_ref[i] = (mm(w_ref[layer, 2], w_ref[layer, 4]) * (0.5 / degree)).astype(BF16)
        d_out[...] = mm_t(cot_ref[...], w_ref[2, 5])
        rows, columns = grids()
        for v in range(doms):
            for q in range(held):
                tile_at = v * held + q
                around = infos_ref[q].astype(I32)
                upright = jnp.transpose(infos_ref[q]).astype(I32)
                listed = (v + 1) * listed_rows - 1
                own = sender[rows_of(q), :]
                for e in range(degree):
                    edge = tile_at * degree + e
                    near = jnp.broadcast_to(around[listed : listed + 1, e : e + 1], (1, size))
                    at = v * listed_rows + e
                    hit = columns == upright[:, at : at + 1]
                    picked = mm((hit & (near == v)).astype(BF16), own)
                    pre[edge] = picked + recv[rows_of(q), :] if v == 0 else picked
                    for i, source in enumerate([n for n in range(doms) if n != v]):
                        far_pick[rows_of(edge), i * size : (i + 1) * size] = (hit & (near == source)).astype(BF16)
                    if v == 0:
                        to = rows == around[e : e + 1, :]
                        for r in range(doms):
                            cput[q, r * size : (r + 1) * size, e * size : (e + 1) * size] = (to & (near == r)).astype(BF16)
        for edge in range(edges):
            put[edge] = (rows == ends[edge : edge + 1, :]).astype(BF16)

    coarse_edges = doms * held * degree
    pre1, node1, fold, coarse_far, coarse_put, put, d_out2 = run(
        coarse_prepare,
        [
            ((coarse_edges,) + tile, F32), (wide, F32), ((2,) + tile, BF16),
            ((coarse_edges * size, far_size), BF16), ((held, size + far_size, degree * size), BF16),
            ((edges, size, size), BF16), (fine, F32),
        ],
        coarse_start, w, bias, cot, infos, ends,
        scratch=[pltpu.VMEM(wide, F32), pltpu.VMEM(wide, BF16)],
    )

    def coarse_layer(other_ref, g0, g1, h_ref, pre, node, far_pick, w_ref, b_ref, fold_ref, end_ref, slope_ref, node_slope_ref, sum_scr):
        halos = [g[0:at_tail, :] for _, g in sorted(zip(ORDER, (g0, g1)))]
        states = [h_ref[...]] + halos
        third = (0.5 * mm(other_ref[...], w_ref[1, 1])).astype(BF16)
        arrived = [(0.5 * mm(g, w_ref[1, 1])).astype(BF16) for g in halos]
        recvs = [None] + [0.5 * (mm(g, w_ref[1, 0]) + b_ref[1, 0:1, :]) for g in halos]
        nodes_all = [node[...]] + [0.5 * (mm(g, w_ref[1, 3]) + b_ref[1, 1:2, :]) for g in halos]
        sources = [arrived, [arrived[0], third], [arrived[1], third]]
        width = degree * size
        picked = []
        for v in range(doms):
            for q in range(held):
                at = (v * held + q) * width
                senders = jnp.concatenate([a[q * size : (q + 1) * size, :] for a in sources[v]], axis=0)
                picked.append(mm(far_pick[at : at + width, :], senders))

        def pre_of(b, e):
            v, q = divmod(b, held)
            value = pre[b * degree + e] + picked[b][e * size : (e + 1) * size, :]
            return value if v == 0 else value + recvs[v][q * size : (q + 1) * size, :]

        hidden = layer_forward(
            doms * held, fold_ref[0], pre_of, jnp.concatenate(nodes_all, axis=0), slope_ref, node_slope_ref, sum_scr
        )
        state = jnp.concatenate(states, axis=0).astype(F32)
        end_ref[...] = (state + mm(hidden, w_ref[1, 5])).astype(BF16)
    coarse_end, slope1, node_slope1 = run(
        coarse_layer,
        [((doms * held * size, features), BF16), ((held * degree,) + tile, BF16), (wide, BF16)],
        other, coarse_halo[0], coarse_halo[1], coarse_start, pre1, node1, coarse_far, w, bias, fold,
        scratch=[pltpu.VMEM((doms * held * size, features), BF16)],
    )
    coarse_ends = share(coarse_end)

    back_out = [(tile, BF16)] * rounds + [(fine, BF16), (fine, BF16), (tiles, BF16)]
    back_scratch = [pltpu.VMEM(fine, F32), pltpu.VMEM((everyone,) + tile, F32)]

    def last_layer(s_ref, slots_ref, g0, g1, *refs):
        parts = refs[:sub_size]
        first_ref, pick, put, w_ref, b_ref, fold_ref, d_out = refs[sub_size : sub_size + 7]
        (r0, r1, d_node, d_recv, d_send, hidden_ref, middle_ref,
         lift_scr, recv, node, sender, send_scr, sum_scr, slope_scr, node_slope_scr, act_scr, acc_scr) = refs[sub_size + 7 :]
        lift_into(parts, s_ref, lift_scr)
        for b in range(blocks):
            lifted = lift_scr[scalar(s_ref, at_pool + b)].astype(F32)
            middle_ref[rows_of(b), :] = (first_ref[rows_of(b), :].astype(F32) + lifted).astype(BF16)
        halos = []
        for r, g in zip(ORDER, (g0, g1)):
            lifted = lift_scr[(1 + r) * slots + scalar(slots_ref, r)].astype(F32)
            halos.append((g[at_tail:, :].astype(F32) + lifted).astype(BF16))
        own_into(middle_ref[...], 2, w_ref, b_ref, recv, node, sender)
        senders_into(sender, halos, 2, w_ref, send_scr)
        fold = fold_ref[1]
        pre_of = fine_pre(s_ref, recv, pick, send_scr)
        hidden_ref[...] = layer_forward(blocks, fold, pre_of, node[...], slope_scr, node_slope_scr, sum_scr)
        fine_backward(d_out[...], s_ref, fold, put, slope_scr, node_slope_scr, d_node, d_recv, act_scr, acc_scr)
        halo_grads_into((r0, r1), [acc_scr[blocks:].reshape(far_size, features)], 2, w_ref)
        d_send[...] = acc_scr[0:blocks].astype(BF16)

    *halo_grads, d_node, d_recv, d_send, hidden2, middle = run(
        last_layer,
        back_out + [(fine, BF16), (fine, BF16)],
        table, halo_slots, *coarse_halo, *coarse_ends, first, pick, put, w, bias, fold, d_out2,
        scratch=[pltpu.VMEM((doms * slots,) + tile, BF16)]
        + [pltpu.VMEM(fine, F32), pltpu.VMEM(fine, F32), pltpu.VMEM(fine, BF16)]
        + layer_scratch + [pltpu.VMEM((edges,) + tile, BF16), pltpu.VMEM(fine, BF16)] + back_scratch,
    )
    returned = exchange(halo_grads)

    def last_own(cot_ref, d_node, d_recv, d_send, h_ref, hidden_ref, w_ref, grad_ref, out_ref):
        grad_ref[...] = own_back(cot_ref[...].astype(F32), 2, w_ref, d_node[...], d_recv[...], d_send[...])
        out_ref[...] = (h_ref[...].astype(F32) + mm(hidden_ref[...], w_ref[2, 5])).astype(BF16)

    grad_own, out_nodes = run(
        last_own, [(fine, F32), (fine, BF16)], cot, d_node, d_recv, d_send.reshape(fine), middle, hidden2, w
    )

    def pool_grads(s_ref, r0, r1, own_ref, grad_ref, *sends):
        grad_ref[...] = own_ref[...]
        for r, arrived in zip(ORDER, (r0, r1)):
            at = scalar(s_ref, r)
            grad_ref[at] = grad_ref[at] + arrived[...].astype(F32)
        pooled_into(lambda b: grad_ref[b], s_ref, sends)

    grad_middle, *grad_sends = run(
        pool_grads,
        [(tiles, F32)] + [(wide, BF16)] * sub_size,
        table, returned[0], returned[1], grad_own.reshape(tiles),
    )
    grads_in = reduced(grad_sends)

    def coarse_back(*refs):
        parts = refs[:pair_size]
        put, slope_ref, node_slope_ref, w_ref, fold_ref, r0, r1, grad_ref, d_node, d_pre, act_scr = refs[pair_size:]
        grad = parts[0][...].astype(F32)
        for part in parts[1:]:
            grad = grad + part[...].astype(F32)
        grad_ref[...] = grad
        d_out = mm_t(grad.astype(BF16), w_ref[1, 5])
        node_backward(d_out, fold_ref[0], node_slope_ref, d_node, act_scr)
        for q in range(held):
            for e in range(degree):
                edge = q * degree + e
                d_pre[rows_of(edge), :] = (act_scr[rows_of(q), :] * slope_ref[edge].astype(F32)).astype(BF16)
        width = degree * size
        grads = [mm(put[q, size:, :], d_pre[q * width : (q + 1) * width, :]) for q in range(held)]
        halo_grads_into((r0, r1), grads, 1, w_ref)

    *coarse_sends, coarse_grad, d_node, d_pre = run(
        coarse_back,
        [(wide, BF16)] * rounds + [(wide, F32), (wide, BF16), ((held * degree * size, features), BF16)],
        *grads_in, coarse_put, slope1, node_slope1, w, fold,
        scratch=[pltpu.VMEM(wide, F32)],
    )
    coarse_returned = exchange(coarse_sends)

    def coarse_own(grad_ref, put, d_node, d_pre, w_ref, own_ref):
        width = degree * size
        d_send = [mm(put[q, 0:size, :], d_pre[q * width : (q + 1) * width, :]) for q in range(held)]
        d_recv = []
        for q in range(held):
            total = None
            for e in range(degree):
                part = d_pre[rows_of(q * degree + e), :].astype(F32)
                total = part if total is None else total + part
            d_recv.append(total.astype(BF16))
        own_ref[...] = own_back(
            grad_ref[...], 1, w_ref, d_node[...], jnp.concatenate(d_recv, axis=0), jnp.concatenate(d_send, axis=0)
        )

    (coarse_grad,) = run(coarse_own, [(wide, F32)], coarse_grad, coarse_put, d_node, d_pre, w)

    def scale(own_ref, r0, r1, divisor_ref, out_ref):
        for q in range(held):
            rows = rows_of(q)
            total = own_ref[rows, :] + r0[rows, :].astype(F32) + r1[rows, :].astype(F32)
            out_ref[rows, :] = (total / divisor_ref[q : q + 1, :]).astype(BF16)

    (scaled,) = run(scale, [(wide, BF16)], coarse_grad, *coarse_returned, divisor)
    scaled_parts = share(scaled)

    def first_back(s_ref, *refs):
        parts = refs[:sub_size]
        middle_ref, put, slope_ref, node_slope_ref, w_ref, fold_ref = refs[sub_size : sub_size + 6]
        r0, r1, d_node, d_recv, d_send, grad_ref, lift_scr, act_scr, acc_scr = refs[sub_size + 6 :]
        lift_into(parts, s_ref, lift_scr)
        for b in range(blocks):
            lifted = lift_scr[scalar(s_ref, at_pool + b)].astype(F32)
            grad_ref[rows_of(b), :] = middle_ref[b] + lifted
        d_out = mm_t(grad_ref[...].astype(BF16), w_ref[0, 5])
        fine_backward(d_out, s_ref, fold_ref[...], put, slope_ref, node_slope_ref, d_node, d_recv, act_scr, acc_scr)
        halo_grads_into((r0, r1), [acc_scr[blocks:].reshape(far_size, features)], 0, w_ref)
        d_send[...] = acc_scr[0:blocks].astype(BF16)

    *halo_grads, d_node, d_recv, d_send, grad_first = run(
        first_back,
        back_out + [(fine, F32)],
        table, *scaled_parts, grad_middle, put, slope0, node_slope0, w, fold0,
        scratch=[pltpu.VMEM((slots,) + tile, BF16)] + back_scratch,
    )
    returned = exchange(halo_grads)

    def first_own(first_ref, d_node, d_recv, d_send, w_ref, grad_ref):
        grad_ref[...] = own_back(first_ref[...], 0, w_ref, d_node[...], d_recv[...], d_send[...])

    (grad_own,) = run(first_own, [(fine, F32)], grad_first, d_node, d_recv, d_send.reshape(fine), w)

    def finish(s_ref, r0, r1, own_ref, out_ref):
        out_ref[...] = own_ref[...]
        for r, arrived in zip(ORDER, (r0, r1)):
            at = scalar(s_ref, r)
            out_ref[at] = out_ref[at] + arrived[...].astype(F32)

    (grad_nodes,) = run(finish, [(tiles, F32)], table, returned[0], returned[1], grad_own.reshape(tiles))
    return (out_nodes, grad_nodes.reshape(fine))


def solution(mesh):
    split = ("groups", "dom", "pair", "sub")
    placed = (
        P(split, None),
        P(split, None),
        P(split, None, None),
        P(split, None),
        P(split, None, None),
        P(split),
        P(split, None),
        P(split, None, None),
        P(),
        P(),
    )
    return jax.shard_map(
        per_device,
        mesh=mesh,
        in_specs=placed,
        out_specs=(P(split, None), P(split, None)),
        check_vma=False,
    )
```

```python
import jax
import jax.numpy as jnp
from jax import lax
from jax.experimental import pallas as pl
from jax.experimental.pallas import tpu as pltpu
from jax.sharding import PartitionSpec as P

F32 = jnp.float32
BF16 = jnp.bfloat16
I32 = jnp.int32
TAIL = 16
GROUP_AXES = ("pair", "sub")
ORDER = (1, 0)


def swapped(value, axis, mask):
    size = lax.axis_size(axis)
    return lax.ppermute(value, axis, [(source, source ^ mask) for source in range(size)])


def mm(a, b):
    return jnp.dot(a, b, preferred_element_type=F32)


def mm_t(a, b):
    return lax.dot_general(a, b, (((1,), (1,)), ((), ())), preferred_element_type=F32)


def scalar(table, index):
    return table[index : index + 1, :][0, 0]


def run(kernel, outs, *arrays, scratch=(), flops=0):
    return pl.pallas_call(
        kernel,
        out_shape=[jax.ShapeDtypeStruct(shape, dtype) for shape, dtype in outs],
        in_specs=[pl.BlockSpec(memory_space=pltpu.VMEM)] * len(arrays),
        out_specs=[pl.BlockSpec(memory_space=pltpu.VMEM)] * len(outs),
        scratch_shapes=list(scratch),
        compiler_params=pltpu.CompilerParams(vmem_limit_bytes=12 * 2**20),
        cost_estimate=pl.CostEstimate(flops=flops, bytes_accessed=2**20, transcendentals=0),
    )(*arrays)


def run_hbm(kernel, outs, far, *near, scratch=()):
    return pl.pallas_call(
        kernel,
        out_shape=[pltpu.VMEM(shape, dtype) for shape, dtype in outs],
        in_specs=[pl.BlockSpec(memory_space=pltpu.HBM)] * len(far) + [pl.BlockSpec(memory_space=pltpu.VMEM)] * len(near),
        out_specs=[pl.BlockSpec(memory_space=pltpu.VMEM)] * len(outs),
        scratch_shapes=list(scratch),
        compiler_params=pltpu.CompilerParams(vmem_limit_bytes=12 * 2**20),
        cost_estimate=pl.CostEstimate(flops=0, bytes_accessed=2**20, transcendentals=0),
    )(*[pltpu.with_memory_space_constraint(array, pltpu.HBM) for array in far], *near)


def per_device(
    nodes,
    cotangent,
    send_blocks,
    neighbour_blocks,
    neighbour_nodes,
    pool_map,
    coarse_blocks,
    coarse_nodes,
    weights,
    biases,
):
    size, features = neighbour_nodes.shape[2], nodes.shape[1]
    blocks, degree = neighbour_blocks.shape
    xor_bits = (1, lax.axis_size("dom") // 2)
    rounds = len(xor_bits)
    slots = lax.axis_size(GROUP_AXES)
    pair_size, sub_size = lax.axis_size("pair"), lax.axis_size("sub")
    edges = blocks * degree
    far_size = rounds * size
    everyone = blocks + rounds
    tile = (size, features)
    fine = (blocks * size, features)
    tiles = (blocks,) + tile

    held = pair_size
    wide = (held * size, features)
    doms = 1 + rounds
    listed_rows = degree + 1
    at_last = doms * listed_rows
    at_tail = held * size
    pool_rows = at_tail + TAIL
    halo_rows = at_tail + size

    at_near = rounds
    at_pool = at_near + edges
    at_pair = at_pool + blocks
    at_sub = at_pair + 1
    table_rows = -(-(at_sub + 1) // 8) * 8

    def exchange(pieces):
        return [swapped(piece, "dom", xor_bits[r]) for r, piece in zip(ORDER, pieces)]

    def reduced(pieces):
        arrived = [swapped(piece, "sub", mask) for mask, piece in enumerate(pieces) if mask > 0]
        (chip,) = run(add_parts, [(pieces[0].shape, BF16)], pieces[0], *arrived)
        return [chip] + [swapped(chip, "pair", mask) for mask in range(1, pair_size)]

    def add_parts(*refs):
        total = refs[0][...].astype(F32)
        for part in refs[1:-1]:
            total = total + part[...].astype(F32)
        refs[-1][...] = total.astype(BF16)

    def share(piece):
        return [piece] + [swapped(piece, "sub", mask) for mask in range(1, sub_size)]

    def rows_of(b):
        return pl.ds(b * size, size)

    def begun(pairs, sems):
        copies = [pltpu.make_async_copy(source, target, sems.at[i]) for i, (source, target) in enumerate(pairs)]
        for copy in copies:
            copy.start()
        return copies

    def fetch(pairs, sems):
        for copy in begun(pairs, sems):
            copy.wait()

    def choose(send_in, ends_in, listed_in, pool_in, nodes_in, h_ref, info_ref, out0, out1,
               send_scr, ends_scr, listed_scr, pool_scr, sems):
        parts = [(nodes_in.at[rows_of(b)], h_ref.at[rows_of(b)]) for b in range(blocks)]
        lists = [(send_in, send_scr), (ends_in, ends_scr), (listed_in, listed_scr), (pool_in, pool_scr)]
        copies = begun(lists + parts, sems)
        for copy in copies[: len(lists)]:
            copy.wait()
        lanes = lax.broadcasted_iota(I32, (1, features), 1)
        listed = jnp.zeros((1, features), I32)
        for e in range(degree):
            listed = jnp.where(lanes == e, jnp.broadcast_to(listed_scr[0:1, e : e + 1], (1, features)), listed)
        listed = [ends_scr[...].astype(F32), listed.astype(F32)]

        def tail_of(v, last):
            before = [jnp.zeros((v * listed_rows, features), F32)] if v else []
            left = TAIL - 1 - (v + 1) * listed_rows
            after = [jnp.zeros((left, features), F32)] if left else []
            return jnp.concatenate(before + listed + after + [last.astype(F32)], axis=0).astype(BF16)

        info_ref[...] = tail_of(0, jnp.zeros((1, features), I32))
        for r, out in zip(ORDER, (out0, out1)):
            chosen = send_scr[0:1, r : r + 1]
            slot = jnp.zeros((1, 1), I32)
            for b in range(blocks):
                slot = jnp.where(chosen == b, pool_scr[0:1, b : b + 1], slot)
            out[size:, :] = tail_of(1 + r, jnp.broadcast_to(slot, (1, features)))
        starts = [pl.multiple_of(send_scr[0:1, r : r + 1][0, 0] * size, size) for r in ORDER]
        for copy in copies[len(lists) :]:
            copy.wait()
        for at, out in zip(starts, (out0, out1)):
            out[0:size, :] = h_ref[pl.ds(at, size), :]

    sent = send_blocks.reshape(1, rounds)
    coarse_ends = coarse_nodes.reshape(degree, size)
    pools = pool_map.reshape(1, blocks)
    h0, info, *first_sends = run_hbm(
        choose,
        [(fine, BF16), ((TAIL, features), BF16)] + [((size + TAIL, features), BF16)] * rounds,
        [sent, coarse_ends, coarse_blocks, pools, nodes],
        scratch=[pltpu.VMEM(a.shape, I32) for a in (sent, coarse_ends, coarse_blocks, pools)]
        + [pltpu.SemaphoreType.DMA((4 + blocks,))],
    )
    halo = exchange(first_sends)

    def grids():
        return lax.broadcasted_iota(I32, (size, size), 0), lax.broadcasted_iota(I32, (size, size), 1)

    def own_into(state, layer, w_ref, b_ref, recv_ref, node_ref, sender_ref):
        recv_ref[...] = 0.5 * (mm(state, w_ref[layer, 0]) + b_ref[layer, 0:1, :])
        node_ref[...] = 0.5 * (mm(state, w_ref[layer, 3]) + b_ref[layer, 1:2, :])
        sender_ref[...] = (0.5 * mm(state, w_ref[layer, 1])).astype(BF16)

    def layer_forward(count, fold, pre_of, node, slope_ref, node_slope_ref, sum_scr):
        for b in range(count):
            total = None
            for e in range(degree):
                edge = b * degree + e
                half = pre_of(b, e)
                up = 1.0 + jnp.tanh(half)
                active = half * up
                if edge < slope_ref.shape[0]:
                    slope_ref[edge] = (up + active * (2.0 - up)).astype(BF16)
                total = active if total is None else total + active
            sum_scr[rows_of(b), :] = total.astype(BF16)
        half = node + mm(sum_scr[...], fold)
        up = 1.0 + jnp.tanh(half)
        hidden = half * up
        kept = node_slope_ref.shape[0]
        node_slope_ref[...] = (0.5 * (up + hidden * (2.0 - up))).astype(BF16)[0:kept, :]
        return hidden.astype(BF16)

    def senders_into(own, halos, layer, w_ref, send_scr):
        for r, g in zip(ORDER, halos):
            send_scr[blocks + r] = (0.5 * mm(g, w_ref[layer, 1])).astype(BF16)
        for b in range(blocks):
            send_scr[b] = own[rows_of(b), :]

    def fine_pre(s_ref, recv, pick, send_scr):
        def pre_of(b, e):
            edge = b * degree + e
            return recv[rows_of(b), :] + mm(pick[edge], send_scr[scalar(s_ref, at_near + edge)])

        return pre_of

    def node_backward(d_out, fold, node_slope_ref, d_node, act_scr):
        d_hidden = (d_out * node_slope_ref[...].astype(F32)).astype(BF16)
        d_node[...] = d_hidden
        act_scr[...] = mm_t(d_hidden, fold)

    def fine_backward(d_out, s_ref, fold, put_ref, slope_ref, node_slope_ref, d_node, d_recv, act_scr, acc_scr):
        node_backward(d_out, fold, node_slope_ref, d_node, act_scr)
        acc_scr[...] = jnp.zeros_like(acc_scr)
        for b in range(blocks):
            d_active = act_scr[rows_of(b), :]
            total = None
            for e in range(degree):
                edge = b * degree + e
                d_pre = d_active * slope_ref[edge].astype(F32)
                total = d_pre if total is None else total + d_pre
                near = scalar(s_ref, at_near + edge)
                acc_scr[near] = acc_scr[near] + mm(put_ref[edge], d_pre.astype(BF16))
            d_recv[rows_of(b), :] = total.astype(BF16)

    def halo_grads_into(outs, grads, layer, w_ref):
        for r, out in zip(ORDER, outs):
            own = jnp.concatenate([g[r * size : (r + 1) * size, :] for g in grads], axis=0)
            out[...] = mm_t(own.astype(BF16), w_ref[layer, 1]).astype(BF16)

    def own_back(grad, layer, w_ref, d_node, d_recv, d_send):
        return (
            grad
            + mm_t(d_recv, w_ref[layer, 0])
            + mm_t(d_node, w_ref[layer, 3])
            + mm_t(d_send.astype(BF16), w_ref[layer, 1])
        )

    def pooled_into(read, s_ref, out_refs, tail=None):
        sub = scalar(s_ref, at_sub)
        lanes = lax.broadcasted_iota(I32, (1, features), 1)
        for sub_mask, out in enumerate(out_refs):
            counts = jnp.zeros((1, features), F32)
            for q in range(held):
                slot = q * sub_size + (sub ^ sub_mask)
                total, count = None, None
                for b in range(blocks):
                    hit = (scalar(s_ref, at_pool + b) == slot).astype(F32)
                    part = read(b) * hit
                    total = part if total is None else total + part
                    count = hit if count is None else count + hit
                out[rows_of(q), :] = total.astype(BF16)
                counts = counts + jnp.where(lanes == q, count, 0.0)
            if tail is not None:
                last = lax.broadcasted_iota(I32, (TAIL, features), 0) == at_last
                kept = tail if sub_mask == 0 else jnp.zeros_like(tail)
                out[at_tail:, :] = jnp.where(last, jnp.broadcast_to(counts, tail.shape), kept).astype(BF16)

    def lift_into(parts, s_ref, lift_scr):
        sub = scalar(s_ref, at_sub)
        for mask, part in enumerate(parts):
            for q in range(held):
                for v in range(part.shape[0] // (held * size)):
                    lift_scr[v * slots + q * sub_size + (sub ^ mask)] = part[rows_of(v * held + q), :]

    inputs = [
        sent,
        neighbour_blocks,
        pools,
        neighbour_nodes.reshape(edges, size),
        weights,
        biases,
        cotangent,
    ]
    own_out = [(fine, F32), (fine, F32), (fine, BF16)]

    def prepare(*refs):
        sources, h_ref = refs[: len(inputs)], refs[len(inputs)]
        ends, w_ref, b_ref, c_ref, s_ref, fold_ref, pick, recv, node, sender, *kept, sems = refs[len(inputs) + 1 :]
        send_scr, near_scr, pool_scr = kept
        fetch(list(zip(sources, kept + [ends, w_ref, b_ref, c_ref])), sems)

        def put_row(index, ref, i, j):
            s_ref[index : index + 1, :] = jnp.broadcast_to(ref[i : i + 1, j : j + 1], (1, features))

        for r in range(rounds):
            put_row(r, send_scr, 0, r)
        for b in range(blocks):
            for e in range(degree):
                put_row(at_near + b * degree + e, near_scr, b, e)
            put_row(at_pool + b, pool_scr, 0, b)
        s_ref[at_pair : at_pair + 1, :] = jnp.full((1, features), lax.axis_index("pair"), I32)
        s_ref[at_sub : at_sub + 1, :] = jnp.full((1, features), lax.axis_index("sub"), I32)
        own_into(h_ref[...], 0, w_ref, b_ref, recv, node, sender)
        columns = grids()[1]
        upright = jnp.transpose(ends[...])
        for edge in range(edges):
            pick[edge] = (columns == upright[:, edge : edge + 1]).astype(BF16)
        fold_ref[...] = (mm(w_ref[0, 2], w_ref[0, 4]) * (0.5 / degree)).astype(BF16)

    ends, w, bias, cot, table, fold0, pick, recv0, node0, sender0 = run_hbm(
        prepare,
        [
            ((edges, size), I32), (weights.shape, BF16), (biases.shape, F32), (fine, BF16),
            ((table_rows, features), I32), (tile, BF16),
            ((edges, size, size), BF16),
        ] + own_out,
        inputs,
        h0,
        scratch=[pltpu.VMEM(a.shape, I32) for a in inputs[:3]]
        + [pltpu.SemaphoreType.DMA((len(inputs),))],
    )

    slopes = [((edges,) + tile, BF16), (fine, BF16)]

    layer_scratch = [pltpu.VMEM((everyone,) + tile, BF16), pltpu.VMEM(fine, BF16)]

    def first_layer(s_ref, g0, g1, h_ref, recv, node, sender, pick, w_ref, fold_ref, info_ref, *rest):
        first_ref, slope_ref, node_slope_ref, slots_ref, *sends, send_scr, sum_scr = rest
        senders_into(sender, (g0[0:size, :], g1[0:size, :]), 0, w_ref, send_scr)
        pre_of = fine_pre(s_ref, recv, pick, send_scr)
        hidden = layer_forward(blocks, fold_ref[...], pre_of, node[...], slope_ref, node_slope_ref, sum_scr)
        first_ref[...] = (h_ref[...].astype(F32) + mm(hidden, w_ref[0, 5])).astype(BF16)
        tail = info_ref[...].astype(F32) + g0[size:, :].astype(F32) + g1[size:, :].astype(F32)
        pooled_into(lambda b: first_ref[rows_of(b), :].astype(F32), s_ref, sends, tail)
        for r, g in zip(ORDER, (g0, g1)):
            last = g[size:, :].astype(F32).astype(I32)[at_last : at_last + 1, :]
            slots_ref[r : r + 1, :] = last

    first, slope0, node_slope0, halo_slots, *pool_sends = run(
        first_layer,
        [(fine, BF16)] + slopes + [((8, features), I32)] + [((pool_rows, features), BF16)] * sub_size,
        table, halo[0], halo[1], h0, recv0, node0, sender0, pick, w, fold0, info,
        scratch=layer_scratch,
    )

    pool_in = reduced(pool_sends)

    def coarse_begin(s_ref, first_ref, *refs):
        parts, (start_ref, divisor_ref, infos_ref, other, out0, out1) = refs[:pair_size], refs[pair_size:]
        total = parts[0][0:at_tail, :].astype(F32)
        tails = [part[at_tail:, :].astype(F32) for part in parts]
        counts = tails[0][at_last : at_last + 1, :]
        for part, tail in zip(parts[1:], tails[1:]):
            total = total + part[0:at_tail, :].astype(F32)
            counts = counts + tail[at_last : at_last + 1, :]
        for q in range(held):
            divisor_ref[q : q + 1, :] = jnp.broadcast_to(jnp.maximum(counts[:, q : q + 1], 1.0), (1, features))
        for q in range(held):
            start = (total[q * size : (q + 1) * size, :] / divisor_ref[q : q + 1, :]).astype(BF16)
            for out in (start_ref, other, out0, out1):
                out[rows_of(q), :] = start
        for r, out in zip(ORDER, (out0, out1)):
            at = pl.multiple_of(scalar(s_ref, r) * size, size)
            out[at_tail:, :] = first_ref[pl.ds(at, size), :]
        pair = scalar(s_ref, at_pair)
        for mask, tail in enumerate(tails):
            infos_ref[pair ^ mask] = tail

    coarse_start, divisor, infos, other_send, *halo_sends = run(
        coarse_begin,
        [(wide, BF16), ((8, features), F32), ((held, TAIL, features), F32), (wide, BF16)]
        + [((halo_rows, features), BF16)] * rounds,
        table, first, *pool_in,
    )
    other = swapped(other_send, "dom", xor_bits[0] ^ xor_bits[1])
    coarse_halo = exchange(halo_sends)

    def coarse_prepare(h_ref, w_ref, b_ref, cot_ref, infos_ref, ends, pre, node, fold_ref, join_ref, bias_ref,
                       far_pick, cput, put, d_out, recv, sender):
        own_into(h_ref[...], 1, w_ref, b_ref, recv, node, sender)
        for i, layer in enumerate((1, 2)):
            fold_ref[i] = (mm(w_ref[layer, 2], w_ref[layer, 4]) * (0.5 / degree)).astype(BF16)
            for j, part in enumerate((0, 3)):
                columns_j = slice(j * features, (j + 1) * features)
                join_ref[i, :, columns_j] = w_ref[layer, part] * 0.5
                bias_ref[i : i + 1, columns_j] = b_ref[layer, j : j + 1, :] * 0.5
        d_out[...] = mm_t(cot_ref[...], w_ref[2, 5])
        rows, columns = grids()
        for v in range(doms):
            for q in range(held):
                tile_at = v * held + q
                around = infos_ref[q].astype(I32)
                upright = jnp.transpose(infos_ref[q]).astype(I32)
                listed = (v + 1) * listed_rows - 1
                own = sender[rows_of(q), :]
                for e in range(degree):
                    edge = tile_at * degree + e
                    near = jnp.broadcast_to(around[listed : listed + 1, e : e + 1], (1, size))
                    at = v * listed_rows + e
                    hit = columns == upright[:, at : at + 1]
                    picked = mm((hit & (near == v)).astype(BF16), own)
                    pre[edge] = picked + recv[rows_of(q), :] if v == 0 else picked
                    for i, source in enumerate([n for n in range(doms) if n != v]):
                        far_pick[rows_of(edge), i * size : (i + 1) * size] = (hit & (near == source)).astype(BF16)
                    if v == 0:
                        to = rows == around[e : e + 1, :]
                        for r in range(doms):
                            cput[q, r * size : (r + 1) * size, e * size : (e + 1) * size] = (to & (near == r)).astype(BF16)
        for edge in range(edges):
            put[edge] = (rows == ends[edge : edge + 1, :]).astype(BF16)

    coarse_edges = doms * held * degree
    pre1, node1, fold, joined, joined_bias, coarse_far, coarse_put, put, d_out2 = run(
        coarse_prepare,
        [
            ((coarse_edges,) + tile, F32), (wide, F32), ((2,) + tile, BF16),
            ((2, features, 2 * features), BF16), ((8, 2 * features), F32),
            ((coarse_edges * size, far_size), BF16), ((held, size + far_size, degree * size), BF16),
            ((edges, size, size), BF16), (fine, F32),
        ],
        coarse_start, w, bias, cot, infos, ends,
        scratch=[pltpu.VMEM(wide, F32), pltpu.VMEM(wide, BF16)],
    )

    def coarse_layer(other_ref, g0, g1, h_ref, pre, node, far_pick, w_ref, join_ref, bias_ref, fold_ref, end_ref, slope_ref, node_slope_ref, sum_scr):
        halos = [g[0:at_tail, :] for _, g in sorted(zip(ORDER, (g0, g1)))]
        states = [h_ref[...]] + halos
        arrived = (0.5 * mm(jnp.concatenate(halos + [other_ref[...]], axis=0), w_ref[1, 1])).astype(BF16)
        rows_all = held * size
        third = arrived[rounds * rows_all :, :]
        arrived = [arrived[r * rows_all : (r + 1) * rows_all, :] for r in range(rounds)]
        own = mm(jnp.concatenate(halos, axis=0), join_ref[0]) + bias_ref[0:1, :]
        recvs = [None] + [own[r * rows_all : (r + 1) * rows_all, 0:features] for r in range(rounds)]
        nodes_all = [node[...], own[:, features:]]
        sources = [arrived, [arrived[0], third], [arrived[1], third]]
        width = degree * size
        picked = []
        for v in range(doms):
            for q in range(held):
                at = (v * held + q) * width
                senders = jnp.concatenate([a[q * size : (q + 1) * size, :] for a in sources[v]], axis=0)
                picked.append(mm(far_pick[at : at + width, :], senders))

        def pre_of(b, e):
            v, q = divmod(b, held)
            value = pre[b * degree + e] + picked[b][e * size : (e + 1) * size, :]
            return value if v == 0 else value + recvs[v][q * size : (q + 1) * size, :]

        hidden = layer_forward(
            doms * held, fold_ref[0], pre_of, jnp.concatenate(nodes_all, axis=0), slope_ref, node_slope_ref, sum_scr
        )
        state = jnp.concatenate(states, axis=0).astype(F32)
        end_ref[...] = (state + mm(hidden, w_ref[1, 5])).astype(BF16)
    coarse_end, slope1, node_slope1 = run(
        coarse_layer,
        [((doms * held * size, features), BF16), ((held * degree,) + tile, BF16), (wide, BF16)],
        other, coarse_halo[0], coarse_halo[1], coarse_start, pre1, node1, coarse_far, w, joined, joined_bias, fold,
        scratch=[pltpu.VMEM((doms * held * size, features), BF16)],
    )
    coarse_ends = share(coarse_end)

    back_out = [(tile, BF16)] * rounds + [(fine, BF16), (fine, BF16), (tiles, BF16)]
    back_scratch = [pltpu.VMEM(fine, F32), pltpu.VMEM((everyone,) + tile, F32)]

    def last_layer(s_ref, slots_ref, g0, g1, *refs):
        parts = refs[:sub_size]
        first_ref, pick, put, w_ref, join_ref, bias_ref, fold_ref, d_out = refs[sub_size : sub_size + 8]
        (r0, r1, d_node, d_recv, d_send, hidden_ref, middle_ref,
         lift_scr, own_scr, state_scr, send_scr, sum_scr, slope_scr, node_slope_scr, act_scr, acc_scr) = refs[sub_size + 8 :]
        lift_into(parts, s_ref, lift_scr)
        for b in range(blocks):
            lifted = lift_scr[scalar(s_ref, at_pool + b)].astype(F32)
            state_scr[rows_of(b), :] = (first_ref[rows_of(b), :].astype(F32) + lifted).astype(BF16)
        for r, g in zip(ORDER, (g0, g1)):
            lifted = lift_scr[(1 + r) * slots + scalar(slots_ref, r)].astype(F32)
            state_scr[rows_of(blocks + r), :] = (g[at_tail:, :].astype(F32) + lifted).astype(BF16)
        senders = (0.5 * mm(state_scr[...], w_ref[2, 1])).astype(BF16)
        send_scr[...] = senders.reshape((everyone,) + tile)
        middle = state_scr[0 : blocks * size, :]
        middle_ref[...] = middle
        own_scr[...] = mm(middle, join_ref[1]) + bias_ref[1:2, :]
        recv, node = own_scr.at[:, 0:features], own_scr.at[:, features:]
        fold = fold_ref[1]
        pre_of = fine_pre(s_ref, recv, pick, send_scr)
        hidden_ref[...] = layer_forward(blocks, fold, pre_of, node[...], slope_scr, node_slope_scr, sum_scr)
        fine_backward(d_out[...], s_ref, fold, put, slope_scr, node_slope_scr, d_node, d_recv, act_scr, acc_scr)
        halo_grads_into((r0, r1), [acc_scr[blocks:].reshape(far_size, features)], 2, w_ref)
        d_send[...] = acc_scr[0:blocks].astype(BF16)

    *halo_grads, d_node, d_recv, d_send, hidden2, middle = run(
        last_layer,
        back_out + [(fine, BF16), (fine, BF16)],
        table, halo_slots, *coarse_halo, *coarse_ends, first, pick, put, w, joined, joined_bias, fold, d_out2,
        scratch=[pltpu.VMEM((doms * slots,) + tile, BF16)]
        + [pltpu.VMEM((blocks * size, 2 * features), F32), pltpu.VMEM((everyone * size, features), BF16)]
        + layer_scratch + [pltpu.VMEM((edges,) + tile, BF16), pltpu.VMEM(fine, BF16)] + back_scratch,
    )
    returned = exchange(halo_grads)

    def last_own(cot_ref, d_node, d_recv, d_send, h_ref, hidden_ref, w_ref, grad_ref, out_ref):
        grad_ref[...] = own_back(cot_ref[...].astype(F32), 2, w_ref, d_node[...], d_recv[...], d_send[...])
        out_ref[...] = (h_ref[...].astype(F32) + mm(hidden_ref[...], w_ref[2, 5])).astype(BF16)

    grad_own, out_nodes = run(
        last_own, [(fine, F32), (fine, BF16)], cot, d_node, d_recv, d_send.reshape(fine), middle, hidden2, w
    )

    def pool_grads(s_ref, r0, r1, own_ref, grad_ref, *sends):
        grad_ref[...] = own_ref[...]
        for r, arrived in zip(ORDER, (r0, r1)):
            at = scalar(s_ref, r)
            grad_ref[at] = grad_ref[at] + arrived[...].astype(F32)
        pooled_into(lambda b: grad_ref[b], s_ref, sends)

    grad_middle, *grad_sends = run(
        pool_grads,
        [(tiles, F32)] + [(wide, BF16)] * sub_size,
        table, returned[0], returned[1], grad_own.reshape(tiles),
    )
    grads_in = reduced(grad_sends)

    def coarse_back(*refs):
        parts = refs[:pair_size]
        put, slope_ref, node_slope_ref, w_ref, fold_ref, r0, r1, grad_ref, d_node, d_pre, act_scr = refs[pair_size:]
        grad = parts[0][...].astype(F32)
        for part in parts[1:]:
            grad = grad + part[...].astype(F32)
        grad_ref[...] = grad
        d_out = mm_t(grad.astype(BF16), w_ref[1, 5])
        node_backward(d_out, fold_ref[0], node_slope_ref, d_node, act_scr)
        for q in range(held):
            for e in range(degree):
                edge = q * degree + e
                d_pre[rows_of(edge), :] = (act_scr[rows_of(q), :] * slope_ref[edge].astype(F32)).astype(BF16)
        width = degree * size
        grads = [mm(put[q, size:, :], d_pre[q * width : (q + 1) * width, :]) for q in range(held)]
        halo_grads_into((r0, r1), grads, 1, w_ref)

    *coarse_sends, coarse_grad, d_node, d_pre = run(
        coarse_back,
        [(wide, BF16)] * rounds + [(wide, F32), (wide, BF16), ((held * degree * size, features), BF16)],
        *grads_in, coarse_put, slope1, node_slope1, w, fold,
        scratch=[pltpu.VMEM(wide, F32)],
    )
    coarse_returned = exchange(coarse_sends)

    def coarse_own(grad_ref, put, d_node, d_pre, w_ref, own_ref):
        width = degree * size
        d_send = [mm(put[q, 0:size, :], d_pre[q * width : (q + 1) * width, :]) for q in range(held)]
        d_recv = []
        for q in range(held):
            total = None
            for e in range(degree):
                part = d_pre[rows_of(q * degree + e), :].astype(F32)
                total = part if total is None else total + part
            d_recv.append(total.astype(BF16))
        own_ref[...] = own_back(
            grad_ref[...], 1, w_ref, d_node[...], jnp.concatenate(d_recv, axis=0), jnp.concatenate(d_send, axis=0)
        )

    (coarse_grad,) = run(coarse_own, [(wide, F32)], coarse_grad, coarse_put, d_node, d_pre, w)

    def scale(own_ref, r0, r1, divisor_ref, out_ref):
        for q in range(held):
            rows = rows_of(q)
            total = own_ref[rows, :] + r0[rows, :].astype(F32) + r1[rows, :].astype(F32)
            out_ref[rows, :] = (total / divisor_ref[q : q + 1, :]).astype(BF16)

    (scaled,) = run(scale, [(wide, BF16)], coarse_grad, *coarse_returned, divisor)
    scaled_parts = share(scaled)

    def first_back(s_ref, *refs):
        parts = refs[:sub_size]
        middle_ref, put, slope_ref, node_slope_ref, w_ref, fold_ref = refs[sub_size : sub_size + 6]
        r0, r1, d_node, d_recv, d_send, grad_ref, lift_scr, act_scr, acc_scr = refs[sub_size + 6 :]
        lift_into(parts, s_ref, lift_scr)
        for b in range(blocks):
            lifted = lift_scr[scalar(s_ref, at_pool + b)].astype(F32)
            grad_ref[rows_of(b), :] = middle_ref[b] + lifted
        d_out = mm_t(grad_ref[...].astype(BF16), w_ref[0, 5])
        fine_backward(d_out, s_ref, fold_ref[...], put, slope_ref, node_slope_ref, d_node, d_recv, act_scr, acc_scr)
        halo_grads_into((r0, r1), [acc_scr[blocks:].reshape(far_size, features)], 0, w_ref)
        d_send[...] = acc_scr[0:blocks].astype(BF16)

    *halo_grads, d_node, d_recv, d_send, grad_first = run(
        first_back,
        back_out + [(fine, F32)],
        table, *scaled_parts, grad_middle, put, slope0, node_slope0, w, fold0,
        scratch=[pltpu.VMEM((slots,) + tile, BF16)] + back_scratch,
    )
    returned = exchange(halo_grads)

    def first_own(first_ref, d_node, d_recv, d_send, w_ref, grad_ref):
        grad_ref[...] = own_back(first_ref[...], 0, w_ref, d_node[...], d_recv[...], d_send[...])

    (grad_own,) = run(first_own, [(fine, F32)], grad_first, d_node, d_recv, d_send.reshape(fine), w)

    def finish(s_ref, r0, r1, own_ref, out_ref):
        out_ref[...] = own_ref[...]
        for r, arrived in zip(ORDER, (r0, r1)):
            at = scalar(s_ref, r)
            out_ref[at] = out_ref[at] + arrived[...].astype(F32)

    (grad_nodes,) = run(finish, [(tiles, F32)], table, returned[0], returned[1], grad_own.reshape(tiles))
    return (out_nodes, grad_nodes.reshape(fine))


def solution(mesh):
    split = ("groups", "dom", "pair", "sub")
    placed = (
        P(split, None),
        P(split, None),
        P(split, None, None),
        P(split, None),
        P(split, None, None),
        P(split),
        P(split, None),
        P(split, None, None),
        P(),
        P(),
    )
    return jax.shard_map(
        per_device,
        mesh=mesh,
        in_specs=placed,
        out_specs=(P(split, None), P(split, None)),
        check_vma=False,
    )
```

```python
import jax
import jax.numpy as jnp
from jax import lax
from jax.experimental import pallas as pl
from jax.experimental.pallas import tpu as pltpu
from jax.sharding import PartitionSpec as P

F32 = jnp.float32
BF16 = jnp.bfloat16
I32 = jnp.int32
TAIL = 16
GROUP_AXES = ("pair", "sub")
ORDER = (1, 0)


def swapped(value, axis, mask):
    size = lax.axis_size(axis)
    return lax.ppermute(value, axis, [(source, source ^ mask) for source in range(size)])


def mm(a, b):
    return jnp.dot(a, b, preferred_element_type=F32)


def mm_t(a, b):
    return lax.dot_general(a, b, (((1,), (1,)), ((), ())), preferred_element_type=F32)


def scalar(table, index):
    return table[index : index + 1, :][0, 0]


def run(kernel, outs, *arrays, scratch=(), flops=0):
    return pl.pallas_call(
        kernel,
        out_shape=[jax.ShapeDtypeStruct(shape, dtype) for shape, dtype in outs],
        in_specs=[pl.BlockSpec(memory_space=pltpu.VMEM)] * len(arrays),
        out_specs=[pl.BlockSpec(memory_space=pltpu.VMEM)] * len(outs),
        scratch_shapes=list(scratch),
        compiler_params=pltpu.CompilerParams(vmem_limit_bytes=12 * 2**20),
        cost_estimate=pl.CostEstimate(flops=flops, bytes_accessed=2**20, transcendentals=0),
    )(*arrays)


def run_hbm(kernel, outs, far, *near, scratch=()):
    return pl.pallas_call(
        kernel,
        out_shape=[pltpu.VMEM(shape, dtype) for shape, dtype in outs],
        in_specs=[pl.BlockSpec(memory_space=pltpu.HBM)] * len(far) + [pl.BlockSpec(memory_space=pltpu.VMEM)] * len(near),
        out_specs=[pl.BlockSpec(memory_space=pltpu.VMEM)] * len(outs),
        scratch_shapes=list(scratch),
        compiler_params=pltpu.CompilerParams(vmem_limit_bytes=12 * 2**20),
        cost_estimate=pl.CostEstimate(flops=0, bytes_accessed=2**20, transcendentals=0),
    )(*[pltpu.with_memory_space_constraint(array, pltpu.HBM) for array in far], *near)


def per_device(
    nodes,
    cotangent,
    send_blocks,
    neighbour_blocks,
    neighbour_nodes,
    pool_map,
    coarse_blocks,
    coarse_nodes,
    weights,
    biases,
):
    size, features = neighbour_nodes.shape[2], nodes.shape[1]
    blocks, degree = neighbour_blocks.shape
    xor_bits = (1, lax.axis_size("dom") // 2)
    rounds = len(xor_bits)
    slots = lax.axis_size(GROUP_AXES)
    pair_size, sub_size = lax.axis_size("pair"), lax.axis_size("sub")
    edges = blocks * degree
    far_size = rounds * size
    everyone = blocks + rounds
    tile = (size, features)
    fine = (blocks * size, features)
    tiles = (blocks,) + tile

    held = pair_size
    wide = (held * size, features)
    doms = 1 + rounds
    listed_rows = degree + 1
    at_last = doms * listed_rows
    at_tail = held * size
    pool_rows = at_tail + TAIL
    halo_rows = at_tail + size

    at_near = rounds
    at_pool = at_near + edges
    at_pair = at_pool + blocks
    at_sub = at_pair + 1
    table_rows = -(-(at_sub + 1) // 8) * 8

    def exchange(pieces):
        return [swapped(piece, "dom", xor_bits[r]) for r, piece in zip(ORDER, pieces)]

    def reduced(pieces):
        arrived = [swapped(piece, "sub", mask) for mask, piece in enumerate(pieces) if mask > 0]
        (chip,) = run(add_parts, [(pieces[0].shape, BF16)], pieces[0], *arrived)
        return [chip] + [swapped(chip, "pair", mask) for mask in range(1, pair_size)]

    def add_parts(*refs):
        total = refs[0][...].astype(F32)
        for part in refs[1:-1]:
            total = total + part[...].astype(F32)
        refs[-1][...] = total.astype(BF16)

    def share(piece):
        return [piece] + [swapped(piece, "sub", mask) for mask in range(1, sub_size)]

    def rows_of(b):
        return pl.ds(b * size, size)

    def begun(pairs, sems):
        copies = [pltpu.make_async_copy(source, target, sems.at[i]) for i, (source, target) in enumerate(pairs)]
        for copy in copies:
            copy.start()
        return copies

    def fetch(pairs, sems):
        for copy in begun(pairs, sems):
            copy.wait()

    def choose(send_in, ends_in, listed_in, pool_in, nodes_in, h_ref, info_ref, out0, out1,
               send_scr, ends_scr, listed_scr, pool_scr, sems):
        parts = [(nodes_in.at[rows_of(b)], h_ref.at[rows_of(b)]) for b in range(blocks)]
        lists = [(send_in, send_scr), (ends_in, ends_scr), (listed_in, listed_scr), (pool_in, pool_scr)]
        copies = begun(lists + parts, sems)
        for copy in copies[: len(lists)]:
            copy.wait()
        lanes = lax.broadcasted_iota(I32, (1, features), 1)
        listed = jnp.zeros((1, features), I32)
        for e in range(degree):
            listed = jnp.where(lanes == e, jnp.broadcast_to(listed_scr[0:1, e : e + 1], (1, features)), listed)
        listed = [ends_scr[...].astype(F32), listed.astype(F32)]

        def tail_of(v, last):
            before = [jnp.zeros((v * listed_rows, features), F32)] if v else []
            left = TAIL - 1 - (v + 1) * listed_rows
            after = [jnp.zeros((left, features), F32)] if left else []
            return jnp.concatenate(before + listed + after + [last.astype(F32)], axis=0).astype(BF16)

        info_ref[...] = tail_of(0, jnp.zeros((1, features), I32))
        for r, out in zip(ORDER, (out0, out1)):
            chosen = send_scr[0:1, r : r + 1]
            slot = jnp.zeros((1, 1), I32)
            for b in range(blocks):
                slot = jnp.where(chosen == b, pool_scr[0:1, b : b + 1], slot)
            out[size:, :] = tail_of(1 + r, jnp.broadcast_to(slot, (1, features)))
        starts = [pl.multiple_of(send_scr[0:1, r : r + 1][0, 0] * size, size) for r in ORDER]
        for copy in copies[len(lists) :]:
            copy.wait()
        for at, out in zip(starts, (out0, out1)):
            out[0:size, :] = h_ref[pl.ds(at, size), :]

    sent = send_blocks.reshape(1, rounds)
    coarse_ends = coarse_nodes.reshape(degree, size)
    pools = pool_map.reshape(1, blocks)
    h0, info, *first_sends = run_hbm(
        choose,
        [(fine, BF16), ((TAIL, features), BF16)] + [((size + TAIL, features), BF16)] * rounds,
        [sent, coarse_ends, coarse_blocks, pools, nodes],
        scratch=[pltpu.VMEM(a.shape, I32) for a in (sent, coarse_ends, coarse_blocks, pools)]
        + [pltpu.SemaphoreType.DMA((4 + blocks,))],
    )
    halo = exchange(first_sends)

    def grids():
        return lax.broadcasted_iota(I32, (size, size), 0), lax.broadcasted_iota(I32, (size, size), 1)

    def own_into(state, layer, w_ref, b_ref, recv_ref, node_ref, sender_ref):
        recv_ref[...] = 0.5 * (mm(state, w_ref[layer, 0]) + b_ref[layer, 0:1, :])
        node_ref[...] = 0.5 * (mm(state, w_ref[layer, 3]) + b_ref[layer, 1:2, :])
        sender_ref[...] = (0.5 * mm(state, w_ref[layer, 1])).astype(BF16)

    def layer_forward(count, fold, pre_of, node, slope_ref, node_slope_ref, sum_scr):
        for b in range(count):
            total = None
            for e in range(degree):
                edge = b * degree + e
                half = pre_of(b, e)
                up = 1.0 + jnp.tanh(half)
                active = half * up
                if slope_ref is not None:
                    slope_ref[edge] = (up + active * (2.0 - up)).astype(BF16)
                total = active if total is None else total + active
            sum_scr[rows_of(b), :] = total.astype(BF16)
        half = node + mm(sum_scr[...], fold)
        up = 1.0 + jnp.tanh(half)
        hidden = half * up
        if slope_ref is not None:
            node_slope_ref[...] = (0.5 * (up + hidden * (2.0 - up))).astype(BF16)
        return hidden.astype(BF16)

    def senders_into(own, halos, layer, w_ref, send_scr):
        for r, g in zip(ORDER, halos):
            send_scr[blocks + r] = (0.5 * mm(g, w_ref[layer, 1])).astype(BF16)
        for b in range(blocks):
            send_scr[b] = own[rows_of(b), :]

    def fine_pre(s_ref, recv, pick, send_scr):
        def pre_of(b, e):
            edge = b * degree + e
            return recv[rows_of(b), :] + mm(pick[edge], send_scr[scalar(s_ref, at_near + edge)])

        return pre_of

    def node_backward(d_out, fold, node_slope_ref, d_node, act_scr):
        d_hidden = (d_out * node_slope_ref[...].astype(F32)).astype(BF16)
        d_node[...] = d_hidden
        act_scr[...] = mm_t(d_hidden, fold)

    def fine_backward(d_out, s_ref, fold, put_ref, slope_ref, node_slope_ref, d_node, d_recv, act_scr, acc_scr):
        node_backward(d_out, fold, node_slope_ref, d_node, act_scr)
        acc_scr[...] = jnp.zeros_like(acc_scr)
        for b in range(blocks):
            d_active = act_scr[rows_of(b), :]
            total = None
            for e in range(degree):
                edge = b * degree + e
                d_pre = d_active * slope_ref[edge].astype(F32)
                total = d_pre if total is None else total + d_pre
                near = scalar(s_ref, at_near + edge)
                acc_scr[near] = acc_scr[near] + mm(put_ref[edge], d_pre.astype(BF16))
            d_recv[rows_of(b), :] = total.astype(BF16)

    def halo_grads_into(outs, grads, layer, w_ref):
        for r, out in zip(ORDER, outs):
            own = jnp.concatenate([g[r * size : (r + 1) * size, :] for g in grads], axis=0)
            out[...] = mm_t(own.astype(BF16), w_ref[layer, 1]).astype(BF16)

    def own_back(grad, layer, w_ref, d_node, d_recv, d_send):
        return (
            grad
            + mm_t(d_recv, w_ref[layer, 0])
            + mm_t(d_node, w_ref[layer, 3])
            + mm_t(d_send.astype(BF16), w_ref[layer, 1])
        )

    def pooled_into(read, s_ref, out_refs, tail=None):
        sub = scalar(s_ref, at_sub)
        lanes = lax.broadcasted_iota(I32, (1, features), 1)
        for sub_mask, out in enumerate(out_refs):
            counts = jnp.zeros((1, features), F32)
            for q in range(held):
                slot = q * sub_size + (sub ^ sub_mask)
                total, count = None, None
                for b in range(blocks):
                    hit = (scalar(s_ref, at_pool + b) == slot).astype(F32)
                    part = read(b) * hit
                    total = part if total is None else total + part
                    count = hit if count is None else count + hit
                out[rows_of(q), :] = total.astype(BF16)
                counts = counts + jnp.where(lanes == q, count, 0.0)
            if tail is not None:
                last = lax.broadcasted_iota(I32, (TAIL, features), 0) == at_last
                kept = tail if sub_mask == 0 else jnp.zeros_like(tail)
                out[at_tail:, :] = jnp.where(last, jnp.broadcast_to(counts, tail.shape), kept).astype(BF16)

    def lift_into(parts, s_ref, lift_scr):
        sub = scalar(s_ref, at_sub)
        for mask, part in enumerate(parts):
            for q in range(held):
                for v in range(part.shape[0] // (held * size)):
                    lift_scr[v * slots + q * sub_size + (sub ^ mask)] = part[rows_of(v * held + q), :]

    inputs = [
        sent,
        neighbour_blocks,
        pools,
        neighbour_nodes.reshape(edges, size),
        weights,
        biases,
        cotangent,
    ]
    own_out = [(fine, F32), (fine, F32), (fine, BF16)]

    def prepare(*refs):
        sources, h_ref = refs[: len(inputs)], refs[len(inputs)]
        ends, w_ref, b_ref, c_ref, s_ref, fold_ref, pick, recv, node, sender, *kept, sems = refs[len(inputs) + 1 :]
        send_scr, near_scr, pool_scr = kept
        fetch(list(zip(sources, kept + [ends, w_ref, b_ref, c_ref])), sems)

        def put_row(index, ref, i, j):
            s_ref[index : index + 1, :] = jnp.broadcast_to(ref[i : i + 1, j : j + 1], (1, features))

        for r in range(rounds):
            put_row(r, send_scr, 0, r)
        for b in range(blocks):
            for e in range(degree):
                put_row(at_near + b * degree + e, near_scr, b, e)
            put_row(at_pool + b, pool_scr, 0, b)
        s_ref[at_pair : at_pair + 1, :] = jnp.full((1, features), lax.axis_index("pair"), I32)
        s_ref[at_sub : at_sub + 1, :] = jnp.full((1, features), lax.axis_index("sub"), I32)
        own_into(h_ref[...], 0, w_ref, b_ref, recv, node, sender)
        columns = grids()[1]
        upright = jnp.transpose(ends[...])
        for edge in range(edges):
            pick[edge] = (columns == upright[:, edge : edge + 1]).astype(BF16)
        fold_ref[...] = (mm(w_ref[0, 2], w_ref[0, 4]) * (0.5 / degree)).astype(BF16)

    ends, w, bias, cot, table, fold0, pick, recv0, node0, sender0 = run_hbm(
        prepare,
        [
            ((edges, size), I32), (weights.shape, BF16), (biases.shape, F32), (fine, BF16),
            ((table_rows, features), I32), (tile, BF16),
            ((edges, size, size), BF16),
        ] + own_out,
        inputs,
        h0,
        scratch=[pltpu.VMEM(a.shape, I32) for a in inputs[:3]]
        + [pltpu.SemaphoreType.DMA((len(inputs),))],
    )

    slopes = [((edges,) + tile, BF16), (fine, BF16)]

    layer_scratch = [pltpu.VMEM((everyone,) + tile, BF16), pltpu.VMEM(fine, BF16)]

    def first_layer(s_ref, g0, g1, h_ref, recv, node, sender, pick, w_ref, fold_ref, info_ref, *rest):
        first_ref, slots_ref, send_ref, *sends, sum_scr = rest
        senders_into(sender, (g0[0:size, :], g1[0:size, :]), 0, w_ref, send_ref)
        pre_of = fine_pre(s_ref, recv, pick, send_ref)
        hidden = layer_forward(blocks, fold_ref[...], pre_of, node[...], None, None, sum_scr)
        first_ref[...] = (h_ref[...].astype(F32) + mm(hidden, w_ref[0, 5])).astype(BF16)
        tail = info_ref[...].astype(F32) + g0[size:, :].astype(F32) + g1[size:, :].astype(F32)
        pooled_into(lambda b: first_ref[rows_of(b), :].astype(F32), s_ref, sends, tail)
        for r, g in zip(ORDER, (g0, g1)):
            last = g[size:, :].astype(F32).astype(I32)[at_last : at_last + 1, :]
            slots_ref[r : r + 1, :] = last

    first, halo_slots, senders0, *pool_sends = run(
        first_layer,
        [(fine, BF16), ((8, features), I32), ((everyone,) + tile, BF16)] + [((pool_rows, features), BF16)] * sub_size,
        table, halo[0], halo[1], h0, recv0, node0, sender0, pick, w, fold0, info,
        scratch=[pltpu.VMEM(fine, BF16)],
    )

    def first_slopes(s_ref, recv, node, send_ref, pick, fold_ref, slope_ref, node_slope_ref, sum_scr):
        pre_of = fine_pre(s_ref, recv, pick, send_ref)
        layer_forward(blocks, fold_ref[...], pre_of, node[...], slope_ref, node_slope_ref, sum_scr)

    slope0, node_slope0 = run(
        first_slopes, slopes, table, recv0, node0, senders0, pick, fold0, scratch=[pltpu.VMEM(fine, BF16)]
    )

    pool_in = reduced(pool_sends)

    def coarse_begin(s_ref, first_ref, *refs):
        parts, (start_ref, inverse_ref, infos_ref, other, out0, out1) = refs[:pair_size], refs[pair_size:]
        total = parts[0][0:at_tail, :].astype(F32)
        tails = [part[at_tail:, :].astype(F32) for part in parts]
        counts = tails[0][at_last : at_last + 1, :]
        for part, tail in zip(parts[1:], tails[1:]):
            total = total + part[0:at_tail, :].astype(F32)
            counts = counts + tail[at_last : at_last + 1, :]
        for q in range(held):
            inverse_ref[q : q + 1, :] = jnp.broadcast_to(1.0 / jnp.maximum(counts[:, q : q + 1], 1.0), (1, features))
        for q in range(held):
            start = (total[q * size : (q + 1) * size, :] * inverse_ref[q : q + 1, :]).astype(BF16)
            for out in (start_ref, other, out0, out1):
                out[rows_of(q), :] = start
        for r, out in zip(ORDER, (out0, out1)):
            at = pl.multiple_of(scalar(s_ref, r) * size, size)
            out[at_tail:, :] = first_ref[pl.ds(at, size), :]
        pair = scalar(s_ref, at_pair)
        for mask, tail in enumerate(tails):
            infos_ref[pair ^ mask] = tail

    coarse_start, inverse, infos, other_send, *halo_sends = run(
        coarse_begin,
        [(wide, BF16), ((8, features), F32), ((held, TAIL, features), F32), (wide, BF16)]
        + [((halo_rows, features), BF16)] * rounds,
        table, first, *pool_in,
    )
    other = swapped(other_send, "dom", xor_bits[0] ^ xor_bits[1])
    coarse_halo = exchange(halo_sends)

    def coarse_prepare(h_ref, w_ref, b_ref, cot_ref, infos_ref, ends, pre, node, fold_ref, join_ref, bias_ref,
                       far_pick, cput, put, d_out, recv, sender):
        own_into(h_ref[...], 1, w_ref, b_ref, recv, node, sender)
        for i, layer in enumerate((1, 2)):
            fold_ref[i] = (mm(w_ref[layer, 2], w_ref[layer, 4]) * (0.5 / degree)).astype(BF16)
            for j, part in enumerate((0, 3)):
                columns_j = slice(j * features, (j + 1) * features)
                join_ref[i, :, columns_j] = w_ref[layer, part] * 0.5
                bias_ref[i : i + 1, columns_j] = b_ref[layer, j : j + 1, :] * 0.5
        d_out[...] = mm_t(cot_ref[...], w_ref[2, 5])
        rows, columns = grids()
        for v in range(doms):
            for q in range(held):
                tile_at = v * held + q
                around = infos_ref[q].astype(I32)
                upright = jnp.transpose(infos_ref[q]).astype(I32)
                listed = (v + 1) * listed_rows - 1
                own = sender[rows_of(q), :]
                for e in range(degree):
                    edge = tile_at * degree + e
                    near = jnp.broadcast_to(around[listed : listed + 1, e : e + 1], (1, size))
                    at = v * listed_rows + e
                    hit = columns == upright[:, at : at + 1]
                    picked = mm((hit & (near == v)).astype(BF16), own)
                    pre[edge] = picked + recv[rows_of(q), :] if v == 0 else picked
                    for i, source in enumerate([n for n in range(doms) if n != v]):
                        far_pick[rows_of(edge), i * size : (i + 1) * size] = (hit & (near == source)).astype(BF16)
                    if v == 0:
                        to = rows == around[e : e + 1, :]
                        for r in range(doms):
                            cput[q, r * size : (r + 1) * size, e * size : (e + 1) * size] = (to & (near == r)).astype(BF16)
        for edge in range(edges):
            put[edge] = (rows == ends[edge : edge + 1, :]).astype(BF16)

    coarse_edges = doms * held * degree
    pre1, node1, fold, joined, joined_bias, coarse_far, coarse_put, put, d_out2 = run(
        coarse_prepare,
        [
            ((coarse_edges,) + tile, F32), (wide, F32), ((2,) + tile, BF16),
            ((2, features, 2 * features), BF16), ((8, 2 * features), F32),
            ((coarse_edges * size, far_size), BF16), ((held, size + far_size, degree * size), BF16),
            ((edges, size, size), BF16), (fine, F32),
        ],
        coarse_start, w, bias, cot, infos, ends,
        scratch=[pltpu.VMEM(wide, F32), pltpu.VMEM(wide, BF16)],
    )

    def coarse_layer(other_ref, g0, g1, h_ref, pre, node, far_pick, w_ref, join_ref, bias_ref, fold_ref, end_ref, arrived_ref, sum_scr):
        halos = [g[0:at_tail, :] for _, g in sorted(zip(ORDER, (g0, g1)))]
        states = [h_ref[...]] + halos
        arrived = (0.5 * mm(jnp.concatenate(halos + [other_ref[...]], axis=0), w_ref[1, 1])).astype(BF16)
        arrived_ref[...] = arrived[0 : rounds * held * size, :]
        rows_all = held * size
        third = arrived[rounds * rows_all :, :]
        arrived = [arrived[r * rows_all : (r + 1) * rows_all, :] for r in range(rounds)]
        own = mm(jnp.concatenate(halos, axis=0), join_ref[0]) + bias_ref[0:1, :]
        recvs = [None] + [own[r * rows_all : (r + 1) * rows_all, 0:features] for r in range(rounds)]
        nodes_all = [node[...], own[:, features:]]
        sources = [arrived, [arrived[0], third], [arrived[1], third]]
        width = degree * size
        picked = []
        for v in range(doms):
            for q in range(held):
                at = (v * held + q) * width
                senders = jnp.concatenate([a[q * size : (q + 1) * size, :] for a in sources[v]], axis=0)
                picked.append(mm(far_pick[at : at + width, :], senders))

        def pre_of(b, e):
            v, q = divmod(b, held)
            value = pre[b * degree + e] + picked[b][e * size : (e + 1) * size, :]
            return value if v == 0 else value + recvs[v][q * size : (q + 1) * size, :]

        hidden = layer_forward(
            doms * held, fold_ref[0], pre_of, jnp.concatenate(nodes_all, axis=0), None, None, sum_scr
        )
        state = jnp.concatenate(states, axis=0).astype(F32)
        end_ref[...] = (state + mm(hidden, w_ref[1, 5])).astype(BF16)
    coarse_end, coarse_arrived = run(
        coarse_layer,
        [((doms * held * size, features), BF16), ((rounds * held * size, features), BF16)],
        other, coarse_halo[0], coarse_halo[1], coarse_start, pre1, node1, coarse_far, w, joined, joined_bias, fold,
        scratch=[pltpu.VMEM((doms * held * size, features), BF16)],
    )

    def coarse_slopes(arrived, pre, node, far_pick, fold_ref, slope_ref, node_slope_ref, sum_scr):
        width = degree * size
        picked = []
        for q in range(held):
            ats = [pl.ds((r * held + q) * size, size) for r in range(rounds)]
            senders = jnp.concatenate([arrived[at, :] for at in ats], axis=0)
            picked.append(mm(far_pick[q * width : (q + 1) * width, :], senders))

        def pre_of(q, e):
            return pre[q * degree + e] + picked[q][e * size : (e + 1) * size, :]

        layer_forward(held, fold_ref[0], pre_of, node[...], slope_ref, node_slope_ref, sum_scr)

    slope1, node_slope1 = run(
        coarse_slopes,
        [((held * degree,) + tile, BF16), (wide, BF16)],
        coarse_arrived, pre1, node1, coarse_far, fold,
        scratch=[pltpu.VMEM(wide, BF16)],
    )
    coarse_ends = share(coarse_end)

    back_out = [(tile, BF16)] * rounds + [(fine, BF16), (fine, BF16), ((everyone,) + tile, F32)]
    back_scratch = [pltpu.VMEM(fine, F32)]

    def last_layer(s_ref, slots_ref, g0, g1, *refs):
        parts = refs[:sub_size]
        first_ref, pick, put, w_ref, join_ref, bias_ref, fold_ref, d_out = refs[sub_size : sub_size + 8]
        (r0, r1, d_node, d_recv, acc_scr, hidden_ref, state_scr,
         lift_scr, own_scr, send_scr, sum_scr, slope_scr, node_slope_scr, act_scr) = refs[sub_size + 8 :]
        lift_into(parts, s_ref, lift_scr)
        for b in range(blocks):
            lifted = lift_scr[scalar(s_ref, at_pool + b)].astype(F32)
            state_scr[rows_of(b), :] = (first_ref[rows_of(b), :].astype(F32) + lifted).astype(BF16)
        for r, g in zip(ORDER, (g0, g1)):
            lifted = lift_scr[(1 + r) * slots + scalar(slots_ref, r)].astype(F32)
            state_scr[rows_of(blocks + r), :] = (g[at_tail:, :].astype(F32) + lifted).astype(BF16)
        senders = (0.5 * mm(state_scr[...], w_ref[2, 1])).astype(BF16)
        send_scr[...] = senders.reshape((everyone,) + tile)
        own_scr[...] = mm(state_scr[0 : blocks * size, :], join_ref[1]) + bias_ref[1:2, :]
        recv, node = own_scr.at[:, 0:features], own_scr.at[:, features:]
        fold = fold_ref[1]
        pre_of = fine_pre(s_ref, recv, pick, send_scr)
        hidden_ref[...] = layer_forward(blocks, fold, pre_of, node[...], slope_scr, node_slope_scr, sum_scr)
        fine_backward(d_out[...], s_ref, fold, put, slope_scr, node_slope_scr, d_node, d_recv, act_scr, acc_scr)
        halo_grads_into((r0, r1), [acc_scr[blocks:].reshape(far_size, features)], 2, w_ref)

    *halo_grads, d_node, d_recv, d_send, hidden2, middle = run(
        last_layer,
        back_out + [(fine, BF16), ((everyone * size, features), BF16)],
        table, halo_slots, *coarse_halo, *coarse_ends, first, pick, put, w, joined, joined_bias, fold, d_out2,
        scratch=[pltpu.VMEM((doms * slots,) + tile, BF16)]
        + [pltpu.VMEM((blocks * size, 2 * features), F32)]
        + layer_scratch + [pltpu.VMEM((edges,) + tile, BF16), pltpu.VMEM(fine, BF16)] + back_scratch,
    )
    returned = exchange(halo_grads)

    def last_own(cot_ref, d_node, d_recv, d_send, h_ref, hidden_ref, w_ref, grad_ref, out_ref):
        grad_ref[...] = own_back(cot_ref[...].astype(F32), 2, w_ref, d_node[...], d_recv[...], d_send[0:blocks].reshape(fine))
        out_ref[...] = (h_ref[0 : blocks * size, :].astype(F32) + mm(hidden_ref[...], w_ref[2, 5])).astype(BF16)

    grad_own, out_nodes = run(
        last_own, [(fine, F32), (fine, BF16)], cot, d_node, d_recv, d_send, middle, hidden2, w
    )

    def pool_grads(s_ref, r0, r1, own_ref, grad_ref, *sends):
        grad_ref[...] = own_ref[...]
        for r, arrived in zip(ORDER, (r0, r1)):
            at = scalar(s_ref, r)
            grad_ref[at] = grad_ref[at] + arrived[...].astype(F32)
        pooled_into(lambda b: grad_ref[b], s_ref, sends)

    grad_middle, *grad_sends = run(
        pool_grads,
        [(tiles, F32)] + [(wide, BF16)] * sub_size,
        table, returned[0], returned[1], grad_own.reshape(tiles),
    )
    grads_in = reduced(grad_sends)

    def coarse_back(*refs):
        parts = refs[:pair_size]
        put, slope_ref, node_slope_ref, w_ref, fold_ref, r0, r1, grad_ref, d_node, d_pre, act_scr = refs[pair_size:]
        grad = parts[0][...].astype(F32)
        for part in parts[1:]:
            grad = grad + part[...].astype(F32)
        grad_ref[...] = grad
        d_out = mm_t(grad.astype(BF16), w_ref[1, 5])
        node_backward(d_out, fold_ref[0], node_slope_ref, d_node, act_scr)
        for q in range(held):
            for e in range(degree):
                edge = q * degree + e
                d_pre[rows_of(edge), :] = (act_scr[rows_of(q), :] * slope_ref[edge].astype(F32)).astype(BF16)
        width = degree * size
        grads = [mm(put[q, size:, :], d_pre[q * width : (q + 1) * width, :]) for q in range(held)]
        halo_grads_into((r0, r1), grads, 1, w_ref)

    *coarse_sends, coarse_grad, d_node, d_pre = run(
        coarse_back,
        [(wide, BF16)] * rounds + [(wide, F32), (wide, BF16), ((held * degree * size, features), BF16)],
        *grads_in, coarse_put, slope1, node_slope1, w, fold,
        scratch=[pltpu.VMEM(wide, F32)],
    )
    coarse_returned = exchange(coarse_sends)

    def coarse_own(grad_ref, put, d_node, d_pre, w_ref, own_ref):
        width = degree * size
        d_send = [mm(put[q, 0:size, :], d_pre[q * width : (q + 1) * width, :]) for q in range(held)]
        d_recv = []
        for q in range(held):
            total = None
            for e in range(degree):
                part = d_pre[rows_of(q * degree + e), :].astype(F32)
                total = part if total is None else total + part
            d_recv.append(total.astype(BF16))
        own_ref[...] = own_back(
            grad_ref[...], 1, w_ref, d_node[...], jnp.concatenate(d_recv, axis=0), jnp.concatenate(d_send, axis=0)
        )

    (coarse_grad,) = run(coarse_own, [(wide, F32)], coarse_grad, coarse_put, d_node, d_pre, w)

    def scale(own_ref, r0, r1, inverse_ref, out_ref):
        for q in range(held):
            rows = rows_of(q)
            total = own_ref[rows, :] + r0[rows, :].astype(F32) + r1[rows, :].astype(F32)
            out_ref[rows, :] = (total * inverse_ref[q : q + 1, :]).astype(BF16)

    (scaled,) = run(scale, [(wide, BF16)], coarse_grad, *coarse_returned, inverse)
    scaled_parts = share(scaled)

    def first_back(s_ref, *refs):
        parts = refs[:sub_size]
        middle_ref, put, slope_ref, node_slope_ref, w_ref, fold_ref = refs[sub_size : sub_size + 6]
        r0, r1, d_node, d_recv, acc_scr, grad_ref, lift_scr, act_scr = refs[sub_size + 6 :]
        lift_into(parts, s_ref, lift_scr)
        for b in range(blocks):
            lifted = lift_scr[scalar(s_ref, at_pool + b)].astype(F32)
            grad_ref[rows_of(b), :] = middle_ref[b] + lifted
        d_out = mm_t(grad_ref[...].astype(BF16), w_ref[0, 5])
        fine_backward(d_out, s_ref, fold_ref[...], put, slope_ref, node_slope_ref, d_node, d_recv, act_scr, acc_scr)
        halo_grads_into((r0, r1), [acc_scr[blocks:].reshape(far_size, features)], 0, w_ref)

    *halo_grads, d_node, d_recv, d_send, grad_first = run(
        first_back,
        back_out + [(fine, F32)],
        table, *scaled_parts, grad_middle, put, slope0, node_slope0, w, fold0,
        scratch=[pltpu.VMEM((slots,) + tile, BF16)] + back_scratch,
    )
    returned = exchange(halo_grads)

    def first_own(first_ref, d_node, d_recv, d_send, w_ref, grad_ref):
        grad_ref[...] = own_back(first_ref[...], 0, w_ref, d_node[...], d_recv[...], d_send[0:blocks].reshape(fine))

    (grad_own,) = run(first_own, [(fine, F32)], grad_first, d_node, d_recv, d_send, w)

    def finish(s_ref, r0, r1, own_ref, out_ref):
        out_ref[...] = own_ref[...]
        for r, arrived in zip(ORDER, (r0, r1)):
            at = scalar(s_ref, r)
            out_ref[at] = out_ref[at] + arrived[...].astype(F32)

    (grad_nodes,) = run(finish, [(tiles, F32)], table, returned[0], returned[1], grad_own.reshape(tiles))
    return (out_nodes, grad_nodes.reshape(fine))


def solution(mesh):
    split = ("groups", "dom", "pair", "sub")
    placed = (
        P(split, None),
        P(split, None),
        P(split, None, None),
        P(split, None),
        P(split, None, None),
        P(split),
        P(split, None),
        P(split, None, None),
        P(),
        P(),
    )
    return jax.shard_map(
        per_device,
        mesh=mesh,
        in_specs=placed,
        out_specs=(P(split, None), P(split, None)),
        check_vma=False,
    )
```

```python
import jax
import jax.numpy as jnp
from jax import lax
from jax.experimental import pallas as pl
from jax.experimental.pallas import tpu as pltpu
from jax.sharding import PartitionSpec as P

F32 = jnp.float32
BF16 = jnp.bfloat16
I32 = jnp.int32
TAIL = 16
GROUP_AXES = ("pair", "sub")
ORDER = (1, 0)


def swapped(value, axis, mask):
    size = lax.axis_size(axis)
    return lax.ppermute(value, axis, [(source, source ^ mask) for source in range(size)])


def mm(a, b):
    return jnp.dot(a, b, preferred_element_type=F32)


def mm_t(a, b):
    return lax.dot_general(a, b, (((1,), (1,)), ((), ())), preferred_element_type=F32)


def scalar(table, index):
    return table[index : index + 1, :][0, 0]


def run(kernel, outs, *arrays, scratch=(), flops=0):
    return pl.pallas_call(
        kernel,
        out_shape=[jax.ShapeDtypeStruct(shape, dtype) for shape, dtype in outs],
        in_specs=[pl.BlockSpec(memory_space=pltpu.VMEM)] * len(arrays),
        out_specs=[pl.BlockSpec(memory_space=pltpu.VMEM)] * len(outs),
        scratch_shapes=list(scratch),
        compiler_params=pltpu.CompilerParams(vmem_limit_bytes=12 * 2**20),
        cost_estimate=pl.CostEstimate(flops=flops, bytes_accessed=2**20, transcendentals=0),
    )(*arrays)


def run_hbm(kernel, outs, far, *near, scratch=()):
    return pl.pallas_call(
        kernel,
        out_shape=[pltpu.VMEM(shape, dtype) for shape, dtype in outs],
        in_specs=[pl.BlockSpec(memory_space=pltpu.HBM)] * len(far) + [pl.BlockSpec(memory_space=pltpu.VMEM)] * len(near),
        out_specs=[pl.BlockSpec(memory_space=pltpu.VMEM)] * len(outs),
        scratch_shapes=list(scratch),
        compiler_params=pltpu.CompilerParams(vmem_limit_bytes=12 * 2**20),
        cost_estimate=pl.CostEstimate(flops=0, bytes_accessed=2**20, transcendentals=0),
    )(*[pltpu.with_memory_space_constraint(array, pltpu.HBM) for array in far], *near)


def per_device(
    nodes,
    cotangent,
    send_blocks,
    neighbour_blocks,
    neighbour_nodes,
    pool_map,
    coarse_blocks,
    coarse_nodes,
    weights,
    biases,
):
    size, features = neighbour_nodes.shape[2], nodes.shape[1]
    blocks, degree = neighbour_blocks.shape
    xor_bits = (1, lax.axis_size("dom") // 2)
    rounds = len(xor_bits)
    slots = lax.axis_size(GROUP_AXES)
    pair_size, sub_size = lax.axis_size("pair"), lax.axis_size("sub")
    edges = blocks * degree
    far_size = rounds * size
    everyone = blocks + rounds
    tile = (size, features)
    fine = (blocks * size, features)
    tiles = (blocks,) + tile

    held = pair_size
    wide = (held * size, features)
    doms = 1 + rounds
    listed_rows = degree + 1
    at_last = doms * listed_rows
    at_tail = held * size
    pool_rows = at_tail + TAIL
    halo_rows = at_tail + size

    at_near = rounds
    at_pool = at_near + edges
    at_pair = at_pool + blocks
    at_sub = at_pair + 1
    table_rows = -(-(at_sub + 1) // 8) * 8

    def exchange(pieces):
        return [swapped(piece, "dom", xor_bits[r]) for r, piece in zip(ORDER, pieces)]

    def reduced(pieces):
        arrived = [swapped(piece, "sub", mask) for mask, piece in enumerate(pieces) if mask > 0]
        (chip,) = run(add_parts, [(pieces[0].shape, BF16)], pieces[0], *arrived)
        return [chip] + [swapped(chip, "pair", mask) for mask in range(1, pair_size)]

    def add_parts(*refs):
        total = refs[0][...].astype(F32)
        for part in refs[1:-1]:
            total = total + part[...].astype(F32)
        refs[-1][...] = total.astype(BF16)

    def share(piece):
        return [piece] + [swapped(piece, "sub", mask) for mask in range(1, sub_size)]

    def rows_of(b):
        return pl.ds(b * size, size)

    def begun(pairs, sems):
        copies = [pltpu.make_async_copy(source, target, sems.at[i]) for i, (source, target) in enumerate(pairs)]
        for copy in copies:
            copy.start()
        return copies

    def fetch(pairs, sems):
        for copy in begun(pairs, sems):
            copy.wait()

    def choose(send_in, ends_in, listed_in, pool_in, nodes_in, h_ref, info_ref, out0, out1,
               send_scr, ends_scr, listed_scr, pool_scr, sems):
        parts = [(nodes_in.at[rows_of(b)], h_ref.at[rows_of(b)]) for b in range(blocks)]
        lists = [(send_in, send_scr), (ends_in, ends_scr), (listed_in, listed_scr), (pool_in, pool_scr)]
        copies = begun(lists + parts, sems)
        for copy in copies[: len(lists)]:
            copy.wait()
        lanes = lax.broadcasted_iota(I32, (1, features), 1)
        listed = jnp.zeros((1, features), I32)
        for e in range(degree):
            listed = jnp.where(lanes == e, jnp.broadcast_to(listed_scr[0:1, e : e + 1], (1, features)), listed)
        listed = [ends_scr[...].astype(F32), listed.astype(F32)]

        def tail_of(v, last):
            before = [jnp.zeros((v * listed_rows, features), F32)] if v else []
            left = TAIL - 1 - (v + 1) * listed_rows
            after = [jnp.zeros((left, features), F32)] if left else []
            return jnp.concatenate(before + listed + after + [last.astype(F32)], axis=0).astype(BF16)

        info_ref[...] = tail_of(0, jnp.zeros((1, features), I32))
        for r, out in zip(ORDER, (out0, out1)):
            chosen = send_scr[0:1, r : r + 1]
            slot = jnp.zeros((1, 1), I32)
            for b in range(blocks):
                slot = jnp.where(chosen == b, pool_scr[0:1, b : b + 1], slot)
            out[size:, :] = tail_of(1 + r, jnp.broadcast_to(slot, (1, features)))
        starts = [pl.multiple_of(send_scr[0:1, r : r + 1][0, 0] * size, size) for r in ORDER]
        for copy in copies[len(lists) :]:
            copy.wait()
        for at, out in zip(starts, (out0, out1)):
            out[0:size, :] = h_ref[pl.ds(at, size), :]

    sent = send_blocks.reshape(1, rounds)
    coarse_ends = coarse_nodes.reshape(degree, size)
    pools = pool_map.reshape(1, blocks)
    h0, info, *first_sends = run_hbm(
        choose,
        [(fine, BF16), ((TAIL, features), BF16)] + [((size + TAIL, features), BF16)] * rounds,
        [sent, coarse_ends, coarse_blocks, pools, nodes],
        scratch=[pltpu.VMEM(a.shape, I32) for a in (sent, coarse_ends, coarse_blocks, pools)]
        + [pltpu.SemaphoreType.DMA((4 + blocks,))],
    )
    halo = exchange(first_sends)

    def grids():
        return lax.broadcasted_iota(I32, (size, size), 0), lax.broadcasted_iota(I32, (size, size), 1)

    def own_into(state, layer, w_ref, b_ref, recv_ref, node_ref, sender_ref):
        recv_ref[...] = 0.5 * (mm(state, w_ref[layer, 0]) + b_ref[layer, 0:1, :])
        node_ref[...] = 0.5 * (mm(state, w_ref[layer, 3]) + b_ref[layer, 1:2, :])
        sender_ref[...] = (0.5 * mm(state, w_ref[layer, 1])).astype(BF16)

    def layer_forward(count, fold, pre_of, node, slope_ref, node_slope_ref, sum_scr):
        for b in range(count):
            total = None
            for e in range(degree):
                edge = b * degree + e
                half = pre_of(b, e)
                up = 1.0 + jnp.tanh(half)
                active = half * up
                if slope_ref is not None:
                    slope_ref[edge] = (up + active * (2.0 - up)).astype(BF16)
                total = active if total is None else total + active
            sum_scr[rows_of(b), :] = total.astype(BF16)
        half = node + mm(sum_scr[...], fold)
        up = 1.0 + jnp.tanh(half)
        hidden = half * up
        if slope_ref is not None:
            node_slope_ref[...] = (0.5 * (up + hidden * (2.0 - up))).astype(BF16)
        return hidden.astype(BF16)

    def senders_into(own, halos, layer, w_ref, send_scr):
        for r, g in zip(ORDER, halos):
            send_scr[blocks + r] = (0.5 * mm(g, w_ref[layer, 1])).astype(BF16)
        for b in range(blocks):
            send_scr[b] = own[rows_of(b), :]

    def fine_pre(s_ref, recv, pick, send_scr):
        def pre_of(b, e):
            edge = b * degree + e
            return recv[rows_of(b), :] + mm(pick[edge], send_scr[scalar(s_ref, at_near + edge)])

        return pre_of

    def node_backward(d_out, fold, node_slope_ref, d_node, act_scr):
        d_hidden = (d_out * node_slope_ref[...].astype(F32)).astype(BF16)
        d_node[...] = d_hidden
        act_scr[...] = mm_t(d_hidden, fold)

    def fine_backward(d_out, s_ref, fold, put_ref, slope_ref, node_slope_ref, d_node, d_recv, act_scr, acc_scr):
        node_backward(d_out, fold, node_slope_ref, d_node, act_scr)
        acc_scr[...] = jnp.zeros_like(acc_scr)
        for b in range(blocks):
            d_active = act_scr[rows_of(b), :]
            total = None
            for e in range(degree):
                edge = b * degree + e
                d_pre = d_active * slope_ref[edge].astype(F32)
                total = d_pre if total is None else total + d_pre
                near = scalar(s_ref, at_near + edge)
                acc_scr[near] = acc_scr[near] + mm(put_ref[edge], d_pre.astype(BF16))
            d_recv[rows_of(b), :] = total.astype(BF16)

    def halo_grads_into(outs, grads, layer, w_ref):
        for r, out in zip(ORDER, outs):
            own = jnp.concatenate([g[r * size : (r + 1) * size, :] for g in grads], axis=0)
            out[...] = mm_t(own.astype(BF16), w_ref[layer, 1]).astype(BF16)

    def own_back(grad, layer, w_ref, d_node, d_recv, d_send):
        return (
            grad
            + mm_t(d_recv, w_ref[layer, 0])
            + mm_t(d_node, w_ref[layer, 3])
            + mm_t(d_send.astype(BF16), w_ref[layer, 1])
        )

    def pooled_into(read, s_ref, out_refs, tail=None):
        sub = scalar(s_ref, at_sub)
        lanes = lax.broadcasted_iota(I32, (1, features), 1)
        for sub_mask, out in enumerate(out_refs):
            counts = jnp.zeros((1, features), F32)
            for q in range(held):
                slot = q * sub_size + (sub ^ sub_mask)
                total, count = None, None
                for b in range(blocks):
                    hit = (scalar(s_ref, at_pool + b) == slot).astype(F32)
                    part = read(b) * hit
                    total = part if total is None else total + part
                    count = hit if count is None else count + hit
                out[rows_of(q), :] = total.astype(BF16)
                counts = counts + jnp.where(lanes == q, count, 0.0)
            if tail is not None:
                last = lax.broadcasted_iota(I32, (TAIL, features), 0) == at_last
                kept = tail if sub_mask == 0 else jnp.zeros_like(tail)
                out[at_tail:, :] = jnp.where(last, jnp.broadcast_to(counts, tail.shape), kept).astype(BF16)

    def lift_into(parts, s_ref, lift_scr):
        sub = scalar(s_ref, at_sub)
        for mask, part in enumerate(parts):
            for q in range(held):
                for v in range(part.shape[0] // (held * size)):
                    lift_scr[v * slots + q * sub_size + (sub ^ mask)] = part[rows_of(v * held + q), :]

    inputs = [
        sent,
        neighbour_blocks,
        pools,
        neighbour_nodes.reshape(edges, size),
        weights,
        biases,
        cotangent,
    ]
    own_out = [(fine, F32), (fine, F32), (fine, BF16)]

    def prepare(*refs):
        sources, h_ref = refs[: len(inputs)], refs[len(inputs)]
        ends, w_ref, b_ref, c_ref, s_ref, fold_ref, pick, recv, node, sender, *kept, sems = refs[len(inputs) + 1 :]
        send_scr, near_scr, pool_scr = kept
        fetch(list(zip(sources, kept + [ends, w_ref, b_ref, c_ref])), sems)

        def put_row(index, ref, i, j):
            s_ref[index : index + 1, :] = jnp.broadcast_to(ref[i : i + 1, j : j + 1], (1, features))

        for r in range(rounds):
            put_row(r, send_scr, 0, r)
        for b in range(blocks):
            for e in range(degree):
                put_row(at_near + b * degree + e, near_scr, b, e)
            put_row(at_pool + b, pool_scr, 0, b)
        s_ref[at_pair : at_pair + 1, :] = jnp.full((1, features), lax.axis_index("pair"), I32)
        s_ref[at_sub : at_sub + 1, :] = jnp.full((1, features), lax.axis_index("sub"), I32)
        own_into(h_ref[...], 0, w_ref, b_ref, recv, node, sender)
        columns = grids()[1]
        upright = jnp.transpose(ends[...])
        for edge in range(edges):
            pick[edge] = (columns == upright[:, edge : edge + 1]).astype(BF16)
        fold_ref[...] = (mm(w_ref[0, 2], w_ref[0, 4]) * (0.5 / degree)).astype(BF16)

    ends, w, bias, cot, table, fold0, pick, recv0, node0, sender0 = run_hbm(
        prepare,
        [
            ((edges, size), I32), (weights.shape, BF16), (biases.shape, F32), (fine, BF16),
            ((table_rows, features), I32), (tile, BF16),
            ((edges, size, size), BF16),
        ] + own_out,
        inputs,
        h0,
        scratch=[pltpu.VMEM(a.shape, I32) for a in inputs[:3]]
        + [pltpu.SemaphoreType.DMA((len(inputs),))],
    )

    slopes = [((edges,) + tile, BF16), (fine, BF16)]

    layer_scratch = [pltpu.VMEM((everyone,) + tile, BF16), pltpu.VMEM(fine, BF16)]

    def first_layer(s_ref, g0, g1, h_ref, recv, node, sender, pick, w_ref, fold_ref, info_ref, *rest):
        first_ref, slots_ref, send_ref, *sends, sum_scr = rest
        senders_into(sender, (g0[0:size, :], g1[0:size, :]), 0, w_ref, send_ref)
        pre_of = fine_pre(s_ref, recv, pick, send_ref)
        hidden = layer_forward(blocks, fold_ref[...], pre_of, node[...], None, None, sum_scr)
        first_ref[...] = (h_ref[...].astype(F32) + mm(hidden, w_ref[0, 5])).astype(BF16)
        tail = info_ref[...].astype(F32) + g0[size:, :].astype(F32) + g1[size:, :].astype(F32)
        pooled_into(lambda b: first_ref[rows_of(b), :].astype(F32), s_ref, sends, tail)
        for r, g in zip(ORDER, (g0, g1)):
            last = g[size:, :].astype(F32).astype(I32)[at_last : at_last + 1, :]
            slots_ref[r : r + 1, :] = last

    first, halo_slots, senders0, *pool_sends = run(
        first_layer,
        [(fine, BF16), ((8, features), I32), ((everyone,) + tile, BF16)] + [((pool_rows, features), BF16)] * sub_size,
        table, halo[0], halo[1], h0, recv0, node0, sender0, pick, w, fold0, info,
        scratch=[pltpu.VMEM(fine, BF16)],
    )

    def first_slopes(s_ref, recv, node, send_ref, pick, fold_ref, slope_ref, node_slope_ref, sum_scr):
        pre_of = fine_pre(s_ref, recv, pick, send_ref)
        layer_forward(blocks, fold_ref[...], pre_of, node[...], slope_ref, node_slope_ref, sum_scr)

    slope0, node_slope0 = run(
        first_slopes, slopes, table, recv0, node0, senders0, pick, fold0, scratch=[pltpu.VMEM(fine, BF16)]
    )

    pool_in = reduced(pool_sends)

    def coarse_begin(s_ref, first_ref, *refs):
        parts, (start_ref, inverse_ref, infos_ref, other, out0, out1) = refs[:pair_size], refs[pair_size:]
        total = parts[0][0:at_tail, :].astype(F32)
        tails = [part[at_tail:, :].astype(F32) for part in parts]
        counts = tails[0][at_last : at_last + 1, :]
        for part, tail in zip(parts[1:], tails[1:]):
            total = total + part[0:at_tail, :].astype(F32)
            counts = counts + tail[at_last : at_last + 1, :]
        for q in range(held):
            inverse_ref[q : q + 1, :] = jnp.broadcast_to(1.0 / jnp.maximum(counts[:, q : q + 1], 1.0), (1, features))
        for q in range(held):
            start = (total[q * size : (q + 1) * size, :] * inverse_ref[q : q + 1, :]).astype(BF16)
            for out in (start_ref, other, out0, out1):
                out[rows_of(q), :] = start
        for r, out in zip(ORDER, (out0, out1)):
            at = pl.multiple_of(scalar(s_ref, r) * size, size)
            out[at_tail:, :] = first_ref[pl.ds(at, size), :]
        pair = scalar(s_ref, at_pair)
        for mask, tail in enumerate(tails):
            infos_ref[pair ^ mask] = tail

    coarse_start, inverse, infos, other_send, *halo_sends = run(
        coarse_begin,
        [(wide, BF16), ((8, features), F32), ((held, TAIL, features), F32), (wide, BF16)]
        + [((halo_rows, features), BF16)] * rounds,
        table, first, *pool_in,
    )
    other = swapped(other_send, "dom", xor_bits[0] ^ xor_bits[1])
    coarse_halo = exchange(halo_sends)

    def coarse_prepare(h_ref, w_ref, b_ref, cot_ref, infos_ref, ends, pre, node, fold_ref, join_ref, bias_ref,
                       far_pick, cput, put, d_out, recv, sender):
        own_into(h_ref[...], 1, w_ref, b_ref, recv, node, sender)
        for i, layer in enumerate((1, 2)):
            fold_ref[i] = (mm(w_ref[layer, 2], w_ref[layer, 4]) * (0.5 / degree)).astype(BF16)
            for j, part in enumerate((0, 3)):
                columns_j = slice(j * features, (j + 1) * features)
                join_ref[i, :, columns_j] = w_ref[layer, part] * 0.5
                bias_ref[i : i + 1, columns_j] = b_ref[layer, j : j + 1, :] * 0.5
        d_out[...] = mm_t(cot_ref[...], w_ref[2, 5])
        rows, columns = grids()
        for v in range(doms):
            for q in range(held):
                tile_at = v * held + q
                around = infos_ref[q].astype(I32)
                upright = jnp.transpose(infos_ref[q]).astype(I32)
                listed = (v + 1) * listed_rows - 1
                own = sender[rows_of(q), :]
                for e in range(degree):
                    edge = tile_at * degree + e
                    near = jnp.broadcast_to(around[listed : listed + 1, e : e + 1], (1, size))
                    at = v * listed_rows + e
                    hit = columns == upright[:, at : at + 1]
                    picked = mm((hit & (near == v)).astype(BF16), own)
                    pre[edge] = picked + recv[rows_of(q), :] if v == 0 else picked
                    for i, source in enumerate([n for n in range(doms) if n != v]):
                        far_pick[rows_of(edge), i * size : (i + 1) * size] = (hit & (near == source)).astype(BF16)
                    to = rows == around[at : at + 1, :]
                    for r in range(doms):
                        cput[tile_at, r * size : (r + 1) * size, e * size : (e + 1) * size] = (to & (near == r)).astype(BF16)
        for edge in range(edges):
            put[edge] = (rows == ends[edge : edge + 1, :]).astype(BF16)

    coarse_edges = doms * held * degree
    pre1, node1, fold, joined, joined_bias, coarse_far, coarse_put, put, d_out2 = run(
        coarse_prepare,
        [
            ((coarse_edges,) + tile, F32), (wide, F32), ((2,) + tile, BF16),
            ((2, features, 2 * features), BF16), ((8, 2 * features), F32),
            ((coarse_edges * size, far_size), BF16), ((doms * held, doms * size, degree * size), BF16),
            ((edges, size, size), BF16), (fine, F32),
        ],
        coarse_start, w, bias, cot, infos, ends,
        scratch=[pltpu.VMEM(wide, F32), pltpu.VMEM(wide, BF16)],
    )

    def coarse_forward(other_ref, g0, g1, pre, node, far_pick, w_ref, join_ref, bias_ref, fold_ref, slope_ref, node_slope_ref, sum_scr):
        halos = [g[0:at_tail, :] for _, g in sorted(zip(ORDER, (g0, g1)))]
        arrived = (0.5 * mm(jnp.concatenate(halos + [other_ref[...]], axis=0), w_ref[1, 1])).astype(BF16)
        rows_all = held * size
        third = arrived[rounds * rows_all :, :]
        arrived = [arrived[r * rows_all : (r + 1) * rows_all, :] for r in range(rounds)]
        own = mm(jnp.concatenate(halos, axis=0), join_ref[0]) + bias_ref[0:1, :]
        recvs = [None] + [own[r * rows_all : (r + 1) * rows_all, 0:features] for r in range(rounds)]
        nodes_all = [node[...], own[:, features:]]
        sources = [arrived, [arrived[0], third], [arrived[1], third]]
        width = degree * size
        picked = []
        for v in range(doms):
            for q in range(held):
                at = (v * held + q) * width
                senders = jnp.concatenate([a[q * size : (q + 1) * size, :] for a in sources[v]], axis=0)
                picked.append(mm(far_pick[at : at + width, :], senders))

        def pre_of(b, e):
            v, q = divmod(b, held)
            value = pre[b * degree + e] + picked[b][e * size : (e + 1) * size, :]
            return value if v == 0 else value + recvs[v][q * size : (q + 1) * size, :]

        nodes_all = jnp.concatenate(nodes_all, axis=0)
        return layer_forward(doms * held, fold_ref[0], pre_of, nodes_all, slope_ref, node_slope_ref, sum_scr)

    def coarse_layer(other_ref, g0, g1, h_ref, pre, node, far_pick, w_ref, join_ref, bias_ref, fold_ref, end_ref, sum_scr):
        hidden = coarse_forward(
            other_ref, g0, g1, pre, node, far_pick, w_ref, join_ref, bias_ref, fold_ref, None, None, sum_scr
        )
        halos = [g[0:at_tail, :] for _, g in sorted(zip(ORDER, (g0, g1)))]
        state = jnp.concatenate([h_ref[...]] + halos, axis=0).astype(F32)
        end_ref[...] = (state + mm(hidden, w_ref[1, 5])).astype(BF16)

    all_wide = (doms * held * size, features)
    (coarse_end,) = run(
        coarse_layer,
        [(all_wide, BF16)],
        other, *coarse_halo, coarse_start, pre1, node1, coarse_far, w, joined, joined_bias, fold,
        scratch=[pltpu.VMEM(all_wide, BF16)],
    )

    def coarse_slopes(*refs):
        coarse_forward(*refs)

    slope1, node_slope1 = run(
        coarse_slopes,
        [((coarse_edges,) + tile, BF16), (all_wide, BF16)],
        other, *coarse_halo, pre1, node1, coarse_far, w, joined, joined_bias, fold,
        scratch=[pltpu.VMEM(all_wide, BF16)],
    )
    coarse_ends = share(coarse_end)

    back_out = [(tile, BF16)] * rounds + [(fine, BF16), (fine, BF16), ((everyone,) + tile, F32)]
    back_scratch = [pltpu.VMEM(fine, F32)]

    def last_layer(s_ref, slots_ref, g0, g1, *refs):
        parts = refs[:sub_size]
        first_ref, pick, put, w_ref, join_ref, bias_ref, fold_ref, d_out = refs[sub_size : sub_size + 8]
        (r0, r1, d_node, d_recv, acc_scr, hidden_ref, state_scr,
         lift_scr, own_scr, send_scr, sum_scr, slope_scr, node_slope_scr, act_scr) = refs[sub_size + 8 :]
        lift_into(parts, s_ref, lift_scr)
        for b in range(blocks):
            lifted = lift_scr[scalar(s_ref, at_pool + b)].astype(F32)
            state_scr[rows_of(b), :] = (first_ref[rows_of(b), :].astype(F32) + lifted).astype(BF16)
        for r, g in zip(ORDER, (g0, g1)):
            lifted = lift_scr[(1 + r) * slots + scalar(slots_ref, r)].astype(F32)
            state_scr[rows_of(blocks + r), :] = (g[at_tail:, :].astype(F32) + lifted).astype(BF16)
        senders = (0.5 * mm(state_scr[...], w_ref[2, 1])).astype(BF16)
        send_scr[...] = senders.reshape((everyone,) + tile)
        own_scr[...] = mm(state_scr[0 : blocks * size, :], join_ref[1]) + bias_ref[1:2, :]
        recv, node = own_scr.at[:, 0:features], own_scr.at[:, features:]
        fold = fold_ref[1]
        pre_of = fine_pre(s_ref, recv, pick, send_scr)
        hidden_ref[...] = layer_forward(blocks, fold, pre_of, node[...], slope_scr, node_slope_scr, sum_scr)
        fine_backward(d_out[...], s_ref, fold, put, slope_scr, node_slope_scr, d_node, d_recv, act_scr, acc_scr)
        halo_grads_into((r0, r1), [acc_scr[blocks:].reshape(far_size, features)], 2, w_ref)

    *halo_grads, d_node, d_recv, d_send, hidden2, middle = run(
        last_layer,
        back_out + [(fine, BF16), ((everyone * size, features), BF16)],
        table, halo_slots, *coarse_halo, *coarse_ends, first, pick, put, w, joined, joined_bias, fold, d_out2,
        scratch=[pltpu.VMEM((doms * slots,) + tile, BF16)]
        + [pltpu.VMEM((blocks * size, 2 * features), F32)]
        + layer_scratch + [pltpu.VMEM((edges,) + tile, BF16), pltpu.VMEM(fine, BF16)] + back_scratch,
    )

    def last_pool(s_ref, slots_ref, cot_ref, d_node, d_recv, d_send, g0, g1, w_ref, grad_ref, *outs):
        grad_ref[...] = own_back(
            cot_ref[...].astype(F32), 2, w_ref, d_node[...], d_recv[...], d_send[0:blocks].reshape(fine)
        )
        pooled_into(lambda b: grad_ref[rows_of(b), :], s_ref, outs)
        sub = scalar(s_ref, at_sub)
        for r, g in zip(ORDER, (g0, g1)):
            slot = scalar(slots_ref, r)
            for sub_mask, out in enumerate(outs):
                for q in range(held):
                    hit = (slot == q * sub_size + (sub ^ sub_mask)).astype(F32)
                    out[rows_of((1 + r) * held + q), :] = (g[...].astype(F32) * hit).astype(BF16)

    grad_own, *grad_sends = run(
        last_pool,
        [(fine, F32)] + [(all_wide, BF16)] * sub_size,
        table, halo_slots, cot, d_node, d_recv, d_send, *halo_grads, w,
    )
    grad_parts = grad_sends[:1] + [swapped(piece, "sub", mask) for mask, piece in enumerate(grad_sends) if mask > 0]

    def last_out(h_ref, hidden_ref, w_ref, out_ref):
        out_ref[...] = (h_ref[0 : blocks * size, :].astype(F32) + mm(hidden_ref[...], w_ref[2, 5])).astype(BF16)

    (out_nodes,) = run(last_out, [(fine, BF16)], middle, hidden2, w)

    def coarse_back(*refs):
        parts = refs[:sub_size]
        g0, g1, put, slope_ref, node_slope_ref, w_ref, fold_ref = refs[sub_size : sub_size + 7]
        other_ref, out0, out1, grad_ref, d_node, recv_ref, send_ref, act_scr, pre_scr = refs[sub_size + 7 :]
        grad = parts[0][...].astype(F32)
        for part in parts[1:]:
            grad = grad + part[...].astype(F32)
        rows_all, width = held * size, degree * size
        grad_ref[...] = grad[0:rows_all, :]
        node_backward(mm_t(grad.astype(BF16), w_ref[1, 5]), fold_ref[0], node_slope_ref, d_node, act_scr)
        recvs = []
        for b in range(doms * held):
            total = None
            for e in range(degree):
                edge = b * degree + e
                d_pre = act_scr[rows_of(b), :] * slope_ref[edge].astype(F32)
                total = d_pre if total is None else total + d_pre
                pre_scr[rows_of(edge), :] = d_pre.astype(BF16)
            recvs.append(total.astype(BF16))
        senders = []
        for v in range(doms):
            tiles_v = [mm(put[v * held + q], pre_scr[pl.ds((v * held + q) * width, width), :]) for q in range(held)]
            senders.append(
                [jnp.concatenate([t[n * size : (n + 1) * size, :] for t in tiles_v], axis=0) for n in range(doms)]
            )
        send_ref[...] = (senders[0][0] + senders[1][1] + senders[2][2]).astype(BF16)
        recv_ref[...] = jnp.concatenate(recvs[:held], axis=0)
        to_rounds = [senders[0][1] + senders[1][0], senders[0][2] + senders[2][0]]
        to_other = senders[1][2] + senders[2][1]
        sent = mm_t(jnp.concatenate(to_rounds + [to_other], axis=0).astype(BF16), w_ref[1, 1])
        sums = (
            grad[rows_all:, :]
            + mm_t(jnp.concatenate(recvs[held:], axis=0), w_ref[1, 0])
            + mm_t(d_node[rows_all:, :], w_ref[1, 3])
            + sent[0 : rounds * rows_all, :]
        ).astype(BF16)
        other_ref[...] = sent[rounds * rows_all :, :].astype(BF16)
        for r, g, out in zip(ORDER, (g0, g1), (out0, out1)):
            out[0:at_tail, :] = sums[r * rows_all : (r + 1) * rows_all, :]
            out[at_tail:, :] = g[...]

    other_send, *coarse_sends, coarse_grad, d_node, d_recv, d_send = run(
        coarse_back,
        [(wide, BF16)] + [((halo_rows, features), BF16)] * rounds
        + [(wide, F32), (all_wide, BF16), (wide, BF16), (wide, BF16)],
        *grad_parts, *halo_grads, coarse_put, slope1, node_slope1, w, fold,
        scratch=[pltpu.VMEM(all_wide, F32), pltpu.VMEM((coarse_edges * size, features), BF16)],
    )
    other = swapped(other_send, "dom", xor_bits[0] ^ xor_bits[1])
    returned = exchange(coarse_sends)

    def coarse_own(grad_ref, d_node, d_recv, d_send, w_ref, own_ref):
        own_ref[...] = own_back(grad_ref[...], 1, w_ref, d_node[0 : held * size, :], d_recv[...], d_send[...])

    (coarse_grad,) = run(coarse_own, [(wide, F32)], coarse_grad, d_node, d_recv, d_send, w)

    def chip_sum(own_ref, other_ref, r0, r1, out_ref):
        total = own_ref[...] + other_ref[...].astype(F32)
        for r in (r0, r1):
            total = total + r[0:at_tail, :].astype(F32)
        out_ref[...] = total.astype(BF16)

    (chip,) = run(chip_sum, [(wide, BF16)], coarse_grad, other, *returned)
    chips = [chip] + [swapped(chip, "pair", mask) for mask in range(1, pair_size)]

    def middle_grads(s_ref, own_ref, r0, r1, grad_ref):
        grad_ref[...] = own_ref[...]
        for r, arrived in zip(ORDER, (r0, r1)):
            at = scalar(s_ref, r)
            grad_ref[at] = grad_ref[at] + arrived[at_tail:, :].astype(F32)

    (grad_middle,) = run(middle_grads, [(tiles, F32)], table, grad_own.reshape(tiles), *returned)

    def scale(*refs):
        parts, (inverse_ref, out_ref) = refs[:pair_size], refs[pair_size:]
        for q in range(held):
            rows = rows_of(q)
            total = parts[0][rows, :].astype(F32)
            for part in parts[1:]:
                total = total + part[rows, :].astype(F32)
            out_ref[rows, :] = (total * inverse_ref[q : q + 1, :]).astype(BF16)

    (scaled,) = run(scale, [(wide, BF16)], *chips, inverse)
    scaled_parts = share(scaled)

    def first_back(s_ref, *refs):
        parts = refs[:sub_size]
        middle_ref, put, slope_ref, node_slope_ref, w_ref, fold_ref = refs[sub_size : sub_size + 6]
        r0, r1, d_node, d_recv, acc_scr, grad_ref, lift_scr, act_scr = refs[sub_size + 6 :]
        lift_into(parts, s_ref, lift_scr)
        for b in range(blocks):
            lifted = lift_scr[scalar(s_ref, at_pool + b)].astype(F32)
            grad_ref[rows_of(b), :] = middle_ref[b] + lifted
        d_out = mm_t(grad_ref[...].astype(BF16), w_ref[0, 5])
        fine_backward(d_out, s_ref, fold_ref[...], put, slope_ref, node_slope_ref, d_node, d_recv, act_scr, acc_scr)
        halo_grads_into((r0, r1), [acc_scr[blocks:].reshape(far_size, features)], 0, w_ref)

    *halo_grads, d_node, d_recv, d_send, grad_first = run(
        first_back,
        back_out + [(fine, F32)],
        table, *scaled_parts, grad_middle, put, slope0, node_slope0, w, fold0,
        scratch=[pltpu.VMEM((slots,) + tile, BF16)] + back_scratch,
    )
    returned = exchange(halo_grads)

    def first_own(first_ref, d_node, d_recv, d_send, w_ref, grad_ref):
        grad_ref[...] = own_back(first_ref[...], 0, w_ref, d_node[...], d_recv[...], d_send[0:blocks].reshape(fine))

    (grad_own,) = run(first_own, [(fine, F32)], grad_first, d_node, d_recv, d_send, w)

    def finish(s_ref, r0, r1, own_ref, out_ref):
        out_ref[...] = own_ref[...]
        for r, arrived in zip(ORDER, (r0, r1)):
            at = scalar(s_ref, r)
            out_ref[at] = out_ref[at] + arrived[...].astype(F32)

    (grad_nodes,) = run(finish, [(tiles, F32)], table, returned[0], returned[1], grad_own.reshape(tiles))
    return (out_nodes, grad_nodes.reshape(fine))


def solution(mesh):
    split = ("groups", "dom", "pair", "sub")
    placed = (
        P(split, None),
        P(split, None),
        P(split, None, None),
        P(split, None),
        P(split, None, None),
        P(split),
        P(split, None),
        P(split, None, None),
        P(),
        P(),
    )
    return jax.shard_map(
        per_device,
        mesh=mesh,
        in_specs=placed,
        out_specs=(P(split, None), P(split, None)),
        check_vma=False,
    )
```

```python
import jax
import jax.numpy as jnp
from jax import lax
from jax.experimental import pallas as pl
from jax.experimental.pallas import tpu as pltpu
from jax.sharding import PartitionSpec as P

F32 = jnp.float32
BF16 = jnp.bfloat16
I32 = jnp.int32
TAIL = 16
GROUP_AXES = ("pair", "sub")
ORDER = (1, 0)


def swapped(value, axis, mask):
    size = lax.axis_size(axis)
    return lax.ppermute(value, axis, [(source, source ^ mask) for source in range(size)])


def mm(a, b):
    return jnp.dot(a, b, preferred_element_type=F32)


def mm_t(a, b):
    return lax.dot_general(a, b, (((1,), (1,)), ((), ())), preferred_element_type=F32)


def scalar(table, index):
    return table[index : index + 1, :][0, 0]


def run(kernel, outs, *arrays, scratch=(), flops=0):
    return pl.pallas_call(
        kernel,
        out_shape=[jax.ShapeDtypeStruct(shape, dtype) for shape, dtype in outs],
        in_specs=[pl.BlockSpec(memory_space=pltpu.VMEM)] * len(arrays),
        out_specs=[pl.BlockSpec(memory_space=pltpu.VMEM)] * len(outs),
        scratch_shapes=list(scratch),
        compiler_params=pltpu.CompilerParams(vmem_limit_bytes=12 * 2**20),
        cost_estimate=pl.CostEstimate(flops=flops, bytes_accessed=2**20, transcendentals=0),
    )(*arrays)


def run_hbm(kernel, outs, far, *near, scratch=()):
    return pl.pallas_call(
        kernel,
        out_shape=[pltpu.VMEM(shape, dtype) for shape, dtype in outs],
        in_specs=[pl.BlockSpec(memory_space=pltpu.HBM)] * len(far) + [pl.BlockSpec(memory_space=pltpu.VMEM)] * len(near),
        out_specs=[pl.BlockSpec(memory_space=pltpu.VMEM)] * len(outs),
        scratch_shapes=list(scratch),
        compiler_params=pltpu.CompilerParams(vmem_limit_bytes=12 * 2**20),
        cost_estimate=pl.CostEstimate(flops=0, bytes_accessed=2**20, transcendentals=0),
    )(*[pltpu.with_memory_space_constraint(array, pltpu.HBM) for array in far], *near)


def per_device(
    nodes,
    cotangent,
    send_blocks,
    neighbour_blocks,
    neighbour_nodes,
    pool_map,
    coarse_blocks,
    coarse_nodes,
    weights,
    biases,
):
    size, features = neighbour_nodes.shape[2], nodes.shape[1]
    blocks, degree = neighbour_blocks.shape
    xor_bits = (1, lax.axis_size("dom") // 2)
    rounds = len(xor_bits)
    slots = lax.axis_size(GROUP_AXES)
    pair_size, sub_size = lax.axis_size("pair"), lax.axis_size("sub")
    edges = blocks * degree
    far_size = rounds * size
    everyone = blocks + rounds
    tile = (size, features)
    fine = (blocks * size, features)
    tiles = (blocks,) + tile

    held = pair_size
    wide = (held * size, features)
    doms = 1 + rounds
    listed_rows = degree + 1
    at_last = doms * listed_rows
    at_tail = held * size
    pool_rows = at_tail + TAIL
    halo_rows = at_tail + size

    at_near = rounds
    at_pool = at_near + edges
    at_pair = at_pool + blocks
    at_sub = at_pair + 1
    table_rows = -(-(at_sub + 1) // 8) * 8

    def exchange(pieces):
        return [swapped(piece, "dom", xor_bits[r]) for r, piece in zip(ORDER, pieces)]

    def reduced(pieces):
        arrived = [swapped(piece, "sub", mask) for mask, piece in enumerate(pieces) if mask > 0]
        (chip,) = run(add_parts, [(pieces[0].shape, BF16)], pieces[0], *arrived)
        return [chip] + [swapped(chip, "pair", mask) for mask in range(1, pair_size)]

    def add_parts(*refs):
        total = refs[0][...].astype(F32)
        for part in refs[1:-1]:
            total = total + part[...].astype(F32)
        refs[-1][...] = total.astype(BF16)

    def share(piece):
        return [piece] + [swapped(piece, "sub", mask) for mask in range(1, sub_size)]

    def rows_of(b):
        return pl.ds(b * size, size)

    def begun(pairs, sems):
        copies = [pltpu.make_async_copy(source, target, sems.at[i]) for i, (source, target) in enumerate(pairs)]
        for copy in copies:
            copy.start()
        return copies

    def fetch(pairs, sems):
        for copy in begun(pairs, sems):
            copy.wait()

    def choose(send_in, ends_in, listed_in, pool_in, nodes_in, h_ref, info_ref, out0, out1,
               send_scr, ends_scr, listed_scr, pool_scr, sems):
        parts = [(nodes_in.at[rows_of(b)], h_ref.at[rows_of(b)]) for b in range(blocks)]
        lists = [(send_in, send_scr), (ends_in, ends_scr), (listed_in, listed_scr), (pool_in, pool_scr)]
        copies = begun(lists + parts, sems)
        for copy in copies[: len(lists)]:
            copy.wait()
        lanes = lax.broadcasted_iota(I32, (1, features), 1)
        listed = jnp.zeros((1, features), I32)
        for e in range(degree):
            listed = jnp.where(lanes == e, jnp.broadcast_to(listed_scr[0:1, e : e + 1], (1, features)), listed)
        listed = [ends_scr[...].astype(F32), listed.astype(F32)]

        def tail_of(v, last):
            before = [jnp.zeros((v * listed_rows, features), F32)] if v else []
            left = TAIL - 1 - (v + 1) * listed_rows
            after = [jnp.zeros((left, features), F32)] if left else []
            return jnp.concatenate(before + listed + after + [last.astype(F32)], axis=0).astype(BF16)

        info_ref[...] = tail_of(0, jnp.zeros((1, features), I32))
        for r, out in zip(ORDER, (out0, out1)):
            chosen = send_scr[0:1, r : r + 1]
            slot = jnp.zeros((1, 1), I32)
            for b in range(blocks):
                slot = jnp.where(chosen == b, pool_scr[0:1, b : b + 1], slot)
            out[size:, :] = tail_of(1 + r, jnp.broadcast_to(slot, (1, features)))
        starts = [pl.multiple_of(send_scr[0:1, r : r + 1][0, 0] * size, size) for r in ORDER]
        for copy in copies[len(lists) :]:
            copy.wait()
        for at, out in zip(starts, (out0, out1)):
            out[0:size, :] = h_ref[pl.ds(at, size), :]

    sent = send_blocks.reshape(1, rounds)
    coarse_ends = coarse_nodes.reshape(degree, size)
    pools = pool_map.reshape(1, blocks)
    h0, info, *first_sends = run_hbm(
        choose,
        [(fine, BF16), ((TAIL, features), BF16)] + [((size + TAIL, features), BF16)] * rounds,
        [sent, coarse_ends, coarse_blocks, pools, nodes],
        scratch=[pltpu.VMEM(a.shape, I32) for a in (sent, coarse_ends, coarse_blocks, pools)]
        + [pltpu.SemaphoreType.DMA((4 + blocks,))],
    )
    halo = exchange(first_sends)

    def grids():
        return lax.broadcasted_iota(I32, (size, size), 0), lax.broadcasted_iota(I32, (size, size), 1)

    def own_into(state, layer, w_ref, b_ref, recv_ref, node_ref, sender_ref):
        recv_ref[...] = 0.5 * (mm(state, w_ref[layer, 0]) + b_ref[layer, 0:1, :])
        node_ref[...] = 0.5 * (mm(state, w_ref[layer, 3]) + b_ref[layer, 1:2, :])
        sender_ref[...] = (0.5 * mm(state, w_ref[layer, 1])).astype(BF16)

    def layer_forward(count, fold, pre_of, node, slope_ref, node_slope_ref, sum_scr):
        for b in range(count):
            total = None
            for e in range(degree):
                edge = b * degree + e
                half = pre_of(b, e)
                up = 1.0 + jnp.tanh(half)
                active = half * up
                if slope_ref is not None:
                    slope_ref[edge] = (up + active * (2.0 - up)).astype(BF16)
                total = active if total is None else total + active
            sum_scr[rows_of(b), :] = total.astype(BF16)
        half = node + mm(sum_scr[...], fold)
        up = 1.0 + jnp.tanh(half)
        hidden = half * up
        if slope_ref is not None:
            node_slope_ref[...] = (0.5 * (up + hidden * (2.0 - up))).astype(BF16)
        return hidden.astype(BF16)

    def senders_into(own, halos, layer, w_ref, send_scr):
        for r, g in zip(ORDER, halos):
            send_scr[blocks + r] = (0.5 * mm(g, w_ref[layer, 1])).astype(BF16)
        for b in range(blocks):
            send_scr[b] = own[rows_of(b), :]

    def fine_pre(s_ref, recv, pick, send_scr):
        def pre_of(b, e):
            edge = b * degree + e
            return recv[rows_of(b), :] + mm(pick[edge], send_scr[scalar(s_ref, at_near + edge)])

        return pre_of

    def node_backward(d_out, fold, node_slope_ref, d_node, act_scr):
        d_hidden = (d_out * node_slope_ref[...].astype(F32)).astype(BF16)
        d_node[...] = d_hidden
        act_scr[...] = mm_t(d_hidden, fold)

    def fine_backward(d_out, s_ref, fold, put_ref, slope_ref, node_slope_ref, d_node, d_recv, act_scr, acc_scr):
        node_backward(d_out, fold, node_slope_ref, d_node, act_scr)
        acc_scr[...] = jnp.zeros_like(acc_scr)
        for b in range(blocks):
            d_active = act_scr[rows_of(b), :]
            total = None
            for e in range(degree):
                edge = b * degree + e
                d_pre = d_active * slope_ref[edge].astype(F32)
                total = d_pre if total is None else total + d_pre
                near = scalar(s_ref, at_near + edge)
                acc_scr[near] = acc_scr[near] + mm(put_ref[edge], d_pre.astype(BF16))
            d_recv[rows_of(b), :] = total.astype(BF16)

    def halo_grads_into(outs, grads, layer, w_ref):
        for r, out in zip(ORDER, outs):
            own = jnp.concatenate([g[r * size : (r + 1) * size, :] for g in grads], axis=0)
            out[...] = mm_t(own.astype(BF16), w_ref[layer, 1]).astype(BF16)

    def own_back(grad, layer, w_ref, d_node, d_recv, d_send):
        return (
            grad
            + mm_t(d_recv, w_ref[layer, 0])
            + mm_t(d_node, w_ref[layer, 3])
            + mm_t(d_send.astype(BF16), w_ref[layer, 1])
        )

    def pooled_into(read, s_ref, out_refs, tail=None):
        sub = scalar(s_ref, at_sub)
        lanes = lax.broadcasted_iota(I32, (1, features), 1)
        for sub_mask, out in enumerate(out_refs):
            counts = jnp.zeros((1, features), F32)
            for q in range(held):
                slot = q * sub_size + (sub ^ sub_mask)
                total, count = None, None
                for b in range(blocks):
                    hit = (scalar(s_ref, at_pool + b) == slot).astype(F32)
                    part = read(b) * hit
                    total = part if total is None else total + part
                    count = hit if count is None else count + hit
                out[rows_of(q), :] = total.astype(BF16)
                counts = counts + jnp.where(lanes == q, count, 0.0)
            if tail is not None:
                last = lax.broadcasted_iota(I32, (TAIL, features), 0) == at_last
                kept = tail if sub_mask == 0 else jnp.zeros_like(tail)
                out[at_tail:, :] = jnp.where(last, jnp.broadcast_to(counts, tail.shape), kept).astype(BF16)

    def lift_into(parts, s_ref, lift_scr):
        sub = scalar(s_ref, at_sub)
        for mask, part in enumerate(parts):
            for q in range(held):
                for v in range(part.shape[0] // (held * size)):
                    lift_scr[v * slots + q * sub_size + (sub ^ mask)] = part[rows_of(v * held + q), :]

    inputs = [
        sent,
        neighbour_blocks,
        pools,
        neighbour_nodes.reshape(edges, size),
        weights,
        biases,
        cotangent,
    ]
    own_out = [(fine, F32), (fine, F32), (fine, BF16)]

    def prepare(*refs):
        sources, h_ref = refs[: len(inputs)], refs[len(inputs)]
        ends, w_ref, b_ref, c_ref, s_ref, fold_ref, pick, recv, node, sender, *kept, sems = refs[len(inputs) + 1 :]
        send_scr, near_scr, pool_scr = kept
        fetch(list(zip(sources, kept + [ends, w_ref, b_ref, c_ref])), sems)

        def put_row(index, ref, i, j):
            s_ref[index : index + 1, :] = jnp.broadcast_to(ref[i : i + 1, j : j + 1], (1, features))

        for r in range(rounds):
            put_row(r, send_scr, 0, r)
        for b in range(blocks):
            for e in range(degree):
                put_row(at_near + b * degree + e, near_scr, b, e)
            put_row(at_pool + b, pool_scr, 0, b)
        s_ref[at_pair : at_pair + 1, :] = jnp.full((1, features), lax.axis_index("pair"), I32)
        s_ref[at_sub : at_sub + 1, :] = jnp.full((1, features), lax.axis_index("sub"), I32)
        own_into(h_ref[...], 0, w_ref, b_ref, recv, node, sender)
        columns = grids()[1]
        upright = jnp.transpose(ends[...])
        for edge in range(edges):
            pick[edge] = (columns == upright[:, edge : edge + 1]).astype(BF16)
        fold_ref[...] = (mm(w_ref[0, 2], w_ref[0, 4]) * (0.5 / degree)).astype(BF16)

    ends, w, bias, cot, table, fold0, pick, recv0, node0, sender0 = run_hbm(
        prepare,
        [
            ((edges, size), I32), (weights.shape, BF16), (biases.shape, F32), (fine, BF16),
            ((table_rows, features), I32), (tile, BF16),
            ((edges, size, size), BF16),
        ] + own_out,
        inputs,
        h0,
        scratch=[pltpu.VMEM(a.shape, I32) for a in inputs[:3]]
        + [pltpu.SemaphoreType.DMA((len(inputs),))],
    )

    slopes = [((edges,) + tile, BF16), (fine, BF16)]

    layer_scratch = [pltpu.VMEM((everyone,) + tile, BF16), pltpu.VMEM(fine, BF16)]

    def first_layer(s_ref, g0, g1, h_ref, recv, node, sender, pick, w_ref, fold_ref, info_ref, *rest):
        first_ref, slots_ref, send_ref, *sends, sum_scr = rest
        senders_into(sender, (g0[0:size, :], g1[0:size, :]), 0, w_ref, send_ref)
        pre_of = fine_pre(s_ref, recv, pick, send_ref)
        hidden = layer_forward(blocks, fold_ref[...], pre_of, node[...], None, None, sum_scr)
        first_ref[...] = (h_ref[...].astype(F32) + mm(hidden, w_ref[0, 5])).astype(BF16)
        tail = info_ref[...].astype(F32) + g0[size:, :].astype(F32) + g1[size:, :].astype(F32)
        pooled_into(lambda b: first_ref[rows_of(b), :].astype(F32), s_ref, sends, tail)
        for r, g in zip(ORDER, (g0, g1)):
            last = g[size:, :].astype(F32).astype(I32)[at_last : at_last + 1, :]
            slots_ref[r : r + 1, :] = last

    first, halo_slots, senders0, *pool_sends = run(
        first_layer,
        [(fine, BF16), ((8, features), I32), ((everyone,) + tile, BF16)] + [((pool_rows, features), BF16)] * sub_size,
        table, halo[0], halo[1], h0, recv0, node0, sender0, pick, w, fold0, info,
        scratch=[pltpu.VMEM(fine, BF16)],
    )

    def first_slopes(s_ref, recv, node, send_ref, pick, fold_ref, slope_ref, node_slope_ref, sum_scr):
        pre_of = fine_pre(s_ref, recv, pick, send_ref)
        layer_forward(blocks, fold_ref[...], pre_of, node[...], slope_ref, node_slope_ref, sum_scr)

    slope0, node_slope0 = run(
        first_slopes, slopes, table, recv0, node0, senders0, pick, fold0, scratch=[pltpu.VMEM(fine, BF16)]
    )

    pool_in = reduced(pool_sends)

    def coarse_begin(s_ref, first_ref, *refs):
        parts, (start_ref, inverse_ref, infos_ref, other, out0, out1) = refs[:pair_size], refs[pair_size:]
        total = parts[0][0:at_tail, :].astype(F32)
        tails = [part[at_tail:, :].astype(F32) for part in parts]
        counts = tails[0][at_last : at_last + 1, :]
        for part, tail in zip(parts[1:], tails[1:]):
            total = total + part[0:at_tail, :].astype(F32)
            counts = counts + tail[at_last : at_last + 1, :]
        for q in range(held):
            inverse_ref[q : q + 1, :] = jnp.broadcast_to(1.0 / jnp.maximum(counts[:, q : q + 1], 1.0), (1, features))
        for q in range(held):
            start = (total[q * size : (q + 1) * size, :] * inverse_ref[q : q + 1, :]).astype(BF16)
            for out in (start_ref, other, out0, out1):
                out[rows_of(q), :] = start
        for r, out in zip(ORDER, (out0, out1)):
            at = pl.multiple_of(scalar(s_ref, r) * size, size)
            out[at_tail:, :] = first_ref[pl.ds(at, size), :]
        pair = scalar(s_ref, at_pair)
        for mask, tail in enumerate(tails):
            infos_ref[pair ^ mask] = tail

    coarse_start, inverse, infos, other_send, *halo_sends = run(
        coarse_begin,
        [(wide, BF16), ((8, features), F32), ((held, TAIL, features), F32), (wide, BF16)]
        + [((halo_rows, features), BF16)] * rounds,
        table, first, *pool_in,
    )
    other = swapped(other_send, "dom", xor_bits[0] ^ xor_bits[1])
    coarse_halo = exchange(halo_sends)

    def coarse_prepare(h_ref, w_ref, b_ref, cot_ref, infos_ref, ends, pre, node, fold_ref, join_ref, bias_ref,
                       far_pick, cput, put, d_out, recv, sender):
        own_into(h_ref[...], 1, w_ref, b_ref, recv, node, sender)
        for i, layer in enumerate((1, 2)):
            fold_ref[i] = (mm(w_ref[layer, 2], w_ref[layer, 4]) * (0.5 / degree)).astype(BF16)
            for j, part in enumerate((0, 3)):
                columns_j = slice(j * features, (j + 1) * features)
                join_ref[i, :, columns_j] = w_ref[layer, part] * 0.5
                bias_ref[i : i + 1, columns_j] = b_ref[layer, j : j + 1, :] * 0.5
        d_out[...] = mm_t(cot_ref[...], w_ref[2, 5])
        rows, columns = grids()
        for v in range(doms):
            for q in range(held):
                tile_at = v * held + q
                around = infos_ref[q].astype(I32)
                upright = jnp.transpose(infos_ref[q]).astype(I32)
                listed = (v + 1) * listed_rows - 1
                own = sender[rows_of(q), :]
                for e in range(degree):
                    edge = tile_at * degree + e
                    near = jnp.broadcast_to(around[listed : listed + 1, e : e + 1], (1, size))
                    at = v * listed_rows + e
                    hit = columns == upright[:, at : at + 1]
                    picked = mm((hit & (near == v)).astype(BF16), own)
                    pre[edge] = picked + recv[rows_of(q), :] if v == 0 else picked
                    for i, source in enumerate([n for n in range(doms) if n != v]):
                        far_pick[rows_of(edge), i * size : (i + 1) * size] = (hit & (near == source)).astype(BF16)
                    to = rows == around[at : at + 1, :]
                    for i, source in enumerate([n for n in range(doms) if n != v] + [v]):
                        cput[tile_at, i * size : (i + 1) * size, e * size : (e + 1) * size] = (to & (near == source)).astype(BF16)
        for edge in range(edges):
            put[edge] = (rows == ends[edge : edge + 1, :]).astype(BF16)

    coarse_edges = doms * held * degree
    pre1, node1, fold, joined, joined_bias, coarse_far, coarse_put, put, d_out2 = run(
        coarse_prepare,
        [
            ((coarse_edges,) + tile, F32), (wide, F32), ((2,) + tile, BF16),
            ((2, features, 2 * features), BF16), ((8, 2 * features), F32),
            ((coarse_edges * size, far_size), BF16), ((doms * held, doms * size, degree * size), BF16),
            ((edges, size, size), BF16), (fine, F32),
        ],
        coarse_start, w, bias, cot, infos, ends,
        scratch=[pltpu.VMEM(wide, F32), pltpu.VMEM(wide, BF16)],
    )

    def coarse_forward(other_ref, g0, g1, pre, node, far_pick, w_ref, join_ref, bias_ref, fold_ref, slope_ref, node_slope_ref, sum_scr):
        halos = [g[0:at_tail, :] for _, g in sorted(zip(ORDER, (g0, g1)))]
        arrived = (0.5 * mm(jnp.concatenate(halos + [other_ref[...]], axis=0), w_ref[1, 1])).astype(BF16)
        rows_all = held * size
        third = arrived[rounds * rows_all :, :]
        arrived = [arrived[r * rows_all : (r + 1) * rows_all, :] for r in range(rounds)]
        own = mm(jnp.concatenate(halos, axis=0), join_ref[0]) + bias_ref[0:1, :]
        recvs = [None] + [own[r * rows_all : (r + 1) * rows_all, 0:features] for r in range(rounds)]
        nodes_all = [node[...], own[:, features:]]
        sources = [arrived, [arrived[0], third], [arrived[1], third]]
        width = degree * size
        picked = []
        for v in range(doms):
            for q in range(held):
                at = (v * held + q) * width
                senders = jnp.concatenate([a[q * size : (q + 1) * size, :] for a in sources[v]], axis=0)
                picked.append(mm(far_pick[at : at + width, :], senders))

        def pre_of(b, e):
            v, q = divmod(b, held)
            value = pre[b * degree + e] + picked[b][e * size : (e + 1) * size, :]
            return value if v == 0 else value + recvs[v][q * size : (q + 1) * size, :]

        nodes_all = jnp.concatenate(nodes_all, axis=0)
        return layer_forward(doms * held, fold_ref[0], pre_of, nodes_all, slope_ref, node_slope_ref, sum_scr)

    def coarse_layer(other_ref, g0, g1, h_ref, pre, node, far_pick, w_ref, join_ref, bias_ref, fold_ref, end_ref, sum_scr):
        hidden = coarse_forward(
            other_ref, g0, g1, pre, node, far_pick, w_ref, join_ref, bias_ref, fold_ref, None, None, sum_scr
        )
        halos = [g[0:at_tail, :] for _, g in sorted(zip(ORDER, (g0, g1)))]
        state = jnp.concatenate([h_ref[...]] + halos, axis=0).astype(F32)
        end_ref[...] = (state + mm(hidden, w_ref[1, 5])).astype(BF16)

    all_wide = (doms * held * size, features)
    (coarse_end,) = run(
        coarse_layer,
        [(all_wide, BF16)],
        other, *coarse_halo, coarse_start, pre1, node1, coarse_far, w, joined, joined_bias, fold,
        scratch=[pltpu.VMEM(all_wide, BF16)],
    )

    def coarse_slopes(*refs):
        coarse_forward(*refs)

    slope1, node_slope1 = run(
        coarse_slopes,
        [((coarse_edges,) + tile, BF16), (all_wide, BF16)],
        other, *coarse_halo, pre1, node1, coarse_far, w, joined, joined_bias, fold,
        scratch=[pltpu.VMEM(all_wide, BF16)],
    )
    coarse_ends = share(coarse_end)

    back_out = [(tile, BF16)] * rounds + [(fine, BF16), (fine, BF16), ((everyone,) + tile, F32)]
    back_scratch = [pltpu.VMEM(fine, F32)]

    def last_layer(s_ref, slots_ref, g0, g1, *refs):
        parts = refs[:sub_size]
        first_ref, cot_ref, pick, put, w_ref, join_ref, bias_ref, fold_ref, d_out = refs[sub_size : sub_size + 9]
        r0, r1, hidden_ref, state_scr, grad_ref, *outs = refs[sub_size + 9 : 2 * sub_size + 14]
        (d_node, d_recv, acc_scr, lift_scr, own_scr, send_scr, sum_scr, slope_scr, node_slope_scr, act_scr) = refs[2 * sub_size + 14 :]
        lift_into(parts, s_ref, lift_scr)
        for b in range(blocks):
            lifted = lift_scr[scalar(s_ref, at_pool + b)].astype(F32)
            state_scr[rows_of(b), :] = (first_ref[rows_of(b), :].astype(F32) + lifted).astype(BF16)
        for r, g in zip(ORDER, (g0, g1)):
            lifted = lift_scr[(1 + r) * slots + scalar(slots_ref, r)].astype(F32)
            state_scr[rows_of(blocks + r), :] = (g[at_tail:, :].astype(F32) + lifted).astype(BF16)
        senders = (0.5 * mm(state_scr[...], w_ref[2, 1])).astype(BF16)
        send_scr[...] = senders.reshape((everyone,) + tile)
        own_scr[...] = mm(state_scr[0 : blocks * size, :], join_ref[1]) + bias_ref[1:2, :]
        recv, node = own_scr.at[:, 0:features], own_scr.at[:, features:]
        fold = fold_ref[1]
        pre_of = fine_pre(s_ref, recv, pick, send_scr)
        hidden_ref[...] = layer_forward(blocks, fold, pre_of, node[...], slope_scr, node_slope_scr, sum_scr)
        fine_backward(d_out[...], s_ref, fold, put, slope_scr, node_slope_scr, d_node, d_recv, act_scr, acc_scr)
        halo_grads_into((r0, r1), [acc_scr[blocks:].reshape(far_size, features)], 2, w_ref)
        grad_ref[...] = own_back(
            cot_ref[...].astype(F32), 2, w_ref, d_node[...], d_recv[...], acc_scr[0:blocks].reshape(fine)
        )
        pooled_into(lambda b: grad_ref[rows_of(b), :], s_ref, outs)
        sub = scalar(s_ref, at_sub)
        for r, g in zip(ORDER, (r0, r1)):
            slot = scalar(slots_ref, r)
            for sub_mask, out in enumerate(outs):
                for q in range(held):
                    hit = (slot == q * sub_size + (sub ^ sub_mask)).astype(F32)
                    out[rows_of((1 + r) * held + q), :] = (g[...].astype(F32) * hit).astype(BF16)

    rest = run(
        last_layer,
        [(tile, BF16)] * rounds + [(fine, BF16), ((everyone * size, features), BF16), (fine, F32)] + [(all_wide, BF16)] * sub_size,
        table, halo_slots, *coarse_halo, *coarse_ends, first, cot, pick, put, w, joined, joined_bias, fold, d_out2,
        scratch=[pltpu.VMEM(fine, BF16), pltpu.VMEM(fine, BF16), pltpu.VMEM((everyone,) + tile, F32)]
        + [pltpu.VMEM((doms * slots,) + tile, BF16)]
        + [pltpu.VMEM((blocks * size, 2 * features), F32)]
        + layer_scratch + [pltpu.VMEM((edges,) + tile, BF16), pltpu.VMEM(fine, BF16)] + back_scratch,
    )

    halo_grads, (hidden2, middle, grad_own), grad_sends = rest[:rounds], rest[rounds : rounds + 3], list(rest[rounds + 3 :])
    grad_parts = grad_sends[:1] + [swapped(piece, "sub", mask) for mask, piece in enumerate(grad_sends) if mask > 0]

    def last_out(h_ref, hidden_ref, w_ref, out_ref):
        out_ref[...] = (h_ref[0 : blocks * size, :].astype(F32) + mm(hidden_ref[...], w_ref[2, 5])).astype(BF16)

    (out_nodes,) = run(last_out, [(fine, BF16)], middle, hidden2, w)

    def coarse_back(*refs):
        parts = refs[:sub_size]
        g0, g1, put, slope_ref, node_slope_ref, w_ref, fold_ref = refs[sub_size : sub_size + 7]
        other_ref, out0, out1, grad_ref, d_node, pre_ref, act_scr = refs[sub_size + 7 :]
        grad = parts[0][...].astype(F32)
        for part in parts[1:]:
            grad = grad + part[...].astype(F32)
        rows_all, width = held * size, degree * size
        grad_ref[...] = grad[0:rows_all, :]
        node_backward(mm_t(grad.astype(BF16), w_ref[1, 5]), fold_ref[0], node_slope_ref, d_node, act_scr)
        recvs = []
        for b in range(doms * held):
            total = None
            for e in range(degree):
                edge = b * degree + e
                d_pre = act_scr[rows_of(b), :] * slope_ref[edge].astype(F32)
                if b >= held:
                    total = d_pre if total is None else total + d_pre
                pre_ref[rows_of(edge), :] = d_pre.astype(BF16)
            if b >= held:
                recvs.append(total.astype(BF16))
        senders = []
        for v in range(doms):
            tiles_v = [
                mm(put[v * held + q, 0:far_size, :], pre_ref[pl.ds((v * held + q) * width, width), :]) for q in range(held)
            ]
            senders.append(
                [jnp.concatenate([t[n * size : (n + 1) * size, :] for t in tiles_v], axis=0) for n in range(rounds)]
            )
        to_rounds = [senders[0][0] + senders[1][0], senders[0][1] + senders[2][0]]
        to_other = senders[1][1] + senders[2][1]
        sent = mm_t(jnp.concatenate(to_rounds + [to_other], axis=0).astype(BF16), w_ref[1, 1])
        sums = (
            grad[rows_all:, :]
            + mm_t(jnp.concatenate(recvs, axis=0), w_ref[1, 0])
            + mm_t(d_node[rows_all:, :], w_ref[1, 3])
            + sent[0 : rounds * rows_all, :]
        ).astype(BF16)
        other_ref[...] = sent[rounds * rows_all :, :].astype(BF16)
        for r, g, out in zip(ORDER, (g0, g1), (out0, out1)):
            out[0:at_tail, :] = sums[r * rows_all : (r + 1) * rows_all, :]
            out[at_tail:, :] = g[...]

    other_send, *coarse_sends, coarse_grad, d_node, d_pre = run(
        coarse_back,
        [(wide, BF16)] + [((halo_rows, features), BF16)] * rounds
        + [(wide, F32), (all_wide, BF16), ((coarse_edges * size, features), BF16)],
        *grad_parts, *halo_grads, coarse_put, slope1, node_slope1, w, fold,
        scratch=[pltpu.VMEM(all_wide, F32)],
    )
    other = swapped(other_send, "dom", xor_bits[0] ^ xor_bits[1])
    returned = exchange(coarse_sends)

    def coarse_own(grad_ref, put, d_node, d_pre, w_ref, own_ref):
        width = degree * size
        d_send, d_recv = [], []
        for q in range(held):
            total = None
            for v in range(doms):
                at = v * held + q
                part = mm(put[at, far_size:, :], d_pre[pl.ds(at * width, width), :])
                total = part if total is None else total + part
            d_send.append(total)
            total = None
            for e in range(degree):
                part = d_pre[rows_of(q * degree + e), :].astype(F32)
                total = part if total is None else total + part
            d_recv.append(total.astype(BF16))
        own_ref[...] = own_back(
            grad_ref[...], 1, w_ref, d_node[0 : held * size, :],
            jnp.concatenate(d_recv, axis=0), jnp.concatenate(d_send, axis=0),
        )

    (coarse_grad,) = run(coarse_own, [(wide, F32)], coarse_grad, coarse_put, d_node, d_pre, w)

    def chip_sum(own_ref, other_ref, r0, r1, out_ref):
        total = own_ref[...] + other_ref[...].astype(F32)
        for r in (r0, r1):
            total = total + r[0:at_tail, :].astype(F32)
        out_ref[...] = total.astype(BF16)

    (chip,) = run(chip_sum, [(wide, BF16)], coarse_grad, other, *returned)
    chips = [chip] + [swapped(chip, "pair", mask) for mask in range(1, pair_size)]

    def middle_grads(s_ref, own_ref, r0, r1, grad_ref):
        grad_ref[...] = own_ref[...]
        for r, arrived in zip(ORDER, (r0, r1)):
            at = scalar(s_ref, r)
            grad_ref[at] = grad_ref[at] + arrived[at_tail:, :].astype(F32)

    (grad_middle,) = run(middle_grads, [(tiles, F32)], table, grad_own.reshape(tiles), *returned)

    def scale(*refs):
        parts, (inverse_ref, out_ref) = refs[:pair_size], refs[pair_size:]
        for q in range(held):
            rows = rows_of(q)
            total = parts[0][rows, :].astype(F32)
            for part in parts[1:]:
                total = total + part[rows, :].astype(F32)
            out_ref[rows, :] = (total * inverse_ref[q : q + 1, :]).astype(BF16)

    (scaled,) = run(scale, [(wide, BF16)], *chips, inverse)
    scaled_parts = share(scaled)

    def first_back(s_ref, *refs):
        parts = refs[:sub_size]
        middle_ref, put, slope_ref, node_slope_ref, w_ref, fold_ref = refs[sub_size : sub_size + 6]
        r0, r1, d_node, d_recv, acc_scr, grad_ref, lift_scr, act_scr = refs[sub_size + 6 :]
        lift_into(parts, s_ref, lift_scr)
        for b in range(blocks):
            lifted = lift_scr[scalar(s_ref, at_pool + b)].astype(F32)
            grad_ref[rows_of(b), :] = middle_ref[b] + lifted
        d_out = mm_t(grad_ref[...].astype(BF16), w_ref[0, 5])
        fine_backward(d_out, s_ref, fold_ref[...], put, slope_ref, node_slope_ref, d_node, d_recv, act_scr, acc_scr)
        halo_grads_into((r0, r1), [acc_scr[blocks:].reshape(far_size, features)], 0, w_ref)

    *halo_grads, d_node, d_recv, d_send, grad_first = run(
        first_back,
        back_out + [(fine, F32)],
        table, *scaled_parts, grad_middle, put, slope0, node_slope0, w, fold0,
        scratch=[pltpu.VMEM((slots,) + tile, BF16)] + back_scratch,
    )
    returned = exchange(halo_grads)

    def first_own(first_ref, d_node, d_recv, d_send, w_ref, grad_ref):
        grad_ref[...] = own_back(first_ref[...], 0, w_ref, d_node[...], d_recv[...], d_send[0:blocks].reshape(fine))

    (grad_own,) = run(first_own, [(fine, F32)], grad_first, d_node, d_recv, d_send, w)

    def finish(s_ref, r0, r1, own_ref, out_ref):
        out_ref[...] = own_ref[...]
        for r, arrived in zip(ORDER, (r0, r1)):
            at = scalar(s_ref, r)
            out_ref[at] = out_ref[at] + arrived[...].astype(F32)

    (grad_nodes,) = run(finish, [(tiles, F32)], table, returned[0], returned[1], grad_own.reshape(tiles))
    return (out_nodes, grad_nodes.reshape(fine))


def solution(mesh):
    split = ("groups", "dom", "pair", "sub")
    placed = (
        P(split, None),
        P(split, None),
        P(split, None, None),
        P(split, None),
        P(split, None, None),
        P(split),
        P(split, None),
        P(split, None, None),
        P(),
        P(),
    )
    return jax.shard_map(
        per_device,
        mesh=mesh,
        in_specs=placed,
        out_specs=(P(split, None), P(split, None)),
        check_vma=False,
    )
```

```python
import jax
import jax.numpy as jnp
from jax import lax
from jax.experimental import pallas as pl
from jax.experimental.pallas import tpu as pltpu
from jax.sharding import PartitionSpec as P

F32 = jnp.float32
BF16 = jnp.bfloat16
I32 = jnp.int32
TAIL = 16
GROUP_AXES = ("pair", "sub")
ORDER = (1, 0)


def swapped(value, axis, mask):
    size = lax.axis_size(axis)
    return lax.ppermute(value, axis, [(source, source ^ mask) for source in range(size)])


def mm(a, b):
    return jnp.dot(a, b, preferred_element_type=F32)


def mm_t(a, b):
    return lax.dot_general(a, b, (((1,), (1,)), ((), ())), preferred_element_type=F32)


def scalar(table, index):
    return table[index : index + 1, :][0, 0]


def run(kernel, outs, *arrays, scratch=(), flops=0):
    return pl.pallas_call(
        kernel,
        out_shape=[jax.ShapeDtypeStruct(shape, dtype) for shape, dtype in outs],
        in_specs=[pl.BlockSpec(memory_space=pltpu.VMEM)] * len(arrays),
        out_specs=[pl.BlockSpec(memory_space=pltpu.VMEM)] * len(outs),
        scratch_shapes=list(scratch),
        compiler_params=pltpu.CompilerParams(vmem_limit_bytes=12 * 2**20),
        cost_estimate=pl.CostEstimate(flops=flops, bytes_accessed=2**20, transcendentals=0),
    )(*arrays)


def run_hbm(kernel, outs, far, *near, scratch=()):
    return pl.pallas_call(
        kernel,
        out_shape=[pltpu.VMEM(shape, dtype) for shape, dtype in outs],
        in_specs=[pl.BlockSpec(memory_space=pltpu.HBM)] * len(far) + [pl.BlockSpec(memory_space=pltpu.VMEM)] * len(near),
        out_specs=[pl.BlockSpec(memory_space=pltpu.VMEM)] * len(outs),
        scratch_shapes=list(scratch),
        compiler_params=pltpu.CompilerParams(vmem_limit_bytes=12 * 2**20),
        cost_estimate=pl.CostEstimate(flops=0, bytes_accessed=2**20, transcendentals=0),
    )(*[pltpu.with_memory_space_constraint(array, pltpu.HBM) for array in far], *near)


def per_device(
    nodes,
    cotangent,
    send_blocks,
    neighbour_blocks,
    neighbour_nodes,
    pool_map,
    coarse_blocks,
    coarse_nodes,
    weights,
    biases,
):
    size, features = neighbour_nodes.shape[2], nodes.shape[1]
    blocks, degree = neighbour_blocks.shape
    xor_bits = (1, lax.axis_size("dom") // 2)
    rounds = len(xor_bits)
    slots = lax.axis_size(GROUP_AXES)
    pair_size, sub_size = lax.axis_size("pair"), lax.axis_size("sub")
    edges = blocks * degree
    far_size = rounds * size
    everyone = blocks + rounds
    tile = (size, features)
    fine = (blocks * size, features)
    tiles = (blocks,) + tile

    held = pair_size
    wide = (held * size, features)
    doms = 1 + rounds
    listed_rows = degree + 1
    at_last = doms * listed_rows
    at_tail = held * size
    pool_rows = at_tail + TAIL
    halo_rows = at_tail + size

    at_near = rounds
    at_pool = at_near + edges
    at_pair = at_pool + blocks
    at_sub = at_pair + 1
    table_rows = -(-(at_sub + 1) // 8) * 8

    def exchange(pieces):
        return [swapped(piece, "dom", xor_bits[r]) for r, piece in zip(ORDER, pieces)]

    def reduced(pieces):
        arrived = [swapped(piece, "sub", mask) for mask, piece in enumerate(pieces) if mask > 0]
        (chip,) = run(add_parts, [(pieces[0].shape, BF16)], pieces[0], *arrived)
        return [chip] + [swapped(chip, "pair", mask) for mask in range(1, pair_size)]

    def add_parts(*refs):
        total = refs[0][...].astype(F32)
        for part in refs[1:-1]:
            total = total + part[...].astype(F32)
        refs[-1][...] = total.astype(BF16)

    def share(piece):
        return [piece] + [swapped(piece, "sub", mask) for mask in range(1, sub_size)]

    def rows_of(b):
        return pl.ds(b * size, size)

    def begun(pairs, sems):
        copies = [pltpu.make_async_copy(source, target, sems.at[i]) for i, (source, target) in enumerate(pairs)]
        for copy in copies:
            copy.start()
        return copies

    def fetch(pairs, sems):
        for copy in begun(pairs, sems):
            copy.wait()

    def choose(send_in, ends_in, listed_in, pool_in, nodes_in, h_ref, info_ref, out0, out1,
               send_scr, ends_scr, listed_scr, pool_scr, sems):
        parts = [(nodes_in.at[rows_of(b)], h_ref.at[rows_of(b)]) for b in range(blocks)]
        lists = [(send_in, send_scr), (ends_in, ends_scr), (listed_in, listed_scr), (pool_in, pool_scr)]
        copies = begun(lists + parts, sems)
        for copy in copies[: len(lists)]:
            copy.wait()
        lanes = lax.broadcasted_iota(I32, (1, features), 1)
        listed = jnp.zeros((1, features), I32)
        for e in range(degree):
            listed = jnp.where(lanes == e, jnp.broadcast_to(listed_scr[0:1, e : e + 1], (1, features)), listed)
        listed = [ends_scr[...].astype(F32), listed.astype(F32)]

        def tail_of(v, last):
            before = [jnp.zeros((v * listed_rows, features), F32)] if v else []
            left = TAIL - 1 - (v + 1) * listed_rows
            after = [jnp.zeros((left, features), F32)] if left else []
            return jnp.concatenate(before + listed + after + [last.astype(F32)], axis=0).astype(BF16)

        info_ref[...] = tail_of(0, jnp.zeros((1, features), I32))
        for r, out in zip(ORDER, (out0, out1)):
            chosen = send_scr[0:1, r : r + 1]
            slot = jnp.zeros((1, 1), I32)
            for b in range(blocks):
                slot = jnp.where(chosen == b, pool_scr[0:1, b : b + 1], slot)
            out[size:, :] = tail_of(1 + r, jnp.broadcast_to(slot, (1, features)))
        starts = [pl.multiple_of(send_scr[0:1, r : r + 1][0, 0] * size, size) for r in ORDER]
        for copy in copies[len(lists) :]:
            copy.wait()
        for at, out in zip(starts, (out0, out1)):
            out[0:size, :] = h_ref[pl.ds(at, size), :]

    sent = send_blocks.reshape(1, rounds)
    coarse_ends = coarse_nodes.reshape(degree, size)
    pools = pool_map.reshape(1, blocks)
    h0, info, *first_sends = run_hbm(
        choose,
        [(fine, BF16), ((TAIL, features), BF16)] + [((size + TAIL, features), BF16)] * rounds,
        [sent, coarse_ends, coarse_blocks, pools, nodes],
        scratch=[pltpu.VMEM(a.shape, I32) for a in (sent, coarse_ends, coarse_blocks, pools)]
        + [pltpu.SemaphoreType.DMA((4 + blocks,))],
    )
    halo = exchange(first_sends)

    def grids():
        return lax.broadcasted_iota(I32, (size, size), 0), lax.broadcasted_iota(I32, (size, size), 1)

    def own_into(state, layer, w_ref, b_ref, recv_ref, node_ref, sender_ref):
        recv_ref[...] = 0.5 * (mm(state, w_ref[layer, 0]) + b_ref[layer, 0:1, :])
        node_ref[...] = 0.5 * (mm(state, w_ref[layer, 3]) + b_ref[layer, 1:2, :])
        sender_ref[...] = (0.5 * mm(state, w_ref[layer, 1])).astype(BF16)

    def layer_forward(count, fold, pre_of, node, slope_ref, node_slope_ref, sum_scr):
        for b in range(count):
            total = None
            for e in range(degree):
                edge = b * degree + e
                half = pre_of(b, e)
                up = 1.0 + jnp.tanh(half)
                active = half * up
                if slope_ref is not None:
                    slope_ref[edge] = (up + active * (2.0 - up)).astype(BF16)
                total = active if total is None else total + active
            sum_scr[rows_of(b), :] = total.astype(BF16)
        half = node + mm(sum_scr[...], fold)
        up = 1.0 + jnp.tanh(half)
        hidden = half * up
        if slope_ref is not None:
            node_slope_ref[...] = (0.5 * (up + hidden * (2.0 - up))).astype(BF16)
        return hidden.astype(BF16)

    def senders_into(own, halos, layer, w_ref, send_scr):
        for r, g in zip(ORDER, halos):
            send_scr[blocks + r] = (0.5 * mm(g, w_ref[layer, 1])).astype(BF16)
        for b in range(blocks):
            send_scr[b] = own[rows_of(b), :]

    def fine_pre(s_ref, recv, pick, send_scr):
        def pre_of(b, e):
            edge = b * degree + e
            return recv[rows_of(b), :] + mm(pick[edge], send_scr[scalar(s_ref, at_near + edge)])

        return pre_of

    def node_backward(d_out, fold, node_slope_ref, d_node, act_scr):
        d_hidden = (d_out * node_slope_ref[...].astype(F32)).astype(BF16)
        d_node[...] = d_hidden
        act_scr[...] = mm_t(d_hidden, fold)

    def fine_backward(d_out, s_ref, fold, put_ref, slope_ref, node_slope_ref, d_node, d_recv, act_scr, acc_scr):
        node_backward(d_out, fold, node_slope_ref, d_node, act_scr)
        acc_scr[...] = jnp.zeros_like(acc_scr)
        for b in range(blocks):
            d_active = act_scr[rows_of(b), :]
            total = None
            for e in range(degree):
                edge = b * degree + e
                d_pre = d_active * slope_ref[edge].astype(F32)
                total = d_pre if total is None else total + d_pre
                near = scalar(s_ref, at_near + edge)
                acc_scr[near] = acc_scr[near] + mm(put_ref[edge], d_pre.astype(BF16))
            d_recv[rows_of(b), :] = total.astype(BF16)

    def halo_grads_into(outs, grads, layer, w_ref):
        for r, out in zip(ORDER, outs):
            own = jnp.concatenate([g[r * size : (r + 1) * size, :] for g in grads], axis=0)
            out[...] = mm_t(own.astype(BF16), w_ref[layer, 1]).astype(BF16)

    def own_back(grad, layer, w_ref, d_node, d_recv, d_send):
        return (
            grad
            + mm_t(d_recv, w_ref[layer, 0])
            + mm_t(d_node, w_ref[layer, 3])
            + mm_t(d_send.astype(BF16), w_ref[layer, 1])
        )

    def pooled_into(read, s_ref, out_refs, tail=None):
        sub = scalar(s_ref, at_sub)
        lanes = lax.broadcasted_iota(I32, (1, features), 1)
        for sub_mask, out in enumerate(out_refs):
            counts = jnp.zeros((1, features), F32)
            for q in range(held):
                slot = q * sub_size + (sub ^ sub_mask)
                total, count = None, None
                for b in range(blocks):
                    hit = (scalar(s_ref, at_pool + b) == slot).astype(F32)
                    part = read(b) * hit
                    total = part if total is None else total + part
                    count = hit if count is None else count + hit
                out[rows_of(q), :] = total.astype(BF16)
                counts = counts + jnp.where(lanes == q, count, 0.0)
            if tail is not None:
                last = lax.broadcasted_iota(I32, (TAIL, features), 0) == at_last
                kept = tail if sub_mask == 0 else jnp.zeros_like(tail)
                out[at_tail:, :] = jnp.where(last, jnp.broadcast_to(counts, tail.shape), kept).astype(BF16)

    def lift_into(parts, s_ref, lift_scr):
        sub = scalar(s_ref, at_sub)
        for mask, part in enumerate(parts):
            for q in range(held):
                for v in range(part.shape[0] // (held * size)):
                    lift_scr[v * slots + q * sub_size + (sub ^ mask)] = part[rows_of(v * held + q), :]

    inputs = [
        sent,
        neighbour_blocks,
        pools,
        neighbour_nodes.reshape(edges, size),
        weights,
        biases,
        cotangent,
    ]
    own_out = [(fine, F32), (fine, F32), (fine, BF16)]

    def prepare(*refs):
        sources, h_ref = refs[: len(inputs)], refs[len(inputs)]
        ends, w_ref, b_ref, c_ref, s_ref, fold_ref, pick, recv, node, sender, *kept, sems = refs[len(inputs) + 1 :]
        send_scr, near_scr, pool_scr = kept
        fetch(list(zip(sources, kept + [ends, w_ref, b_ref, c_ref])), sems)

        def put_row(index, ref, i, j):
            s_ref[index : index + 1, :] = jnp.broadcast_to(ref[i : i + 1, j : j + 1], (1, features))

        for r in range(rounds):
            put_row(r, send_scr, 0, r)
        for b in range(blocks):
            for e in range(degree):
                put_row(at_near + b * degree + e, near_scr, b, e)
            put_row(at_pool + b, pool_scr, 0, b)
        s_ref[at_pair : at_pair + 1, :] = jnp.full((1, features), lax.axis_index("pair"), I32)
        s_ref[at_sub : at_sub + 1, :] = jnp.full((1, features), lax.axis_index("sub"), I32)
        own_into(h_ref[...], 0, w_ref, b_ref, recv, node, sender)
        columns = grids()[1]
        upright = jnp.transpose(ends[...])
        for edge in range(edges):
            pick[edge] = (columns == upright[:, edge : edge + 1]).astype(BF16)
        fold_ref[...] = (mm(w_ref[0, 2], w_ref[0, 4]) * (0.5 / degree)).astype(BF16)

    ends, w, bias, cot, table, fold0, pick, recv0, node0, sender0 = run_hbm(
        prepare,
        [
            ((edges, size), I32), (weights.shape, BF16), (biases.shape, F32), (fine, BF16),
            ((table_rows, features), I32), (tile, BF16),
            ((edges, size, size), BF16),
        ] + own_out,
        inputs,
        h0,
        scratch=[pltpu.VMEM(a.shape, I32) for a in inputs[:3]]
        + [pltpu.SemaphoreType.DMA((len(inputs),))],
    )

    slopes = [((edges,) + tile, BF16), (fine, BF16)]

    layer_scratch = [pltpu.VMEM((everyone,) + tile, BF16), pltpu.VMEM(fine, BF16)]

    def first_layer(s_ref, g0, g1, h_ref, recv, node, sender, pick, w_ref, fold_ref, info_ref, *rest):
        first_ref, slots_ref, send_ref, *sends, sum_scr = rest
        senders_into(sender, (g0[0:size, :], g1[0:size, :]), 0, w_ref, send_ref)
        pre_of = fine_pre(s_ref, recv, pick, send_ref)
        hidden = layer_forward(blocks, fold_ref[...], pre_of, node[...], None, None, sum_scr)
        first_ref[...] = (h_ref[...].astype(F32) + mm(hidden, w_ref[0, 5])).astype(BF16)
        tail = info_ref[...].astype(F32) + g0[size:, :].astype(F32) + g1[size:, :].astype(F32)
        pooled_into(lambda b: first_ref[rows_of(b), :].astype(F32), s_ref, sends, tail)
        for r, g in zip(ORDER, (g0, g1)):
            last = g[size:, :].astype(F32).astype(I32)[at_last : at_last + 1, :]
            slots_ref[r : r + 1, :] = last

    first, halo_slots, senders0, *pool_sends = run(
        first_layer,
        [(fine, BF16), ((8, features), I32), ((everyone,) + tile, BF16)] + [((pool_rows, features), BF16)] * sub_size,
        table, halo[0], halo[1], h0, recv0, node0, sender0, pick, w, fold0, info,
        scratch=[pltpu.VMEM(fine, BF16)],
    )

    def first_slopes(s_ref, recv, node, send_ref, pick, fold_ref, slope_ref, node_slope_ref, sum_scr):
        pre_of = fine_pre(s_ref, recv, pick, send_ref)
        layer_forward(blocks, fold_ref[...], pre_of, node[...], slope_ref, node_slope_ref, sum_scr)

    slope0, node_slope0 = run(
        first_slopes, slopes, table, recv0, node0, senders0, pick, fold0, scratch=[pltpu.VMEM(fine, BF16)]
    )

    pool_in = reduced(pool_sends)

    def coarse_begin(s_ref, first_ref, *refs):
        parts, (start_ref, inverse_ref, infos_ref, other, out0, out1) = refs[:pair_size], refs[pair_size:]
        total = parts[0][0:at_tail, :].astype(F32)
        tails = [part[at_tail:, :].astype(F32) for part in parts]
        counts = tails[0][at_last : at_last + 1, :]
        for part, tail in zip(parts[1:], tails[1:]):
            total = total + part[0:at_tail, :].astype(F32)
            counts = counts + tail[at_last : at_last + 1, :]
        inverses = 1.0 / jnp.maximum(counts, 1.0)
        for q in range(held):
            inverse_ref[q : q + 1, :] = jnp.broadcast_to(inverses[:, q : q + 1], (1, features))
        for q in range(held):
            start = (total[q * size : (q + 1) * size, :] * inverse_ref[q : q + 1, :]).astype(BF16)
            for out in (start_ref, other, out0, out1):
                out[rows_of(q), :] = start
        for r, out in zip(ORDER, (out0, out1)):
            at = pl.multiple_of(scalar(s_ref, r) * size, size)
            out[at_tail:, :] = first_ref[pl.ds(at, size), :]
        pair = scalar(s_ref, at_pair)
        for mask, tail in enumerate(tails):
            infos_ref[pair ^ mask] = tail

    coarse_start, inverse, infos, other_send, *halo_sends = run(
        coarse_begin,
        [(wide, BF16), ((8, features), F32), ((held, TAIL, features), F32), (wide, BF16)]
        + [((halo_rows, features), BF16)] * rounds,
        table, first, *pool_in,
    )
    other = swapped(other_send, "dom", xor_bits[0] ^ xor_bits[1])
    coarse_halo = exchange(halo_sends)

    def coarse_prepare(h_ref, w_ref, b_ref, cot_ref, infos_ref, ends, pre, node, fold_ref, join_ref, bias_ref,
                       far_pick, cput, put, d_out, recv, sender):
        own_into(h_ref[...], 1, w_ref, b_ref, recv, node, sender)
        for i, layer in enumerate((1, 2)):
            fold_ref[i] = (mm(w_ref[layer, 2], w_ref[layer, 4]) * (0.5 / degree)).astype(BF16)
            for j, part in enumerate((0, 3)):
                columns_j = slice(j * features, (j + 1) * features)
                join_ref[i, :, columns_j] = w_ref[layer, part] * 0.5
                bias_ref[i : i + 1, columns_j] = b_ref[layer, j : j + 1, :] * 0.5
        d_out[...] = mm_t(cot_ref[...], w_ref[2, 5])
        rows, columns = grids()
        for v in range(doms):
            for q in range(held):
                tile_at = v * held + q
                around = infos_ref[q].astype(I32)
                upright = jnp.transpose(infos_ref[q]).astype(I32)
                listed = (v + 1) * listed_rows - 1
                own = sender[rows_of(q), :]
                for e in range(degree):
                    edge = tile_at * degree + e
                    near = jnp.broadcast_to(around[listed : listed + 1, e : e + 1], (1, size))
                    at = v * listed_rows + e
                    hit = columns == upright[:, at : at + 1]
                    picked = mm((hit & (near == v)).astype(BF16), own)
                    pre[edge] = picked + recv[rows_of(q), :] if v == 0 else picked
                    for i, source in enumerate([n for n in range(doms) if n != v]):
                        far_pick[rows_of(edge), i * size : (i + 1) * size] = (hit & (near == source)).astype(BF16)
                    to = rows == around[at : at + 1, :]
                    for i, source in enumerate([n for n in range(doms) if n != v] + [v]):
                        cput[tile_at, i * size : (i + 1) * size, e * size : (e + 1) * size] = (to & (near == source)).astype(BF16)
        for edge in range(edges):
            put[edge] = (rows == ends[edge : edge + 1, :]).astype(BF16)

    coarse_edges = doms * held * degree
    pre1, node1, fold, joined, joined_bias, coarse_far, coarse_put, put, d_out2 = run(
        coarse_prepare,
        [
            ((coarse_edges,) + tile, F32), (wide, F32), ((2,) + tile, BF16),
            ((2, features, 2 * features), BF16), ((8, 2 * features), F32),
            ((coarse_edges * size, far_size), BF16), ((doms * held, doms * size, degree * size), BF16),
            ((edges, size, size), BF16), (fine, F32),
        ],
        coarse_start, w, bias, cot, infos, ends,
        scratch=[pltpu.VMEM(wide, F32), pltpu.VMEM(wide, BF16)],
    )

    def coarse_forward(other_ref, g0, g1, pre, node, far_pick, w_ref, join_ref, bias_ref, fold_ref, slope_ref, node_slope_ref, sum_scr):
        halos = [g[0:at_tail, :] for _, g in sorted(zip(ORDER, (g0, g1)))]
        arrived = (0.5 * mm(jnp.concatenate(halos + [other_ref[...]], axis=0), w_ref[1, 1])).astype(BF16)
        rows_all = held * size
        third = arrived[rounds * rows_all :, :]
        arrived = [arrived[r * rows_all : (r + 1) * rows_all, :] for r in range(rounds)]
        own = mm(jnp.concatenate(halos, axis=0), join_ref[0]) + bias_ref[0:1, :]
        recvs = [None] + [own[r * rows_all : (r + 1) * rows_all, 0:features] for r in range(rounds)]
        nodes_all = [node[...], own[:, features:]]
        sources = [arrived, [arrived[0], third], [arrived[1], third]]
        width = degree * size
        picked = []
        for v in range(doms):
            for q in range(held):
                at = (v * held + q) * width
                senders = jnp.concatenate([a[q * size : (q + 1) * size, :] for a in sources[v]], axis=0)
                picked.append(mm(far_pick[at : at + width, :], senders))

        def pre_of(b, e):
            v, q = divmod(b, held)
            value = pre[b * degree + e] + picked[b][e * size : (e + 1) * size, :]
            return value if v == 0 else value + recvs[v][q * size : (q + 1) * size, :]

        nodes_all = jnp.concatenate(nodes_all, axis=0)
        return layer_forward(doms * held, fold_ref[0], pre_of, nodes_all, slope_ref, node_slope_ref, sum_scr)

    def coarse_layer(other_ref, g0, g1, h_ref, pre, node, far_pick, w_ref, join_ref, bias_ref, fold_ref, end_ref, sum_scr):
        hidden = coarse_forward(
            other_ref, g0, g1, pre, node, far_pick, w_ref, join_ref, bias_ref, fold_ref, None, None, sum_scr
        )
        halos = [g[0:at_tail, :] for _, g in sorted(zip(ORDER, (g0, g1)))]
        state = jnp.concatenate([h_ref[...]] + halos, axis=0).astype(F32)
        end_ref[...] = (state + mm(hidden, w_ref[1, 5])).astype(BF16)

    all_wide = (doms * held * size, features)
    (coarse_end,) = run(
        coarse_layer,
        [(all_wide, BF16)],
        other, *coarse_halo, coarse_start, pre1, node1, coarse_far, w, joined, joined_bias, fold,
        scratch=[pltpu.VMEM(all_wide, BF16)],
    )

    def coarse_slopes(*refs):
        coarse_forward(*refs)

    slope1, node_slope1 = run(
        coarse_slopes,
        [((coarse_edges,) + tile, BF16), (all_wide, BF16)],
        other, *coarse_halo, pre1, node1, coarse_far, w, joined, joined_bias, fold,
        scratch=[pltpu.VMEM(all_wide, BF16)],
    )
    coarse_ends = share(coarse_end)

    back_out = [(tile, BF16)] * rounds + [(fine, BF16), (fine, BF16), ((everyone,) + tile, F32)]
    back_scratch = [pltpu.VMEM(fine, F32)]

    def last_layer(s_ref, slots_ref, g0, g1, *refs):
        parts = refs[:sub_size]
        first_ref, cot_ref, pick, put, w_ref, join_ref, bias_ref, fold_ref, d_out = refs[sub_size : sub_size + 9]
        r0, r1, hidden_ref, state_scr, grad_ref, *outs = refs[sub_size + 9 : 2 * sub_size + 14]
        (d_node, d_recv, acc_scr, lift_scr, own_scr, send_scr, sum_scr, slope_scr, node_slope_scr, act_scr) = refs[2 * sub_size + 14 :]
        lift_into(parts, s_ref, lift_scr)
        for b in range(blocks):
            lifted = lift_scr[scalar(s_ref, at_pool + b)].astype(F32)
            state_scr[rows_of(b), :] = (first_ref[rows_of(b), :].astype(F32) + lifted).astype(BF16)
        for r, g in zip(ORDER, (g0, g1)):
            lifted = lift_scr[(1 + r) * slots + scalar(slots_ref, r)].astype(F32)
            state_scr[rows_of(blocks + r), :] = (g[at_tail:, :].astype(F32) + lifted).astype(BF16)
        senders = (0.5 * mm(state_scr[...], w_ref[2, 1])).astype(BF16)
        send_scr[...] = senders.reshape((everyone,) + tile)
        own_scr[...] = mm(state_scr[0 : blocks * size, :], join_ref[1]) + bias_ref[1:2, :]
        recv, node = own_scr.at[:, 0:features], own_scr.at[:, features:]
        fold = fold_ref[1]
        pre_of = fine_pre(s_ref, recv, pick, send_scr)
        hidden_ref[...] = layer_forward(blocks, fold, pre_of, node[...], slope_scr, node_slope_scr, sum_scr)
        fine_backward(d_out[...], s_ref, fold, put, slope_scr, node_slope_scr, d_node, d_recv, act_scr, acc_scr)
        halo_grads_into((r0, r1), [acc_scr[blocks:].reshape(far_size, features)], 2, w_ref)
        grad_ref[...] = own_back(
            cot_ref[...].astype(F32), 2, w_ref, d_node[...], d_recv[...], acc_scr[0:blocks].reshape(fine)
        )
        pooled_into(lambda b: grad_ref[rows_of(b), :], s_ref, outs)
        sub = scalar(s_ref, at_sub)
        for r, g in zip(ORDER, (r0, r1)):
            slot = scalar(slots_ref, r)
            for sub_mask, out in enumerate(outs):
                for q in range(held):
                    hit = slot == q * sub_size + (sub ^ sub_mask)
                    out[rows_of((1 + r) * held + q), :] = jnp.where(hit, g[...], jnp.zeros(tile, BF16))

    rest = run(
        last_layer,
        [(tile, BF16)] * rounds + [(fine, BF16), ((everyone * size, features), BF16), (fine, F32)] + [(all_wide, BF16)] * sub_size,
        table, halo_slots, *coarse_halo, *coarse_ends, first, cot, pick, put, w, joined, joined_bias, fold, d_out2,
        scratch=[pltpu.VMEM(fine, BF16), pltpu.VMEM(fine, BF16), pltpu.VMEM((everyone,) + tile, F32)]
        + [pltpu.VMEM((doms * slots,) + tile, BF16)]
        + [pltpu.VMEM((blocks * size, 2 * features), F32)]
        + layer_scratch + [pltpu.VMEM((edges,) + tile, BF16), pltpu.VMEM(fine, BF16)] + back_scratch,
    )

    halo_grads, (hidden2, middle, grad_own), grad_sends = rest[:rounds], rest[rounds : rounds + 3], list(rest[rounds + 3 :])
    grad_parts = grad_sends[:1] + [swapped(piece, "sub", mask) for mask, piece in enumerate(grad_sends) if mask > 0]

    def last_out(h_ref, hidden_ref, w_ref, out_ref):
        out_ref[...] = (h_ref[0 : blocks * size, :].astype(F32) + mm(hidden_ref[...], w_ref[2, 5])).astype(BF16)

    (out_nodes,) = run(last_out, [(fine, BF16)], middle, hidden2, w)

    def coarse_back(*refs):
        parts = refs[:sub_size]
        g0, g1, put, slope_ref, node_slope_ref, w_ref, fold_ref = refs[sub_size : sub_size + 7]
        other_ref, out0, out1, grad_ref, d_node, pre_ref, act_scr = refs[sub_size + 7 :]
        grad = parts[0][...].astype(F32)
        for part in parts[1:]:
            grad = grad + part[...].astype(F32)
        rows_all, width = held * size, degree * size
        grad_ref[...] = grad[0:rows_all, :]
        node_backward(mm_t(grad.astype(BF16), w_ref[1, 5]), fold_ref[0], node_slope_ref, d_node, act_scr)
        recvs = []
        for b in range(doms * held):
            total = None
            for e in range(degree):
                edge = b * degree + e
                d_pre = act_scr[rows_of(b), :] * slope_ref[edge].astype(F32)
                if b >= held:
                    total = d_pre if total is None else total + d_pre
                pre_ref[rows_of(edge), :] = d_pre.astype(BF16)
            if b >= held:
                recvs.append(total.astype(BF16))
        senders = []
        for v in range(doms):
            tiles_v = [
                mm(put[v * held + q, 0:far_size, :], pre_ref[pl.ds((v * held + q) * width, width), :]) for q in range(held)
            ]
            senders.append(
                [jnp.concatenate([t[n * size : (n + 1) * size, :] for t in tiles_v], axis=0) for n in range(rounds)]
            )
        to_rounds = [senders[0][0] + senders[1][0], senders[0][1] + senders[2][0]]
        to_other = senders[1][1] + senders[2][1]
        sent = mm_t(jnp.concatenate(to_rounds + [to_other], axis=0).astype(BF16), w_ref[1, 1])
        sums = (
            grad[rows_all:, :]
            + mm_t(jnp.concatenate(recvs, axis=0), w_ref[1, 0])
            + mm_t(d_node[rows_all:, :], w_ref[1, 3])
            + sent[0 : rounds * rows_all, :]
        ).astype(BF16)
        other_ref[...] = sent[rounds * rows_all :, :].astype(BF16)
        for r, g, out in zip(ORDER, (g0, g1), (out0, out1)):
            out[0:at_tail, :] = sums[r * rows_all : (r + 1) * rows_all, :]
            out[at_tail:, :] = g[...]

    other_send, *coarse_sends, coarse_grad, d_node, d_pre = run(
        coarse_back,
        [(wide, BF16)] + [((halo_rows, features), BF16)] * rounds
        + [(wide, F32), (all_wide, BF16), ((coarse_edges * size, features), BF16)],
        *grad_parts, *halo_grads, coarse_put, slope1, node_slope1, w, fold,
        scratch=[pltpu.VMEM(all_wide, F32)],
    )
    other = swapped(other_send, "dom", xor_bits[0] ^ xor_bits[1])
    returned = exchange(coarse_sends)

    def coarse_own(grad_ref, put, d_node, d_pre, w_ref, own_ref):
        width = degree * size
        d_send, d_recv = [], []
        for q in range(held):
            total = None
            for v in range(doms):
                at = v * held + q
                part = mm(put[at, far_size:, :], d_pre[pl.ds(at * width, width), :])
                total = part if total is None else total + part
            d_send.append(total)
            total = None
            for e in range(degree):
                part = d_pre[rows_of(q * degree + e), :].astype(F32)
                total = part if total is None else total + part
            d_recv.append(total.astype(BF16))
        own_ref[...] = own_back(
            grad_ref[...], 1, w_ref, d_node[0 : held * size, :],
            jnp.concatenate(d_recv, axis=0), jnp.concatenate(d_send, axis=0),
        )

    (coarse_grad,) = run(coarse_own, [(wide, F32)], coarse_grad, coarse_put, d_node, d_pre, w)

    def chip_sum(own_ref, other_ref, r0, r1, out_ref):
        total = own_ref[...] + other_ref[...].astype(F32)
        for r in (r0, r1):
            total = total + r[0:at_tail, :].astype(F32)
        out_ref[...] = total.astype(BF16)

    (chip,) = run(chip_sum, [(wide, BF16)], coarse_grad, other, *returned)
    chips = [chip] + [swapped(chip, "pair", mask) for mask in range(1, pair_size)]

    def middle_grads(s_ref, own_ref, r0, r1, grad_ref):
        grad_ref[...] = own_ref[...]
        for r, arrived in zip(ORDER, (r0, r1)):
            at = scalar(s_ref, r)
            grad_ref[at] = grad_ref[at] + arrived[at_tail:, :].astype(F32)

    (grad_middle,) = run(middle_grads, [(tiles, F32)], table, grad_own.reshape(tiles), *returned)

    def scale(*refs):
        parts, (inverse_ref, out_ref) = refs[:pair_size], refs[pair_size:]
        for q in range(held):
            rows = rows_of(q)
            total = parts[0][rows, :].astype(F32)
            for part in parts[1:]:
                total = total + part[rows, :].astype(F32)
            out_ref[rows, :] = (total * inverse_ref[q : q + 1, :]).astype(BF16)

    (scaled,) = run(scale, [(wide, BF16)], *chips, inverse)
    scaled_parts = share(scaled)

    def first_back(s_ref, *refs):
        parts = refs[:sub_size]
        middle_ref, put, slope_ref, node_slope_ref, w_ref, fold_ref = refs[sub_size : sub_size + 6]
        r0, r1, d_node, d_recv, acc_scr, grad_ref, lift_scr, act_scr = refs[sub_size + 6 :]
        lift_into(parts, s_ref, lift_scr)
        for b in range(blocks):
            lifted = lift_scr[scalar(s_ref, at_pool + b)].astype(F32)
            grad_ref[rows_of(b), :] = middle_ref[b] + lifted
        d_out = mm_t(grad_ref[...].astype(BF16), w_ref[0, 5])
        fine_backward(d_out, s_ref, fold_ref[...], put, slope_ref, node_slope_ref, d_node, d_recv, act_scr, acc_scr)
        halo_grads_into((r0, r1), [acc_scr[blocks:].reshape(far_size, features)], 0, w_ref)

    *halo_grads, d_node, d_recv, d_send, grad_first = run(
        first_back,
        back_out + [(fine, F32)],
        table, *scaled_parts, grad_middle, put, slope0, node_slope0, w, fold0,
        scratch=[pltpu.VMEM((slots,) + tile, BF16)] + back_scratch,
    )
    returned = exchange(halo_grads)

    def first_own(first_ref, d_node, d_recv, d_send, w_ref, grad_ref):
        grad_ref[...] = own_back(first_ref[...], 0, w_ref, d_node[...], d_recv[...], d_send[0:blocks].reshape(fine))

    (grad_own,) = run(first_own, [(fine, F32)], grad_first, d_node, d_recv, d_send, w)

    def finish(s_ref, r0, r1, own_ref, out_ref):
        out_ref[...] = own_ref[...]
        for r, arrived in zip(ORDER, (r0, r1)):
            at = scalar(s_ref, r)
            out_ref[at] = out_ref[at] + arrived[...].astype(F32)

    (grad_nodes,) = run(finish, [(tiles, F32)], table, returned[0], returned[1], grad_own.reshape(tiles))
    return (out_nodes, grad_nodes.reshape(fine))


def solution(mesh):
    split = ("groups", "dom", "pair", "sub")
    placed = (
        P(split, None),
        P(split, None),
        P(split, None, None),
        P(split, None),
        P(split, None, None),
        P(split),
        P(split, None),
        P(split, None, None),
        P(),
        P(),
    )
    return jax.shard_map(
        per_device,
        mesh=mesh,
        in_specs=placed,
        out_specs=(P(split, None), P(split, None)),
        check_vma=False,
    )
```
